128 devices in a mesh: ts: 32 (over z, x_lo, y), gz: 4 (over x_hi, core).
Axes of the slice: x: 4 (x_hi: 2, x_lo: 2; x = x_hi * 2 + x_lo), y: 4, z: 4, core: 2. Of those that a mesh axis runs over, the one named last changes fastest.
Arguments:
- eigvecs: bfloat16 [2, 3, 4, 32, 64, 32, 128], P(None, None, None, 'ts', 'gz'), may hold values from -0.25 to 0.25
- gauge_links: bfloat16 [3, 18, 4, 32, 64, 32], P(None, None, None, 'ts', 'gz'), may hold values from -3.5 to 3.5
- momenta: int32 [2, 3], replicated, may hold values from -2 to 2
- directions: int32 [3], replicated, may hold values from 0 to 2, each once
Outputs:
- elementals: float32 [128, 4, 2, 2, 384], P('ts', 'gz')
The draws below stay inside these ranges and needn't reach their ends.
Inputs may be any that keep to these rules, and one draw needn't show every extreme that they name: Each of the three directions exactly once.
All inputs are finite; a program needn't handle non-finite values.
Results may differ from the reference program's by a relative error of at most 0.0045.
Values may be sent and summed in bfloat16 or wider, within the bound.
No kernel may reach another device: no remote copies, remote signals or barrier semaphores. Data moves between devices by JAX's collectives and lax.ppermute only.
A program may use at most 128 MiB of HBM per device.

```python
import math
import jax
import jax.numpy as jnp
from jax import lax

NEV = 128
ND = 3
NP = 2
LY = 32
NT = 4
LX = 32
LZ = 64


def plant(array, key, smallest, largest):
    dims = array.shape
    index_at = [jax.random.randint(jax.random.fold_in(key, axis), (), 0, dims[axis]) for axis in range(len(dims))]
    array = array.at[tuple(index_at)].set(smallest)
    longest = dims.index(max(dims))
    index_at[longest] = (index_at[longest] + 1) % dims[longest]
    return array.at[tuple(index_at)].set(largest)


def level_of(stream_key, shape, pieces, least, largest):
    factor_of, own = 1.0, jax.random.fold_in(stream_key, 6)
    for axis_at, shards_of in pieces:
        heights = jnp.exp(jax.random.uniform(jax.random.fold_in(own, axis_at), (shards_of,), jnp.float32, least / len(pieces), largest / len(pieces)))
        factor_of = factor_of * jnp.repeat(heights, shape[axis_at] // shards_of).reshape([-1 if axis == axis_at else 1 for axis in range(len(shape))])
    return factor_of


def normal_values(key, dims, deviation, limit, pieces=(), held_as=jnp.bfloat16):
    values = jax.random.normal(key, dims, jnp.float32) * deviation
    if len(pieces) > 0:
        values = level_of(key, dims, pieces, -0.22, 0.18) * values
    return jnp.clip(values, min=-limit, max=limit).astype(held_as)


def setup_inputs(seed: int = 0) -> dict:
    splits = jax.random.split(jax.random.key(seed), 5)
    eigvecs = normal_values(splits[0], (2, 3, NT, LX, LZ, LY, NEV), ((3 * LX * LY * LZ) ** -0.25), 0.25, ((3, 32), (4, 4)))
    gauge_links = normal_values(splits[1], (3, 18, NT, LX, LZ, LY), 0.57735, 3.5, ((3, 32), (4, 4)))
    momenta = plant(jax.random.randint(splits[2], (NP, 3), -2, 3), jax.random.fold_in(splits[2], 1), -2, 2).astype(jnp.int32)
    directions = jax.random.permutation(splits[3], 3).astype(jnp.int32)
    return {"eigvecs": eigvecs, "gauge_links": gauge_links, "momenta": momenta, "directions": directions}


def transport(link, vectors, adjoint):
    real_in = vectors[0]
    imag_in = vectors[1]
    real_out = []
    imag_out = []
    for a in range(3):
        real_sum = jnp.float32(0.0)
        imag_sum = jnp.float32(0.0)
        for b in range(3):
            if adjoint:
                entry = (b * 3 + a) * 2
                link_re = link[entry][..., None].astype(jnp.float32)
                link_im = -link[entry + 1][..., None].astype(jnp.float32)
            else:
                entry = (a * 3 + b) * 2
                link_re = link[entry][..., None].astype(jnp.float32)
                link_im = link[entry + 1][..., None].astype(jnp.float32)
            vec_re = real_in[b].astype(jnp.float32)
            vec_im = imag_in[b].astype(jnp.float32)
            real_sum = real_sum + link_re * vec_re - link_im * vec_im
            imag_sum = imag_sum + link_re * vec_im + link_im * vec_re
        real_out.append(real_sum)
        imag_out.append(imag_sum)
    return jnp.stack([jnp.stack(real_out), jnp.stack(imag_out)])


def fraction(component, coords, length):
    return jnp.mod(component[:, None] * coords[None, :], length).astype(jnp.float32) / length


def phase_angle(momenta, x_first, z_first, count_x, count_z, count_y, total_x, total_z, total_y):
    coord_x = x_first + jnp.arange(count_x, dtype=jnp.int32)
    coord_z = z_first + jnp.arange(count_z, dtype=jnp.int32)
    coord_y = jnp.arange(count_y, dtype=jnp.int32)
    frac_x = fraction(momenta[:, 0], coord_x, total_x)
    frac_y = fraction(momenta[:, 1], coord_y, total_y)
    frac_z = fraction(momenta[:, 2], coord_z, total_z)
    return (2.0 * math.pi) * ((frac_x[:, :, None, None] + frac_y[:, None, None, :]) + frac_z[:, None, :, None])


def reference(eigvecs, gauge_links, momenta, directions):
    angle = phase_angle(momenta, 0, 0, LX, LZ, LY, LX, LZ, LY)
    cosine = jnp.cos(angle)[:, None, :, :, :, None]
    sine = jnp.sin(angle)[:, None, :, :, :, None]

    def one_slice(t):
        vectors = lax.dynamic_index_in_dim(eigvecs, t, 2, keepdims=False)
        links = lax.dynamic_index_in_dim(gauge_links, t, 2, keepdims=False)
        axes_of = (2, 4, 3)
        shifted = []
        for k in range(3):
            back = transport(links[k], vectors, True).astype(jnp.bfloat16)
            ahead = jnp.roll(vectors, -1, axis=axes_of[k])
            behind = jnp.roll(back, 1, axis=axes_of[k])
            term = 0.5 * (transport(links[k], ahead, False) - behind.astype(jnp.float32))
            shifted.append(term.astype(jnp.bfloat16))
        displaced = jnp.stack(shifted)[directions]
        right_two = jnp.stack([displaced, jnp.stack([displaced[:, 1], -displaced[:, 0]], axis=1)])
        real_in = vectors[0].astype(jnp.float32)
        imag_in = vectors[1].astype(jnp.float32)
        phased = jnp.stack([cosine * real_in - sine * imag_in, sine * real_in + cosine * imag_in], axis=1).astype(jnp.bfloat16)
        result = jnp.einsum('pqcxzyi,rdqcxzyj->iprdj', phased.astype(jnp.float32), right_two.astype(jnp.float32), precision=lax.Precision.HIGHEST)
        return result.reshape(NEV, NP, 2, ND * NEV)

    slices = lax.map(one_slice, jnp.arange(NT, dtype=jnp.int32))
    return jnp.transpose(slices, (1, 0, 2, 3, 4))
```

```python
import functools
import math

import jax
import jax.numpy as jnp
from jax import lax
from jax.experimental import pallas as pl
from jax.experimental.pallas import tpu as pltpu
from jax.sharding import PartitionSpec as P

BF16 = jnp.bfloat16
F32 = jnp.float32


def link_rows(entries, adjoint, width):
    rows = []
    for r in range(2):
        for a in range(3):
            pieces = []
            for q in range(2):
                for b in range(3):
                    first = ((b * 3 + a) if adjoint else (a * 3 + b)) * 2
                    if r == q:
                        pieces.append(entries[first])
                    elif (q == 1) == adjoint:
                        pieces.append(entries[first + 1])
                    else:
                        pieces.append(-entries[first + 1])
            lanes = sum(piece.shape[1] for piece in pieces)
            if lanes < width:
                pieces.append(jnp.zeros((pieces[0].shape[0], width - lanes), F32))
            rows.append(jnp.concatenate(pieces, axis=1))
    return rows


def site_masks(count_y, lanes):
    row = lax.broadcasted_iota(jnp.int32, (count_y, lanes), 0)
    lane = lax.broadcasted_iota(jnp.int32, (count_y, lanes), 1) % count_y
    same = jnp.where(lane == row, 1.0, 0.0).astype(BF16)
    above = jnp.where(lane == (row + 1) % count_y, 1.0, 0.0).astype(BF16)
    below = jnp.where(lane == (row + count_y - 1) % count_y, 1.0, 0.0).astype(BF16)
    return same, above, below


def spread(rows_ref, kind, row, mask):
    count_y, lanes = mask.shape
    blocks = []
    for ra in range(6):
        line = rows_ref[kind, ra, pl.ds(row, 1), :lanes]
        blocks.append(jnp.broadcast_to(line, (count_y, lanes)).astype(BF16) * mask)
    return jnp.concatenate(blocks, axis=0)


def write_phased(vectors, table_ref, x_at, out_ref, first):
    _, _, count_z, count_y, nev = vectors.shape
    planes = nev // count_y
    for b in range(3):
        for block in range(count_z // planes):
            sites = pl.ds(block * planes, planes)
            real = vectors[0, b, sites].reshape(nev, nev).T.astype(F32)
            imag = vectors[1, b, sites].reshape(nev, nev).T.astype(F32)
            lanes = pl.ds(first + b * count_z * count_y + block * nev, nev)
            for p in range(2):
                cosine = table_ref[x_at, 2 * p : 2 * p + 1, block * nev : (block + 1) * nev]
                sine = table_ref[x_at, 2 * p + 1 : 2 * p + 2, block * nev : (block + 1) * nev]
                out_ref[pl.ds(2 * p * nev, nev), lanes] = (cosine * real - sine * imag).astype(BF16)
                out_ref[pl.ds((2 * p + 1) * nev, nev), lanes] = (sine * real + cosine * imag).astype(BF16)


def put_displaced(out_ref, where, z, terms, count_y, nev):
    for r in range(2):
        for a in range(3):
            rows = terms[(r * 3 + a) * count_y : (r * 3 + a + 1) * count_y]
            out_ref[where, a, z, :, r * nev : (r + 1) * nev] = rows.astype(BF16)


def combine(products, nev):
    parts = []
    for p in range(2):
        rr = products[2 * p * nev : (2 * p + 1) * nev, :nev]
        ri = products[2 * p * nev : (2 * p + 1) * nev, nev:]
        ir = products[(2 * p + 1) * nev : (2 * p + 2) * nev, :nev]
        ii = products[(2 * p + 1) * nev : (2 * p + 2) * nev, nev:]
        parts.append(rr + ii)
        parts.append(ri - ir)
    return parts


def yz_kernel(v_ref, up_ref, down_ref, link_ref, below_ref, table_ref, out_ref, rows, padded, phased, moved):
    count_z, count_y, nev = v_ref.shape[3:]
    lanes = 6 * count_y
    same, above, below = site_masks(count_y, lanes)
    padded[:, :, 0] = down_ref[:, :, 0, 0]
    padded[:, :, pl.ds(1, count_z)] = v_ref[:, :, 0]
    padded[:, :, count_z + 1] = up_ref[:, :, 0, 0]

    wide = rows.shape[3]
    lane = lax.broadcasted_iota(jnp.int32, (count_z, wide), 1) % count_y
    link_y = [0.5 * link_ref[1, e, 0].astype(F32) for e in range(18)]
    for ra, line in enumerate(link_rows(link_y, False, wide)):
        shifted = jnp.where(lane == 0, pltpu.roll(line, wide - (count_y - 1), 1), pltpu.roll(line, 1, 1))
        rows[0, ra, pl.ds(8, count_z), :] = shifted
    for ra, line in enumerate(link_rows(link_y, True, wide)):
        rows[1, ra, pl.ds(8, count_z), :] = -line
    link_z = [0.5 * link_ref[2, e, 0].astype(F32) for e in range(18)]
    for ra, line in enumerate(link_rows(link_z, False, wide)):
        rows[2, ra, pl.ds(8, count_z), :] = line
    for ra, line in enumerate(link_rows(link_z, True, wide)):
        rows[3, ra, pl.ds(8, count_z), :] = -line
    link_b = [0.5 * below_ref[e, 0].astype(F32) for e in range(18)]
    for ra, line in enumerate(link_rows(link_b, True, wide)):
        rows[3, ra, 7:8, :] = -line

    write_phased(v_ref.at[:, :, 0], table_ref, 0, phased, 0)

    def plane(z, carry):
        here = padded[:, :, z + 1].reshape(lanes, nev)
        ahead = padded[:, :, z + 2].reshape(lanes, nev)
        behind = padded[:, :, z].reshape(lanes, nev)
        in_y = spread(rows, 0, z + 8, above) + spread(rows, 1, z + 8, below)
        terms = jnp.dot(in_y, here, preferred_element_type=F32)
        put_displaced(moved, 0, z, terms, count_y, nev)
        terms = jnp.dot(spread(rows, 2, z + 8, same), ahead, preferred_element_type=F32)
        terms += jnp.dot(spread(rows, 3, z + 7, same), behind, preferred_element_type=F32)
        put_displaced(moved, 1, z, terms, count_y, nev)
        return carry

    lax.fori_loop(0, count_z, plane, 0, unroll=2)
    for k in range(2):
        products = jnp.dot(
            phased[...], moved[k].reshape(-1, 2 * nev), preferred_element_type=F32
        )
        for at, part in enumerate(combine(products, nev)):
            out_ref[0, :, (2 * at + k) * nev : (2 * at + k + 1) * nev] = part.astype(BF16)


def x_terms(low, high, link, table_ref, x_low, x_high, out_ref, at_t, rows, phased, moved):
    count_z, count_y, nev = low.shape[2:]
    lanes = 6 * count_y
    same = site_masks(count_y, lanes)[0]
    entries = [0.5 * link[e].astype(F32) for e in range(18)]
    for ra, line in enumerate(link_rows(entries, False, lanes)):
        rows[0, ra] = line
    for ra, line in enumerate(link_rows(entries, True, lanes)):
        rows[1, ra] = -line
    sites = 3 * count_z * count_y
    write_phased(low, table_ref, x_low, phased, 0)
    write_phased(high, table_ref, x_high, phased, sites)

    def plane(z, carry):
        terms = jnp.dot(spread(rows, 0, z, same), high[:, :, z].reshape(lanes, nev), preferred_element_type=F32)
        put_displaced(moved, 0, z, terms, count_y, nev)
        terms = jnp.dot(spread(rows, 1, z, same), low[:, :, z].reshape(lanes, nev), preferred_element_type=F32)
        put_displaced(moved, 1, z, terms, count_y, nev)
        return carry

    lax.fori_loop(0, count_z, plane, 0, unroll=2)
    products = jnp.dot(phased[...], moved[...].reshape(-1, 2 * nev), preferred_element_type=F32)
    for at, part in enumerate(combine(products, nev)):
        out_ref[at_t, :, at * nev : (at + 1) * nev] = part.astype(BF16)


def x_kernel(own_up, recv_up, own_down, recv_down, link_up, link_down, table_ref, out_ref, rows, phased, moved):
    x_terms(
        own_up.at[:, :, 0], recv_up.at[:, :, 0], link_up.at[0, :, 0], table_ref, 0, 1, out_ref, 0, rows, phased, moved
    )
    x_terms(
        recv_down.at[:, :, 0], own_down.at[:, :, 0], link_down.at[:, 0], table_ref, 2, 0, out_ref, 1, rows, phased, moved
    )


def fraction(component, coords, length):
    return jnp.mod(component[:, None] * coords[None, :], length).astype(F32) / length


def phase_table(momenta, coord_x, coord_z, coord_y, total_x, total_z, total_y):
    frac_x = fraction(momenta[:, 0], coord_x, total_x)
    frac_y = fraction(momenta[:, 1], coord_y, total_y)
    frac_z = fraction(momenta[:, 2], coord_z, total_z)
    angle = 2.0 * math.pi * (
        (frac_x[:, :, None, None] + frac_y[:, None, None, :]) + frac_z[:, None, :, None]
    )
    table = jnp.stack([jnp.cos(angle), jnp.sin(angle)], axis=1)
    table = jnp.transpose(table, (2, 0, 1, 3, 4))
    return table.reshape(coord_x.shape[0], 4, coord_z.shape[0] * coord_y.shape[0])


def shift(value, axis, steps):
    count = lax.axis_size(axis)
    return lax.ppermute(value, axis, [(source, (source + steps) % count) for source in range(count)])


def shards(eigvecs, gauge_links, momenta, directions):
    _, _, count_t, _, count_z, count_y, nev = eigvecs.shape
    vectors = eigvecs.reshape(2, 3, count_t, count_z, count_y, nev)
    links = gauge_links.reshape(3, 18, count_t, count_z, count_y)
    size_x, size_g = lax.axis_size("ts"), lax.axis_size("gz")
    half = count_t // 2

    recv_up, recv_down = [], []
    for c in range(half):
        recv_up.append(shift(vectors[:, :, c : c + 1], "ts", -1))
        recv_down.append(shift(vectors[:, :, half + c : half + c + 1], "ts", 1))
    link_down = shift(links[0, :, half:], "ts", 1)
    up = shift(vectors[:, :, :, :1], "gz", -1)
    down = shift(vectors[:, :, :, -1:], "gz", 1)
    below = shift(links[2, :, :, -1:], "gz", 1)

    x = lax.axis_index("ts")
    coord_x = x + jnp.array([0, 1, -1], jnp.int32)
    coord_z = lax.axis_index("gz") * count_z + jnp.arange(count_z, dtype=jnp.int32)
    coord_y = jnp.arange(count_y, dtype=jnp.int32)
    table = phase_table(momenta, coord_x, coord_z, coord_y, size_x, count_z * size_g, count_y)

    sites = 3 * count_z * count_y
    table_spec = pl.BlockSpec(table.shape, lambda t: (0, 0, 0))
    yz = pl.pallas_call(
        yz_kernel,
        grid=(count_t,),
        in_specs=[
            pl.BlockSpec((2, 3, 1, count_z, count_y, nev), lambda t: (0, 0, t, 0, 0, 0)),
            pl.BlockSpec((2, 3, 1, 1, count_y, nev), lambda t: (0, 0, t, 0, 0, 0)),
            pl.BlockSpec((2, 3, 1, 1, count_y, nev), lambda t: (0, 0, t, 0, 0, 0)),
            pl.BlockSpec((3, 18, 1, count_z, count_y), lambda t: (0, 0, t, 0, 0)),
            pl.BlockSpec((18, 1, 1, count_y), lambda t: (0, t, 0, 0)),
            table_spec,
        ],
        out_specs=pl.BlockSpec((1, nev, 8 * nev), lambda t: (t, 0, 0)),
        out_shape=jax.ShapeDtypeStruct((count_t, nev, 8 * nev), BF16),
        scratch_shapes=[
            pltpu.VMEM((4, 6, count_z + 8, 256), F32),
            pltpu.VMEM((2, 3, count_z + 2, count_y, nev), BF16),
            pltpu.VMEM((4 * nev, sites), BF16),
            pltpu.VMEM((2, 3, count_z, count_y, 2 * nev), BF16),
        ],
        compiler_params=pltpu.CompilerParams(vmem_limit_bytes=40 * 1024 * 1024),
        cost_estimate=pl.CostEstimate(flops=12_000_000_000, bytes_accessed=6_000_000, transcendentals=0),
        name="yz_terms",
    )(vectors, up, down, links, below, table)

    x_parts = []
    for c in range(half):
        x_parts.append(
            pl.pallas_call(
                x_kernel,
                grid=(1,),
                in_specs=[
                    pl.BlockSpec((2, 3, 1, count_z, count_y, nev), functools.partial(lambda c, i: (0, 0, c, 0, 0, 0), c)),
                    pl.BlockSpec((2, 3, 1, count_z, count_y, nev), lambda i: (0, 0, 0, 0, 0, 0)),
                    pl.BlockSpec((2, 3, 1, count_z, count_y, nev), functools.partial(lambda c, i: (0, 0, c, 0, 0, 0), half + c)),
                    pl.BlockSpec((2, 3, 1, count_z, count_y, nev), lambda i: (0, 0, 0, 0, 0, 0)),
                    pl.BlockSpec((1, 18, 1, count_z, count_y), functools.partial(lambda c, i: (0, 0, c, 0, 0), c)),
                    pl.BlockSpec((18, 1, count_z, count_y), functools.partial(lambda c, i: (0, c, 0, 0), c)),
                    table_spec,
                ],
                out_specs=pl.BlockSpec((2, nev, 4 * nev), lambda i: (0, 0, 0)),
                out_shape=jax.ShapeDtypeStruct((2, nev, 4 * nev), BF16),
                scratch_shapes=[
                    pltpu.VMEM((2, 6, count_z, 6 * count_y), F32),
                    pltpu.VMEM((4 * nev, 2 * sites), BF16),
                    pltpu.VMEM((2, 3, count_z, count_y, 2 * nev), BF16),
                ],
                compiler_params=pltpu.CompilerParams(vmem_limit_bytes=40 * 1024 * 1024),
                cost_estimate=pl.CostEstimate(flops=6_000_000_000, bytes_accessed=4_000_000, transcendentals=0),
                name="x_terms",
            )(vectors, recv_up[c], vectors, recv_down[c], links, link_down, table)
        )
    order = [part[0] for part in x_parts] + [part[1] for part in x_parts]
    in_x = jnp.stack(order)

    group = nev // size_x
    both = jnp.concatenate([in_x, yz], axis=2).reshape(count_t, size_x, group, 12 * nev)
    sent = jnp.transpose(both, (1, 0, 2, 3)).reshape(size_x * count_t, group, 12 * nev)
    got = lax.all_to_all(sent, ("ts", "gz"), 0, 0, tiled=True)
    total = jnp.sum(got.astype(F32), axis=0)
    in_x = total[:, : 4 * nev].reshape(group, 4, 1, nev)
    in_yz = total[:, 4 * nev :].reshape(group, 4, 2, nev)
    chosen = jnp.take(jnp.concatenate([in_x, in_yz], axis=2), directions, axis=2)
    return chosen.reshape(group, 1, 2, 2, 3 * nev)


def solution(mesh):
    in_specs = (
        P(None, None, None, "ts", "gz", None, None),
        P(None, None, None, "ts", "gz", None),
        P(),
        P(),
    )
    out_specs = P("ts", "gz", None, None, None)
    return jax.shard_map(shards, mesh=mesh, in_specs=in_specs, out_specs=out_specs, check_vma=False)
```

```python
import functools
import math

import jax
import jax.numpy as jnp
from jax import lax
from jax.experimental import pallas as pl
from jax.experimental.pallas import tpu as pltpu
from jax.sharding import PartitionSpec as P

BF16 = jnp.bfloat16
F32 = jnp.float32


def link_rows(entries, adjoint, width):
    rows = []
    for r in range(2):
        for a in range(3):
            pieces = []
            for q in range(2):
                for b in range(3):
                    first = ((b * 3 + a) if adjoint else (a * 3 + b)) * 2
                    if r == q:
                        pieces.append(entries[first])
                    elif (q == 1) == adjoint:
                        pieces.append(entries[first + 1])
                    else:
                        pieces.append(-entries[first + 1])
            lanes = sum(piece.shape[1] for piece in pieces)
            if lanes < width:
                pieces.append(jnp.zeros((pieces[0].shape[0], width - lanes), F32))
            rows.append(jnp.concatenate(pieces, axis=1))
    return rows


def site_masks(count_y, lanes):
    row = lax.broadcasted_iota(jnp.int32, (count_y, lanes), 0)
    lane = lax.broadcasted_iota(jnp.int32, (count_y, lanes), 1) % count_y
    same = jnp.where(lane == row, 1.0, 0.0).astype(BF16)
    above = jnp.where(lane == (row + 1) % count_y, 1.0, 0.0).astype(BF16)
    below = jnp.where(lane == (row + count_y - 1) % count_y, 1.0, 0.0).astype(BF16)
    return same, above, below


def spread(rows_ref, kind, row, mask):
    count_y, lanes = mask.shape
    blocks = []
    for ra in range(6):
        line = rows_ref[kind, ra, pl.ds(row, 1), :lanes]
        blocks.append(jnp.broadcast_to(line, (count_y, lanes)).astype(BF16) * mask)
    return jnp.concatenate(blocks, axis=0)


def write_phased(planes_of, table, table_first, blocks, out_ref, first, colour_stride):
    for b in range(3):
        for block in range(blocks):
            real = planes_of(0, b, block).T.astype(F32)
            imag = planes_of(1, b, block).T.astype(F32)
            nev, sites = real.shape
            at = first + b * colour_stride + block * sites
            put_phased(real, imag, table, table_first + block * sites, out_ref, at)


def put_phased(real, imag, table, table_at, out_ref, at):
    nev, sites = real.shape
    for p in range(2):
        cosine = table[2 * p : 2 * p + 1, table_at : table_at + sites]
        sine = table[2 * p + 1 : 2 * p + 2, table_at : table_at + sites]
        out_ref[2 * p * nev : (2 * p + 1) * nev, at : at + sites] = (cosine * real - sine * imag).astype(BF16)
        out_ref[(2 * p + 1) * nev : (2 * p + 2) * nev, at : at + sites] = (sine * real + cosine * imag).astype(BF16)


def put_displaced(out_ref, z, terms, count_y, nev):
    for r in range(2):
        for a in range(3):
            rows = terms[(r * 3 + a) * count_y : (r * 3 + a + 1) * count_y]
            out_ref[a, z, :, r * nev : (r + 1) * nev] = rows.astype(BF16)


def combine(products, nev):
    real, imag = [], []
    for p in range(2):
        rr = products[2 * p * nev : (2 * p + 1) * nev, :nev]
        ri = products[2 * p * nev : (2 * p + 1) * nev, nev:]
        ir = products[(2 * p + 1) * nev : (2 * p + 2) * nev, :nev]
        ii = products[(2 * p + 1) * nev : (2 * p + 2) * nev, nev:]
        real.append(rr + ii)
        imag.append(ri - ir)
    return real + imag


def by_owner(first, second):
    nev, lanes = first.shape
    a = first.reshape(nev // 8, 8, lanes)
    b = second.reshape(nev // 8, 8, lanes)
    upper = lax.broadcasted_iota(jnp.int32, a.shape, 1) < 4
    even = jnp.where(upper, a, pltpu.roll(b, 4, 1))
    odd = jnp.where(upper, pltpu.roll(a, 4, 1), b)
    return jnp.stack([even, odd], axis=1).reshape(nev // 4, 8, lanes)


def put_partials(out_ref, m, at, parts):
    real = by_owner(parts[0], parts[1])
    imag = by_owner(parts[2], parts[3])
    nev = parts[0].shape[1]
    out_ref[:, m, :, at * nev : (at + 1) * nev] = jnp.concatenate([real, imag], axis=1).astype(BF16)


def yz_kernel(core_ref, v_ref, swap0_ref, swap1_ref, halo_ref, link_ref, swap_link_ref, table_ref, out_ref,
              rows, padded, phased, moved_y, moved_z, extra):
    m = pl.program_id(0)
    core = core_ref[0]
    count_z, count_y, nev = v_ref.shape[3:]
    deep = 2 * count_z
    lanes = 6 * count_y
    sites = deep * count_y
    same, above, below = site_masks(count_y, lanes)
    mine = pl.multiple_of(core * count_z, count_z)
    theirs = pl.multiple_of((1 - core) * count_z, count_z)
    padded[:, :, pl.ds(mine, count_z)] = v_ref[:, :, 0]

    @pl.when(m == 0)
    def _():
        padded[:, :, pl.ds(theirs, count_z)] = swap0_ref[:, :, 0]

    @pl.when(m == 1)
    def _():
        padded[:, :, pl.ds(theirs, count_z)] = swap1_ref[:, :, 0]

    padded[:, :, deep] = halo_ref[:, :, 0]

    wide = rows.shape[3]
    lane = lax.broadcasted_iota(jnp.int32, (count_z, wide), 1) % count_y
    for links, start in ((link_ref, mine), (swap_link_ref, theirs)):
        at = pl.ds(start, count_z)
        link_y = [0.5 * links[1, e, 0].astype(F32) for e in range(18)]
        for ra, line in enumerate(link_rows(link_y, False, wide)):
            rows[0, ra, at, :] = jnp.where(
                lane == 0, pltpu.roll(line, wide - (count_y - 1), 1), pltpu.roll(line, 1, 1)
            )
        for ra, line in enumerate(link_rows(link_y, True, wide)):
            rows[1, ra, at, :] = -line
        link_z = [0.5 * links[2, e, 0].astype(F32) for e in range(18)]
        for ra, line in enumerate(link_rows(link_z, False, wide)):
            rows[2, ra, at, :] = line
        for ra, line in enumerate(link_rows(link_z, True, wide)):
            rows[3, ra, at, :] = -line

    table = table_ref[0]
    step = nev // count_y
    write_phased(
        lambda q, b, block: padded[q, b, block * step : (block + 1) * step].reshape(nev, nev),
        table, 0, sites // nev, phased, 0, sites,
    )
    put_phased(
        padded[0, :, deep].reshape(3 * count_y, nev).T.astype(F32),
        padded[1, :, deep].reshape(3 * count_y, nev).T.astype(F32),
        table, sites, phased, 3 * sites,
    )

    def forward(z):
        return jnp.dot(
            spread(rows, 2, z, same), padded[:, :, z + 1].reshape(lanes, nev), preferred_element_type=F32
        )

    def backward(z):
        return jnp.dot(
            spread(rows, 3, z - 1, same), padded[:, :, z - 1].reshape(lanes, nev), preferred_element_type=F32
        )

    def plane(z, carry):
        in_y = spread(rows, 0, z, above) + spread(rows, 1, z, below)
        terms = jnp.dot(in_y, padded[:, :, z].reshape(lanes, nev), preferred_element_type=F32)
        put_displaced(moved_y, z, terms, count_y, nev)
        return carry

    def between(z, carry):
        put_displaced(moved_z, z, forward(z) + backward(z), count_y, nev)
        return carry

    lax.fori_loop(0, deep, plane, 0, unroll=16)
    put_displaced(moved_z, 0, forward(0), count_y, nev)
    lax.fori_loop(1, deep, between, 0, unroll=16)
    terms = backward(deep)
    for r in range(2):
        half = terms[r * 3 * count_y : (r + 1) * 3 * count_y]
        extra[:, r * nev : (r + 1) * nev] = half.astype(BF16)

    products = jnp.dot(
        phased[:, : 3 * sites], moved_y[...].reshape(3 * sites, 2 * nev), preferred_element_type=F32
    )
    put_partials(out_ref, 0, 0, combine(products, nev))
    products = jnp.dot(
        phased[:, : 3 * sites], moved_z[...].reshape(3 * sites, 2 * nev), preferred_element_type=F32
    ) + jnp.dot(phased[:, 3 * sites : 3 * sites + 3 * count_y], extra[...], preferred_element_type=F32)
    put_partials(out_ref, 0, 1, combine(products, nev))


def x_terms(low, high, link, table_low, table_high, rows, phased, moved):
    count_z, count_y, nev = low.shape[2:]
    lanes = 6 * count_y
    same = site_masks(count_y, lanes)[0]
    entries = [0.5 * link[e].astype(F32) for e in range(18)]
    for ra, line in enumerate(link_rows(entries, False, lanes)):
        rows[0, ra] = line
    for ra, line in enumerate(link_rows(entries, True, lanes)):
        rows[1, ra] = -line
    sites = count_z * count_y
    step = nev // count_y
    for vectors, table, first in ((low, table_low, 0), (high, table_high, 3 * sites)):
        write_phased(
            lambda q, b, block: vectors[q, b, block * step : (block + 1) * step].reshape(nev, nev),
            table, 0, sites // nev, phased, first, sites,
        )

    def plane(z, carry):
        terms = jnp.dot(spread(rows, 0, z, same), high[:, :, z].reshape(lanes, nev), preferred_element_type=F32)
        put_displaced(moved.at[0], z, terms, count_y, nev)
        terms = jnp.dot(spread(rows, 1, z, same), low[:, :, z].reshape(lanes, nev), preferred_element_type=F32)
        put_displaced(moved.at[1], z, terms, count_y, nev)
        return carry

    lax.fori_loop(0, count_z, plane, 0, unroll=16)
    products = jnp.dot(phased[...], moved[...].reshape(6 * sites, 2 * nev), preferred_element_type=F32)
    return combine(products, nev)


def x_pairs(own_up, recv_up, own_down, recv_down, link_up, link_down, table_ref, rows, phased, moved):
    yield 0, x_terms(
        own_up.at[:, :, 0], recv_up.at[:, :, 0], link_up.at[0, :, 0], table_ref[0], table_ref[1], rows, phased, moved
    )
    yield 1, x_terms(
        recv_down.at[:, :, 0], own_down.at[:, :, 0], link_down.at[:, 0], table_ref[2], table_ref[0], rows, phased, moved
    )


def x_first_kernel(core_ref, own_up, recv_up, own_down, recv_down, link_up, link_down, table_ref, out_ref, *scratch):
    for m, parts in x_pairs(own_up, recv_up, own_down, recv_down, link_up, link_down, table_ref, *scratch):
        for at, part in enumerate(parts):
            out_ref[m, at] = part


def x_last_kernel(core_ref, own_up, recv_up, own_down, recv_down, link_up, link_down, table_ref, before, _, out_ref, *scratch):
    for m, parts in x_pairs(own_up, recv_up, own_down, recv_down, link_up, link_down, table_ref, *scratch):
        put_partials(out_ref, m, 0, [part + before[m, at] for at, part in enumerate(parts)])


def total_kernel(directions_ref, got_ref, out_ref):
    total = jnp.sum(got_ref[...].astype(F32), axis=0)
    nev = total.shape[1] // 3
    group = out_ref.shape[0]
    in_y, in_z, in_x = (total[:, k * nev : (k + 1) * nev] for k in range(3))
    for d in range(3):
        direction = directions_ref[d]
        chosen = jnp.where(direction == 0, in_x, jnp.where(direction == 1, in_y, in_z))
        for r in range(2):
            for p in range(2):
                for i in range(group):
                    row = (r * 2 + p) * group + i
                    out_ref[i, 0, p, r : r + 1, d * nev : (d + 1) * nev] = chosen[row : row + 1]


def fraction(component, coords, length):
    return jnp.mod(component[:, None] * coords[None, :], length).astype(F32) / length


def phase_table(momenta, coord_x, coord_z, coord_y, total_x, total_z, total_y):
    frac_x = fraction(momenta[:, 0], coord_x, total_x)
    frac_y = fraction(momenta[:, 1], coord_y, total_y)
    frac_z = fraction(momenta[:, 2], coord_z, total_z)
    angle = 2.0 * math.pi * (
        (frac_x[:, :, None, None] + frac_y[:, None, None, :]) + frac_z[:, None, :, None]
    )
    table = jnp.stack([jnp.cos(angle), jnp.sin(angle)], axis=1)
    table = jnp.transpose(table, (2, 0, 1, 3, 4))
    return table.reshape(coord_x.shape[0], 4, coord_z.shape[0] * coord_y.shape[0])


def shift(value, steps):
    count = lax.axis_size("ts")
    return lax.ppermute(value, "ts", [(source, (source + steps) % count) for source in range(count)])


def shards(eigvecs, gauge_links, momenta, directions):
    _, _, count_t, _, count_z, count_y, nev = eigvecs.shape
    vectors = eigvecs.reshape(2, 3, count_t, count_z, count_y, nev)
    links = gauge_links.reshape(3, 18, count_t, count_z, count_y)
    size_x, size_g = lax.axis_size("ts"), lax.axis_size("gz")
    x, g = lax.axis_index("ts"), lax.axis_index("gz")
    core, chip = g % 2, g // 2
    deep = 2 * count_z
    sites = count_z * count_y
    group = nev // size_x

    lowest = vectors[:, :, :, 0].reshape(2, 3, 2, 2, count_y, nev)
    halo = lax.ppermute(lowest[:, :, :, 0], "gz", [(0, 2), (2, 0)])
    halo += lax.ppermute(lowest[:, :, :, 1], "gz", [(0, 3), (2, 1)])

    def times(array, axis, at):
        return lax.dynamic_slice_in_dim(array, at, 1, axis)

    swap = [(0, 1), (1, 0), (2, 3), (3, 2)]
    recv_up = [shift(times(vectors, 2, core), -1)]
    recv_down = [shift(times(vectors, 2, core + 2), 1)]
    swap0 = lax.ppermute(times(vectors, 2, 1 - core), "gz", swap)
    swap1 = lax.ppermute(times(vectors, 2, 3 - core), "gz", swap)
    given = lax.dynamic_index_in_dim(links.reshape(3, 18, 2, 2, count_z, count_y), 1 - core, 3, keepdims=False)
    swap_links = lax.ppermute(given, "gz", swap)
    link_down = shift(jnp.concatenate([times(links[0], 1, core + 2), swap_links[0, :, 1:]], axis=1), 1)
    recv_up.append(shift(swap0, -1))
    recv_down.append(shift(swap1, 1))

    coord_x = x + jnp.array([0, 1, -1], jnp.int32)
    coord_z = chip * deep + jnp.arange(deep + 1, dtype=jnp.int32)
    coord_y = jnp.arange(count_y, dtype=jnp.int32)
    table = phase_table(momenta, coord_x, coord_z, coord_y, size_x, count_z * size_g, count_y)
    top = table[:1, :, 2 * sites :]
    table_yz = jnp.concatenate([table[:1, :, : 2 * sites], top, top, top], axis=2)
    table_x = [lax.dynamic_slice_in_dim(table, at * sites, sites, 2) for at in (core, 1 - core)]

    core_at = jnp.reshape(core, (1,)).astype(jnp.int32)
    limit = pltpu.CompilerParams(vmem_limit_bytes=48 * 1024 * 1024)
    whole = lambda shape: pl.BlockSpec(shape, lambda i, core: (0,) * len(shape))
    one_time = (2, 3, 1, count_z, count_y, nev)
    sent = pl.pallas_call(
        yz_kernel,
        grid_spec=pltpu.PrefetchScalarGridSpec(
            num_scalar_prefetch=1,
            grid=(2,),
            in_specs=[
                pl.BlockSpec(one_time, lambda m, core: (0, 0, core[0] + 2 * m, 0, 0, 0)),
                whole(one_time),
                whole(one_time),
                pl.BlockSpec((2, 3, 1, count_y, nev), lambda m, core: (0, 0, m, 0, 0)),
                pl.BlockSpec((3, 18, 1, count_z, count_y), lambda m, core: (0, 0, core[0] + 2 * m, 0, 0)),
                pl.BlockSpec((3, 18, 1, count_z, count_y), lambda m, core: (0, 0, m, 0, 0)),
                whole(table_yz.shape),
            ],
            out_specs=pl.BlockSpec((size_x, 1, 4 * group, 2 * nev), lambda m, core: (0, m, 0, 0)),
            scratch_shapes=[
                pltpu.VMEM((4, 6, deep, 256), F32),
                pltpu.VMEM((2, 3, deep + 1, count_y, nev), BF16),
                pltpu.VMEM((4 * nev, 6 * sites + nev), BF16),
                pltpu.VMEM((3, deep, count_y, 2 * nev), BF16),
                pltpu.VMEM((3, deep, count_y, 2 * nev), BF16),
                pltpu.VMEM((3 * count_y, 2 * nev), BF16),
            ],
        ),
        out_shape=jax.ShapeDtypeStruct((size_x, 2, 4 * group, 3 * nev), BF16),
        compiler_params=limit,
        cost_estimate=pl.CostEstimate(flops=9_000_000_000, bytes_accessed=6_000_000, transcendentals=0),
        name="yz_terms",
    )(core_at, vectors, swap0, swap1, halo, links, swap_links, table_yz)

    part = None
    for c in range(2):
        if c == 0:
            own = [vectors, vectors]
            own_specs = [
                pl.BlockSpec(one_time, lambda i, core: (0, 0, core[0], 0, 0, 0)),
                pl.BlockSpec(one_time, lambda i, core: (0, 0, core[0] + 2, 0, 0, 0)),
            ]
            link, link_spec = links, pl.BlockSpec((1, 18, 1, count_z, count_y), lambda i, core: (0, 0, core[0], 0, 0))
        else:
            own = [swap0, swap1]
            own_specs = [whole(one_time), whole(one_time)]
            link, link_spec = swap_links, whole((1, 18, 1, count_z, count_y))
        operands = [core_at, own[0], recv_up[c], own[1], recv_down[c], link, link_down, table_x[c]]
        in_specs = [
            own_specs[0],
            whole(one_time),
            own_specs[1],
            whole(one_time),
            link_spec,
            pl.BlockSpec((18, 1, count_z, count_y), functools.partial(lambda c, i, core: (0, c, 0, 0), c)),
            whole(table_x[c].shape),
        ]
        scratch = [
            pltpu.VMEM((2, 6, count_z, 6 * count_y), F32),
            pltpu.VMEM((4 * nev, 6 * sites), BF16),
            pltpu.VMEM((2, 3, count_z, count_y, 2 * nev), BF16),
        ]
        cost = pl.CostEstimate(flops=5_000_000_000, bytes_accessed=4_000_000, transcendentals=0)
        if c == 0:
            shape = (2, 4, nev, nev)
            part = pl.pallas_call(
                x_first_kernel,
                grid_spec=pltpu.PrefetchScalarGridSpec(
                    num_scalar_prefetch=1, grid=(1,), in_specs=in_specs, out_specs=whole(shape), scratch_shapes=scratch
                ),
                out_shape=jax.ShapeDtypeStruct(shape, F32),
                compiler_params=limit,
                cost_estimate=cost,
                name="x_first",
            )(*operands)
        else:
            sent = pl.pallas_call(
                x_last_kernel,
                grid_spec=pltpu.PrefetchScalarGridSpec(
                    num_scalar_prefetch=1,
                    grid=(1,),
                    in_specs=in_specs + [whole(part.shape), pl.BlockSpec(memory_space=pl.ANY)],
                    out_specs=pl.BlockSpec((size_x, 2, 4 * group, nev), lambda i, core: (0, 0, 0, 2)),
                    scratch_shapes=scratch,
                ),
                out_shape=jax.ShapeDtypeStruct(sent.shape, BF16),
                input_output_aliases={len(operands) + 1: 0},
                compiler_params=limit,
                cost_estimate=cost,
                name="x_last",
            )(*operands, part, sent)

    pieces = sent.reshape(2 * size_x, 4 * group, 3 * nev)
    groups = [[(ts * 2 + h) * 2 + c for ts in range(size_x) for h in range(2)] for c in range(2)]
    got = lax.all_to_all(pieces, ("ts", "gz"), 0, 0, tiled=True, axis_index_groups=groups)
    return pl.pallas_call(
        total_kernel,
        in_specs=[pl.BlockSpec(memory_space=pltpu.SMEM), pl.BlockSpec(memory_space=pltpu.VMEM)],
        out_specs=pl.BlockSpec(memory_space=pltpu.VMEM),
        out_shape=jax.ShapeDtypeStruct((group, 1, 2, 2, 3 * nev), F32),
        name="total",
    )(directions, got)


def solution(mesh):
    in_specs = (
        P(None, None, None, "ts", "gz", None, None),
        P(None, None, None, "ts", "gz", None),
        P(),
        P(),
    )
    out_specs = P("ts", "gz", None, None, None)
    return jax.shard_map(shards, mesh=mesh, in_specs=in_specs, out_specs=out_specs, check_vma=False)
```

```python
import functools
import math

import jax
import jax.numpy as jnp
from jax import lax
from jax.experimental import pallas as pl
from jax.experimental.pallas import tpu as pltpu
from jax.sharding import PartitionSpec as P

BF16 = jnp.bfloat16
F32 = jnp.float32


def link_rows(entries, adjoint, width):
    rows = []
    for r in range(2):
        for a in range(3):
            pieces = []
            for q in range(2):
                for b in range(3):
                    first = ((b * 3 + a) if adjoint else (a * 3 + b)) * 2
                    if r == q:
                        pieces.append(entries[first])
                    elif (q == 1) == adjoint:
                        pieces.append(entries[first + 1])
                    else:
                        pieces.append(-entries[first + 1])
            lanes = sum(piece.shape[1] for piece in pieces)
            if lanes < width:
                pieces.append(jnp.zeros((pieces[0].shape[0], width - lanes), F32))
            rows.append(jnp.concatenate(pieces, axis=1))
    return rows


def site_masks(count_y, lanes):
    row = lax.broadcasted_iota(jnp.int32, (count_y, lanes), 0)
    lane = lax.broadcasted_iota(jnp.int32, (count_y, lanes), 1) % count_y
    same = jnp.where(lane == row, 1.0, 0.0).astype(BF16)
    above = jnp.where(lane == (row + 1) % count_y, 1.0, 0.0).astype(BF16)
    below = jnp.where(lane == (row + count_y - 1) % count_y, 1.0, 0.0).astype(BF16)
    return same, above, below


def spread(rows_ref, kind, row, mask):
    count_y, lanes = mask.shape
    blocks = []
    for ra in range(6):
        line = rows_ref[kind, ra, pl.ds(row, 1), :lanes]
        blocks.append(jnp.broadcast_to(line, (count_y, lanes)).astype(BF16) * mask)
    return jnp.concatenate(blocks, axis=0)


def write_phased(planes_of, table, x_at, table_first, blocks, out_ref, first, colour_stride):
    for b in range(3):
        for block in range(blocks):
            real = planes_of(0, b, block).T.astype(F32)
            imag = planes_of(1, b, block).T.astype(F32)
            nev, sites = real.shape
            at = first + b * colour_stride + block * sites
            put_phased(real, imag, table, x_at, table_first + block * sites, out_ref, at)


def put_phased(real, imag, table, x_at, table_at, out_ref, at):
    nev, sites = real.shape
    for p in range(2):
        cosine, sine = (values[2 * x_at + p : 2 * x_at + p + 1, pl.ds(table_at, sites)] for values in table)
        out_ref[2 * p * nev : (2 * p + 1) * nev, at : at + sites] = (cosine * real - sine * imag).astype(BF16)
        out_ref[(2 * p + 1) * nev : (2 * p + 2) * nev, at : at + sites] = (sine * real + cosine * imag).astype(BF16)


def put_displaced(out_ref, z, terms, count_y, nev):
    for r in range(2):
        for a in range(3):
            rows = terms[(r * 3 + a) * count_y : (r * 3 + a + 1) * count_y]
            out_ref[a, z, :, r * nev : (r + 1) * nev] = rows.astype(BF16)


def combine(products, nev):
    real, imag = [], []
    for p in range(2):
        rr = products[2 * p * nev : (2 * p + 1) * nev, :nev]
        ri = products[2 * p * nev : (2 * p + 1) * nev, nev:]
        ir = products[(2 * p + 1) * nev : (2 * p + 2) * nev, :nev]
        ii = products[(2 * p + 1) * nev : (2 * p + 2) * nev, nev:]
        real.append(rr + ii)
        imag.append(ri - ir)
    return real + imag


def by_owner(first, second):
    nev, lanes = first.shape
    a = first.reshape(nev // 8, 8, lanes)
    b = second.reshape(nev // 8, 8, lanes)
    upper = lax.broadcasted_iota(jnp.int32, a.shape, 1) < 4
    even = jnp.where(upper, a, pltpu.roll(b, 4, 1))
    odd = jnp.where(upper, pltpu.roll(a, 4, 1), b)
    return jnp.stack([even, odd], axis=1).reshape(nev // 4, 8, lanes)


def put_partials(out_ref, m, at, parts):
    real = by_owner(parts[0], parts[1])
    imag = by_owner(parts[2], parts[3])
    nev = parts[0].shape[1]
    out_ref[:, m, :, at * nev : (at + 1) * nev] = jnp.concatenate([real, imag], axis=1).astype(BF16)


def packed_plane(packed, q, b, z, count, count_z, count_y):
    first = ((q * 3 + b) * count_z + z) * count_y
    return packed[first : first + count * count_y]


def link_planes(nev, count_z, count_y):
    return -(-18 * count_y * count_z // (nev * count_y))


def packed_link(packed, k, e, count_z, count_y):
    nev = packed.shape[1]
    per_row = nev // count_y
    first = (6 * count_z + k * link_planes(nev, count_z, count_y)) * count_y + e // per_row * count_z
    lane = e % per_row * count_y
    return packed[first : first + count_z, lane : lane + count_y]


def copy_vectors(v_ref, out_ref, at):
    _, _, _, count_z, count_y, nev = v_ref.shape
    for i in range(6):
        out_ref[at, i * count_z : (i + 1) * count_z] = v_ref[i // 3, i % 3, 0]


def pack_up_kernel(core_ref, v_ref, low_ref, up_ref, low0_ref, low1_ref):
    copy_vectors(v_ref, up_ref, 0)
    for m in range(2):
        low0_ref[:, :, m] = low_ref[:, :, 2 * m, 0]
        low1_ref[:, :, m] = low_ref[:, :, 2 * m + 1, 0]


def pack_links_kernel(directions, core_ref, v_ref, link_ref, out_ref):
    _, _, _, count_z, count_y, nev = v_ref.shape
    copy_vectors(v_ref, out_ref, 0)
    per_row = nev // count_y
    planes = link_planes(nev, count_z, count_y)
    per_plane = count_y // count_z
    for k in range(directions):
        for at in range(planes * per_plane):
            held = [link_ref[k, e, 0] for e in range(at * per_row, min(18, (at + 1) * per_row))]
            held += [jnp.zeros((count_z, count_y), BF16)] * (per_row - len(held))
            first = at % per_plane * count_z
            out_ref[0, 6 * count_z + k * planes + at // per_plane, first : first + count_z] = jnp.concatenate(
                held, axis=1
            )


def yz_kernel(core_ref, v_ref, swap_ref, halo_ref, link_ref, cosine_ref, sine_ref, out_ref,
              rows, padded, phased, moved_y, moved_z, extra):
    core = core_ref[0]
    count_z, count_y, nev = v_ref.shape[3:]
    deep = 2 * count_z
    lanes = 6 * count_y
    sites = deep * count_y
    same, above, below = site_masks(count_y, lanes)
    mine = pl.multiple_of(core * count_z, count_z)
    theirs = pl.multiple_of((1 - core) * count_z, count_z)
    wide = rows.shape[3]
    lane = lax.broadcasted_iota(jnp.int32, (count_z, wide), 1) % count_y

    def fill_rows(link, start):
        at = pl.ds(start, count_z)
        link_y = [0.5 * link(1, e).astype(F32) for e in range(18)]
        for ra, line in enumerate(link_rows(link_y, False, wide)):
            rows[0, ra, at, :] = jnp.where(
                lane == 0, pltpu.roll(line, wide - (count_y - 1), 1), pltpu.roll(line, 1, 1)
            )
        for ra, line in enumerate(link_rows(link_y, True, wide)):
            rows[1, ra, at, :] = -line
        link_z = [0.5 * link(2, e).astype(F32) for e in range(18)]
        for ra, line in enumerate(link_rows(link_z, False, wide)):
            rows[2, ra, at, :] = line
        for ra, line in enumerate(link_rows(link_z, True, wide)):
            rows[3, ra, at, :] = -line

    padded[:, :, pl.ds(mine, count_z)] = v_ref[:, :, 0]
    padded[:, :, deep] = halo_ref[:, :, 0]
    swapped = swap_ref.at[0]
    for q in range(2):
        for b in range(3):
            block = packed_plane(swapped, q, b, 0, count_z, count_z, count_y)
            padded[q, b, pl.ds(theirs, count_z)] = block.reshape(count_z, count_y, nev)
    fill_rows(lambda k, e: packed_link(swapped, k, e, count_z, count_y), theirs)
    fill_rows(lambda k, e: link_ref[k, e, 0], mine)

    table = cosine_ref, sine_ref
    step = nev // count_y
    write_phased(
        lambda q, b, block: padded[q, b, block * step : (block + 1) * step].reshape(nev, nev),
        table, 0, 0, sites // nev, phased, 0, sites,
    )
    put_phased(
        padded[0, :, deep].reshape(3 * count_y, nev).T.astype(F32),
        padded[1, :, deep].reshape(3 * count_y, nev).T.astype(F32),
        table, 0, sites, phased, 3 * sites,
    )

    def forward(z):
        return jnp.dot(
            spread(rows, 2, z, same), padded[:, :, z + 1].reshape(lanes, nev), preferred_element_type=F32
        )

    def backward(z):
        return jnp.dot(
            spread(rows, 3, z - 1, same), padded[:, :, z - 1].reshape(lanes, nev), preferred_element_type=F32
        )

    for z in range(deep):
        in_y = spread(rows, 0, z, above) + spread(rows, 1, z, below)
        terms = jnp.dot(in_y, padded[:, :, z].reshape(lanes, nev), preferred_element_type=F32)
        put_displaced(moved_y, z, terms, count_y, nev)
        terms = forward(z)
        if z > 0:
            terms += backward(z)
        put_displaced(moved_z, z, terms, count_y, nev)
    terms = backward(deep)
    for r in range(2):
        half = terms[r * 3 * count_y : (r + 1) * 3 * count_y]
        extra[:, r * nev : (r + 1) * nev] = half.astype(BF16)

    products = jnp.dot(
        phased[:, : 3 * sites], moved_y[...].reshape(3 * sites, 2 * nev), preferred_element_type=F32
    )
    put_partials(out_ref, 0, 0, combine(products, nev))
    products = jnp.dot(
        phased[:, : 3 * sites], moved_z[...].reshape(3 * sites, 2 * nev), preferred_element_type=F32
    ) + jnp.dot(phased[:, 3 * sites : 3 * sites + 3 * count_y], extra[...], preferred_element_type=F32)
    put_partials(out_ref, 0, 1, combine(products, nev))


def x_terms(low, high, link, table, table_first, x_low, x_high, rows, phased, moved):
    count_z, lanes = rows.shape[2:]
    count_y = lanes // 6
    nev = low.shape[1]
    same = site_masks(count_y, lanes)[0]
    entries = [0.5 * link(e).astype(F32) for e in range(18)]
    for ra, line in enumerate(link_rows(entries, False, lanes)):
        rows[0, ra] = line
    for ra, line in enumerate(link_rows(entries, True, lanes)):
        rows[1, ra] = -line
    sites = count_z * count_y
    for vectors, x_at, first in ((low, x_low, 0), (high, x_high, 3 * sites)):
        write_phased(
            lambda q, b, block: vectors[(q * 3 + b) * sites + block * nev : (q * 3 + b) * sites + (block + 1) * nev],
            table, x_at, table_first, sites // nev, phased, first, sites,
        )

    def plane(vectors, z):
        return jnp.concatenate(
            [packed_plane(vectors, q, b, z, 1, count_z, count_y) for q in range(2) for b in range(3)], axis=0
        )

    for z in range(count_z):
        terms = jnp.dot(spread(rows, 0, z, same), plane(high, z), preferred_element_type=F32)
        put_displaced(moved.at[0], z, terms, count_y, nev)
        terms = jnp.dot(spread(rows, 1, z, same), plane(low, z), preferred_element_type=F32)
        put_displaced(moved.at[1], z, terms, count_y, nev)
    products = jnp.dot(phased[...], moved[...].reshape(6 * sites, 2 * nev), preferred_element_type=F32)
    return combine(products, nev)


def x_first_kernel(core_ref, own_up, recv_up, own_down, recv_down, link_ref, cosine_ref, sine_ref, out_ref, rows, phased, moved):
    count_z, count_y = link_ref.shape[3:]
    table = cosine_ref, sine_ref
    at_table = pl.multiple_of(core_ref[0] * (count_z * count_y), count_z * count_y)
    parts = x_terms(
        own_up.at[0], recv_up.at[0], lambda e: link_ref[0, e, 0], table, at_table, 0, 1, rows, phased, moved
    )
    for at, part in enumerate(parts):
        out_ref[0, at] = part
    received = recv_down.at[0]
    parts = x_terms(
        received, own_down.at[0], lambda e: packed_link(received, 0, e, count_z, count_y),
        table, at_table, 2, 0, rows, phased, moved,
    )
    for at, part in enumerate(parts):
        out_ref[1, at] = part


def x_last_kernel(core_ref, swap_ref, recv_up, recv_down, cosine_ref, sine_ref, before, _, out_ref, rows, phased, moved):
    count_z, lanes = rows.shape[2:]
    count_y = lanes // 6
    table = cosine_ref, sine_ref
    at_table = pl.multiple_of((1 - core_ref[0]) * (count_z * count_y), count_z * count_y)
    first = swap_ref.at[0]
    parts = x_terms(
        first, recv_up.at[0], lambda e: packed_link(first, 0, e, count_z, count_y),
        table, at_table, 0, 1, rows, phased, moved,
    )
    put_partials(out_ref, 0, 0, [part + before[0, at] for at, part in enumerate(parts)])
    received = recv_down.at[0]
    parts = x_terms(
        received, swap_ref.at[1], lambda e: packed_link(received, 0, e, count_z, count_y),
        table, at_table, 2, 0, rows, phased, moved,
    )
    put_partials(out_ref, 1, 0, [part + before[1, at] for at, part in enumerate(parts)])


def total_kernel(directions_ref, got_ref, out_ref):
    total = jnp.sum(got_ref[...].astype(F32), axis=0)
    nev = total.shape[1] // 3
    group = out_ref.shape[0]
    in_y, in_z, in_x = (total[:, k * nev : (k + 1) * nev] for k in range(3))
    for d in range(3):
        direction = directions_ref[d]
        chosen = jnp.where(direction == 0, in_x, jnp.where(direction == 1, in_y, in_z))
        for r in range(2):
            for p in range(2):
                for i in range(group):
                    row = (r * 2 + p) * group + i
                    out_ref[i, 0, p, r : r + 1, d * nev : (d + 1) * nev] = chosen[row : row + 1]


def fraction(component, coords, length):
    return jnp.mod(component * coords, length).astype(F32) / length


def table_kernel(lengths, deep, place_ref, momenta_ref, cosine_ref, sine_ref):
    length_x, length_z, length_y = lengths
    shape = cosine_ref.shape
    row = lax.broadcasted_iota(jnp.int32, shape, 0)
    lane = lax.broadcasted_iota(jnp.int32, shape, 1)
    x_at = row // 2
    x = place_ref[0] + jnp.where(x_at == 2, -1, x_at)
    z = place_ref[1] + jnp.minimum(lane // length_y, deep)
    y = lane % length_y
    first = row % 2 == 0
    m_x, m_y, m_z = (jnp.where(first, momenta_ref[0, i], momenta_ref[1, i]) for i in range(3))
    angle = 2.0 * math.pi * (
        (fraction(m_x, x, length_x) + fraction(m_y, y, length_y)) + fraction(m_z, z, length_z)
    )
    cosine_ref[...] = jnp.cos(angle)
    sine_ref[...] = jnp.sin(angle)


def shift(value, steps):
    count = lax.axis_size("ts")
    return lax.ppermute(value, "ts", [(source, (source + steps) % count) for source in range(count)])


def shards(eigvecs, gauge_links, momenta, directions):
    _, _, count_t, _, count_z, count_y, nev = eigvecs.shape
    vectors = eigvecs.reshape(2, 3, count_t, count_z, count_y, nev)
    links = gauge_links.reshape(3, 18, count_t, count_z, count_y)
    size_x, size_g = lax.axis_size("ts"), lax.axis_size("gz")
    x, g = lax.axis_index("ts"), lax.axis_index("gz")
    core, chip = g % 2, g // 2
    deep = 2 * count_z
    sites = count_z * count_y
    full = 6 * sites
    group = nev // size_x

    small = pl.CostEstimate(flops=1_000_000, bytes_accessed=100_000, transcendentals=0)
    limit = pltpu.CompilerParams(vmem_limit_bytes=48 * 1024 * 1024)
    in_vmem = pl.BlockSpec(memory_space=pltpu.VMEM)
    anywhere = pl.BlockSpec(memory_space=pl.ANY)
    planes = link_planes(nev, count_z, count_y)

    core_at = jnp.reshape(core, (1,)).astype(jnp.int32)
    one_time = (2, 3, 1, count_z, count_y, nev)

    def whole(shape):
        return pl.BlockSpec(shape, lambda i, core: (0,) * len(shape))

    lowest = (2, 3, 2, count_y, nev)
    up, low0, low1 = pl.pallas_call(
        pack_up_kernel,
        grid_spec=pltpu.PrefetchScalarGridSpec(
            num_scalar_prefetch=1,
            grid=(1,),
            in_specs=[
                pl.BlockSpec(one_time, lambda i, core: (0, 0, core[0], 0, 0, 0)),
                pl.BlockSpec((2, 3, count_t, 1, count_y, nev), lambda i, core: (0, 0, 0, 0, 0, 0)),
            ],
            out_specs=[whole((1, 6 * count_z, count_y, nev)), whole(lowest), whole(lowest)],
        ),
        out_shape=[
            jax.ShapeDtypeStruct((1, 6 * count_z, count_y, nev), BF16),
            jax.ShapeDtypeStruct(lowest, BF16),
            jax.ShapeDtypeStruct(lowest, BF16),
        ],
        compiler_params=limit,
        cost_estimate=small,
        name="pack_up",
    )(core_at, vectors, vectors)

    def pack_links(kept, times, first_of, core_at):
        shape = (times, 6 * count_z + kept * planes, count_y, nev)
        packed = pl.pallas_call(
            functools.partial(pack_links_kernel, kept),
            grid_spec=pltpu.PrefetchScalarGridSpec(
                num_scalar_prefetch=1,
                grid=(times,),
                in_specs=[
                    pl.BlockSpec(one_time, lambda m, core: (0, 0, first_of(core[0]) + 2 * m, 0, 0, 0)),
                    pl.BlockSpec(
                        (kept, 18, 1, count_z, count_y), lambda m, core: (0, 0, first_of(core[0]) + 2 * m, 0, 0)
                    ),
                ],
                out_specs=pl.BlockSpec((1,) + shape[1:], lambda m, core: (m, 0, 0, 0)),
            ),
            out_shape=jax.ShapeDtypeStruct(shape, BF16),
            compiler_params=limit,
            cost_estimate=small,
            name="pack_links",
        )(core_at, vectors, links)
        return packed.reshape(times, -1, nev)

    halo = lax.ppermute(low0, "gz", [(0, 2), (2, 0)]) + lax.ppermute(low1, "gz", [(0, 3), (2, 1)])
    up, halo = lax.optimization_barrier((up.reshape(1, full, nev), halo))
    recv_up = [shift(up, -1)]
    down = pack_links(1, 1, lambda core: core + 2, core_at)
    down, _ = lax.optimization_barrier((down, halo))
    recv_down = [shift(down, 1)]
    given = pack_links(3, 2, lambda core: 1 - core, core_at)
    swapped = lax.ppermute(given, "gz", [(0, 1), (1, 0), (2, 3), (3, 2)])
    recv_up.append(shift(swapped[:1, :full], -1))
    recv_down.append(shift(swapped[1:, : full + planes * count_y], 1))

    shape = jax.ShapeDtypeStruct((8, 2 * sites + nev), F32)
    table = pl.pallas_call(
        functools.partial(table_kernel, (size_x, count_z * size_g, count_y), deep),
        in_specs=[pl.BlockSpec(memory_space=pltpu.SMEM)] * 2,
        out_specs=[in_vmem] * 2,
        out_shape=[shape, shape],
        cost_estimate=small,
        name="phase_table",
    )(jnp.stack([x, chip * deep]).astype(jnp.int32), momenta)

    sent = pl.pallas_call(
        yz_kernel,
        grid_spec=pltpu.PrefetchScalarGridSpec(
            num_scalar_prefetch=1,
            grid=(2,),
            in_specs=[
                pl.BlockSpec((2, 3, 1, count_z, count_y, nev), lambda m, core: (0, 0, core[0] + 2 * m, 0, 0, 0)),
                pl.BlockSpec((1,) + swapped.shape[1:], lambda m, core: (m, 0, 0)),
                pl.BlockSpec((2, 3, 1, count_y, nev), lambda m, core: (0, 0, m, 0, 0)),
                pl.BlockSpec((3, 18, 1, count_z, count_y), lambda m, core: (0, 0, core[0] + 2 * m, 0, 0)),
                whole(shape.shape),
                whole(shape.shape),
            ],
            out_specs=pl.BlockSpec((size_x, 1, 4 * group, 2 * nev), lambda m, core: (0, m, 0, 0)),
            scratch_shapes=[
                pltpu.VMEM((4, 6, deep, 256), F32),
                pltpu.VMEM((2, 3, deep + 1, count_y, nev), BF16),
                pltpu.VMEM((4 * nev, 6 * sites + nev), BF16),
                pltpu.VMEM((3, deep, count_y, 2 * nev), BF16),
                pltpu.VMEM((3, deep, count_y, 2 * nev), BF16),
                pltpu.VMEM((3 * count_y, 2 * nev), BF16),
            ],
        ),
        out_shape=jax.ShapeDtypeStruct((size_x, 2, 4 * group, 3 * nev), BF16),
        compiler_params=limit,
        cost_estimate=small,
        name="yz_terms",
    )(core_at, vectors, swapped, halo, links, *table)

    core_at, _ = lax.optimization_barrier((core_at, sent))
    scratch = [
        pltpu.VMEM((2, 6, count_z, 6 * count_y), F32),
        pltpu.VMEM((4 * nev, 6 * sites), BF16),
        pltpu.VMEM((2, 3, count_z, count_y, 2 * nev), BF16),
    ]
    part = pl.pallas_call(
        x_first_kernel,
        grid_spec=pltpu.PrefetchScalarGridSpec(
            num_scalar_prefetch=1,
            grid=(1,),
            in_specs=[
                whole(up.shape),
                whole(up.shape),
                whole(down.shape),
                whole(down.shape),
                pl.BlockSpec((1, 18, 1, count_z, count_y), lambda i, core: (0, 0, core[0], 0, 0)),
                whole(shape.shape),
                whole(shape.shape),
            ],
            out_specs=whole((2, 4, nev, nev)),
            scratch_shapes=scratch,
        ),
        out_shape=jax.ShapeDtypeStruct((2, 4, nev, nev), F32),
        compiler_params=limit,
        cost_estimate=small,
        name="x_first",
    )(core_at, up, recv_up[0], down, recv_down[0], links, *table)
    sent = pl.pallas_call(
        x_last_kernel,
        grid=(1,),
        in_specs=[pl.BlockSpec(memory_space=pltpu.SMEM)] + [in_vmem] * 6 + [anywhere],
        out_specs=pl.BlockSpec((size_x, 2, 4 * group, nev), lambda i: (0, 0, 0, 2)),
        out_shape=jax.ShapeDtypeStruct(sent.shape, BF16),
        scratch_shapes=scratch,
        input_output_aliases={7: 0},
        compiler_params=limit,
        cost_estimate=small,
        name="x_last",
    )(core_at, swapped, recv_up[1], recv_down[1], *table, part, sent)

    pieces = sent.reshape(2 * size_x, 4 * group, 3 * nev)
    groups = [[(ts * 2 + h) * 2 + c for ts in range(size_x) for h in range(2)] for c in range(2)]
    got = lax.all_to_all(pieces, ("ts", "gz"), 0, 0, tiled=True, axis_index_groups=groups)
    return pl.pallas_call(
        total_kernel,
        in_specs=[pl.BlockSpec(memory_space=pltpu.SMEM), in_vmem],
        out_specs=in_vmem,
        out_shape=jax.ShapeDtypeStruct((group, 1, 2, 2, 3 * nev), F32),
        name="total",
    )(directions, got)


def solution(mesh):
    in_specs = (
        P(None, None, None, "ts", "gz", None, None),
        P(None, None, None, "ts", "gz", None),
        P(),
        P(),
    )
    out_specs = P("ts", "gz", None, None, None)
    return jax.shard_map(shards, mesh=mesh, in_specs=in_specs, out_specs=out_specs, check_vma=False)
```

```python
import functools
import math

import jax
import jax.numpy as jnp
from jax import lax
from jax.experimental import pallas as pl
from jax.experimental.pallas import tpu as pltpu
from jax.sharding import PartitionSpec as P

BF16 = jnp.bfloat16
F32 = jnp.float32


def link_rows(entries, adjoint, width):
    rows = []
    for r in range(2):
        for a in range(3):
            pieces = []
            for q in range(2):
                for b in range(3):
                    first = ((b * 3 + a) if adjoint else (a * 3 + b)) * 2
                    if r == q:
                        pieces.append(entries[first])
                    elif (q == 1) == adjoint:
                        pieces.append(entries[first + 1])
                    else:
                        pieces.append(-entries[first + 1])
            lanes = sum(piece.shape[1] for piece in pieces)
            if lanes < width:
                pieces.append(jnp.zeros((pieces[0].shape[0], width - lanes), F32))
            rows.append(jnp.concatenate(pieces, axis=1))
    return rows


def site_masks(count_y, lanes):
    row = lax.broadcasted_iota(jnp.int32, (count_y, lanes), 0)
    lane = lax.broadcasted_iota(jnp.int32, (count_y, lanes), 1) % count_y
    same = jnp.where(lane == row, 1.0, 0.0).astype(BF16)
    above = jnp.where(lane == (row + 1) % count_y, 1.0, 0.0).astype(BF16)
    below = jnp.where(lane == (row + count_y - 1) % count_y, 1.0, 0.0).astype(BF16)
    return same, above, below


def spread(rows_ref, kind, row, mask):
    count_y, lanes = mask.shape
    blocks = []
    for ra in range(6):
        line = rows_ref[kind, ra, pl.ds(row, 1), :lanes]
        blocks.append(jnp.broadcast_to(line, (count_y, lanes)).astype(BF16) * mask)
    return jnp.concatenate(blocks, axis=0)


def fraction(component, coords, length):
    return jnp.mod(component * coords, length).astype(F32) / length


def fill_table(lengths, deep, place_ref, momenta_ref, table_ref):
    length_x, length_z, length_y = lengths
    rows = table_ref.shape[0] // 2
    shape = rows, table_ref.shape[1]
    row = lax.broadcasted_iota(jnp.int32, shape, 0)
    lane = lax.broadcasted_iota(jnp.int32, shape, 1)
    x_at = row // 2
    x = place_ref[1] + jnp.where(x_at == 2, -1, x_at)
    plane = lane // length_y
    above = deep + (shape[1] // length_y - deep) // 2
    z = place_ref[2] + jnp.where(plane < deep, plane, jnp.where(plane < above, deep, deep - 1))
    y = lane % length_y
    first = row % 2 == 0
    m_x, m_y, m_z = (jnp.where(first, momenta_ref[0, i], momenta_ref[1, i]) for i in range(3))
    angle = 2.0 * math.pi * (
        (fraction(m_x, x, length_x) + fraction(m_y, y, length_y)) + fraction(m_z, z, length_z)
    )
    table_ref[:rows] = jnp.cos(angle)
    table_ref[rows:] = jnp.sin(angle)


def write_phased(planes_of, table, x_at, table_first, blocks, out_ref, first, colour_stride):
    for b in range(3):
        for block in range(blocks):
            real = planes_of(0, b, block).T.astype(F32)
            imag = planes_of(1, b, block).T.astype(F32)
            nev, sites = real.shape
            at = first + b * colour_stride + block * sites
            put_phased(real, imag, table, x_at, table_first + block * sites, out_ref, at)


def put_phased(real, imag, table, x_at, table_at, out_ref, at):
    nev, sites = real.shape
    for p in range(2):
        cosine, sine = (table[pl.ds(half + 2 * x_at + p, 1), pl.ds(table_at, sites)] for half in (0, table.shape[0] // 2))
        out_ref[2 * p * nev : (2 * p + 1) * nev, at : at + sites] = (cosine * real - sine * imag).astype(BF16)
        out_ref[(2 * p + 1) * nev : (2 * p + 2) * nev, at : at + sites] = (sine * real + cosine * imag).astype(BF16)


def put_displaced(out_ref, z, terms, count_y, nev):
    for r in range(2):
        for a in range(3):
            rows = terms[(r * 3 + a) * count_y : (r * 3 + a + 1) * count_y]
            out_ref[a, z, :, r * nev : (r + 1) * nev] = rows.astype(BF16)


def combine(products, nev):
    real, imag = [], []
    for p in range(2):
        rr = products[2 * p * nev : (2 * p + 1) * nev, :nev]
        ri = products[2 * p * nev : (2 * p + 1) * nev, nev:]
        ir = products[(2 * p + 1) * nev : (2 * p + 2) * nev, :nev]
        ii = products[(2 * p + 1) * nev : (2 * p + 2) * nev, nev:]
        real.append(rr + ii)
        imag.append(ri - ir)
    return real + imag


def by_owner(first, second):
    nev, lanes = first.shape
    a = first.reshape(nev // 8, 8, lanes)
    b = second.reshape(nev // 8, 8, lanes)
    upper = lax.broadcasted_iota(jnp.int32, a.shape, 1) < 4
    even = jnp.where(upper, a, pltpu.roll(b, 4, 1))
    odd = jnp.where(upper, pltpu.roll(a, 4, 1), b)
    return jnp.stack([even, odd], axis=1).reshape(nev // 4, 8, lanes)


def partial_rows(parts):
    return jnp.concatenate([by_owner(parts[0], parts[1]), by_owner(parts[2], parts[3])], axis=1)


def packed_plane(packed, depth, q, b, z, count, count_y):
    first = ((q * 3 + b) * depth + z) * count_y
    return packed[first : first + count * count_y]


def link_planes(nev, count_z, count_y):
    return -(-18 * count_y * count_z // (nev * count_y))


def packed_link(packed, depth, k, e, count_z, count_y):
    nev = packed.shape[1]
    per_row = nev // count_y
    first = (6 * depth + k * link_planes(nev, count_z, count_y)) * count_y + e // per_row * count_z
    lane = e % per_row * count_y
    return packed[first : first + count_z, lane : lane + count_y]


def pack_kernel(times, core_ref, v_ref, link_ref, *out_refs):
    _, _, _, count_z, count_y, nev = v_ref.shape
    per_row = nev // count_y
    planes = link_planes(nev, count_z, count_y)
    per_plane = count_y // count_z
    step = pl.program_id(0)

    def put(out_ref, directions):
        for i in range(6):
            out_ref[0, i * count_z : (i + 1) * count_z] = v_ref[i // 3, i % 3, 0]
        for k in range(directions):
            for at in range(planes * per_plane):
                held = [link_ref[k, e, 0] for e in range(at * per_row, min(18, (at + 1) * per_row))]
                held += [jnp.zeros((count_z, count_y), BF16)] * (per_row - len(held))
                plane = 6 * count_z + k * planes + at // per_plane
                first = at % per_plane * count_z
                out_ref[0, plane, first : first + count_z] = jnp.concatenate(held, axis=1)

    if times == 1:
        pl.when(step == 0)(lambda: put(out_refs[0], 0))
        pl.when(step == 1)(lambda: put(out_refs[1], 1))
    else:
        put(out_refs[0], 3)


def split(swap_ref, start, count_z, up_ref, down_ref):
    depth = up_ref.shape[1] // 6
    for i in range(6):
        first = i * count_z + start
        up_ref[0, i * depth : (i + 1) * depth] = swap_ref[0, first : first + depth]
        down_ref[0, i * depth : (i + 1) * depth] = swap_ref[1, first : first + depth]
    planes = down_ref.shape[1] - 6 * depth
    down_ref[0, 6 * depth :] = swap_ref[1, 6 * count_z : 6 * count_z + planes]


def split_first_kernel(count_z, core_ref, swap_ref, low_ref, up_ref, down_ref, lowest_ref):
    split(swap_ref, 0, count_z, up_ref, down_ref)
    core = core_ref[0]
    for m in range(2):
        for i in range(6):
            own = low_ref[i // 3, i % 3, core + 2 * m, 0]
            lowest_ref[m, i] = jnp.where(core == 0, own, swap_ref[m, i * count_z])


def split_last_kernel(count_z, core_ref, swap_ref, up_ref, down_ref):
    split(swap_ref, count_z - up_ref.shape[1] // 6, count_z, up_ref, down_ref)


def yz_kernel(lengths, place_ref, v_ref, swap_ref, link_ref, momenta_ref, out_ref, top_ref, line_ref, table_ref,
              rows, padded, phased, moved_y, moved_z):
    core = place_ref[0]
    count_z, count_y, nev = v_ref.shape[3:]
    deep = 2 * count_z
    lanes = 6 * count_y
    sites = deep * count_y
    same, above, below = site_masks(count_y, lanes)
    mine = pl.multiple_of(core * count_z, count_z)
    theirs = pl.multiple_of((1 - core) * count_z, count_z)
    wide = rows.shape[3]
    lane = lax.broadcasted_iota(jnp.int32, (count_z, wide), 1) % count_y

    def fill_rows(link, start):
        at = pl.ds(start, count_z)
        link_y = [0.5 * link(1, e).astype(F32) for e in range(18)]
        for ra, line in enumerate(link_rows(link_y, False, wide)):
            rows[0, ra, at, :] = jnp.where(
                lane == 0, pltpu.roll(line, wide - (count_y - 1), 1), pltpu.roll(line, 1, 1)
            )
        for ra, line in enumerate(link_rows(link_y, True, wide)):
            rows[1, ra, at, :] = -line
        link_z = [0.5 * link(2, e).astype(F32) for e in range(18)]
        for ra, line in enumerate(link_rows(link_z, False, wide)):
            rows[2, ra, at, :] = line
        for ra, line in enumerate(link_rows(link_z, True, wide)):
            rows[3, ra, at, :] = -line

    padded[:, :, pl.ds(mine, count_z)] = v_ref[:, :, 0]
    swapped = swap_ref.at[0]
    for q in range(2):
        for b in range(3):
            block = packed_plane(swapped, count_z, q, b, 0, count_z, count_y)
            padded[q, b, pl.ds(theirs, count_z)] = block.reshape(count_z, count_y, nev)
    fill_rows(lambda k, e: packed_link(swapped, count_z, k, e, count_z, count_y), theirs)
    fill_rows(lambda k, e: link_ref[k, e, 0], mine)

    pl.when(pl.program_id(0) == 0)(lambda: fill_table(lengths, deep, place_ref, momenta_ref, table_ref))
    table = table_ref
    step = nev // count_y
    write_phased(
        lambda q, b, block: padded[q, b, block * step : (block + 1) * step].reshape(nev, nev),
        table, 0, 0, sites // nev, phased, 0, sites,
    )
    def forward(z):
        return jnp.dot(
            spread(rows, 2, z, same), padded[:, :, z + 1].reshape(lanes, nev), preferred_element_type=F32
        )

    def backward(z):
        return jnp.dot(
            spread(rows, 3, z - 1, same), padded[:, :, z - 1].reshape(lanes, nev), preferred_element_type=F32
        )

    for z in range(deep):
        in_y = spread(rows, 0, z, above) + spread(rows, 1, z, below)
        terms = jnp.dot(in_y, padded[:, :, z].reshape(lanes, nev), preferred_element_type=F32)
        put_displaced(moved_y, z, terms, count_y, nev)
        terms = forward(z) if z + 1 < deep else 0.0
        if z > 0:
            terms += backward(z)
        put_displaced(moved_z, z, terms, count_y, nev)
    for at, moved in enumerate((moved_y, moved_z)):
        products = jnp.dot(phased[...], moved[...].reshape(3 * sites, 2 * nev), preferred_element_type=F32)
        out_ref[:, 0, :, at * nev : (at + 1) * nev] = partial_rows(combine(products, nev)).astype(BF16)
    top_ref[0] = padded[:, :, deep - 1].reshape(lanes, nev)
    for kind in range(2):
        for ra in range(6):
            line_ref[0, kind * 8 + ra : kind * 8 + ra + 1] = rows[2 + kind, ra, deep - 1 : deep]


def x_terms(low, high, link, table, table_first, x_low, x_high, rows, phased, moved):
    held_z, lanes = rows.shape[2:]
    count_z, count_y = moved.shape[2:4]
    nev = low[0].shape[1]
    same = site_masks(count_y, lanes)[0]
    entries = [0.5 * link(e).astype(F32) for e in range(18)]
    for ra, line in enumerate(link_rows(entries, False, lanes)):
        rows[0, ra] = line
    for ra, line in enumerate(link_rows(entries, True, lanes)):
        rows[1, ra] = -line
    sites = count_z * count_y
    step = nev // count_y
    for (vectors, depth, z), x_at, first in ((low, x_low, 0), (high, x_high, 3 * sites)):
        write_phased(
            lambda q, b, block: packed_plane(vectors, depth, q, b, z + block * step, step, count_y),
            table, x_at, table_first, sites // nev, phased, first, sites,
        )

    def plane(held, at):
        vectors, depth, z = held
        return jnp.concatenate(
            [packed_plane(vectors, depth, q, b, z + at, 1, count_y) for q in range(2) for b in range(3)], axis=0
        )

    first = max(low[2], high[2])
    for z in range(count_z):
        terms = jnp.dot(spread(rows, 0, first + z, same), plane(high, z), preferred_element_type=F32)
        put_displaced(moved.at[0], z, terms, count_y, nev)
        terms = jnp.dot(spread(rows, 1, first + z, same), plane(low, z), preferred_element_type=F32)
        put_displaced(moved.at[1], z, terms, count_y, nev)
    products = jnp.dot(phased[...], moved[...].reshape(6 * sites, 2 * nev), preferred_element_type=F32)
    return combine(products, nev)


def x_first_kernel(core_ref, own_up, recv_up, own_down, recv_down, link_ref, table, out_ref, *scratch):
    count_z, count_y = link_ref.shape[3:]
    at_table = pl.multiple_of(core_ref[0] * (count_z * count_y), count_z * count_y)
    received = recv_down.at[0]
    up = x_terms(
        (own_up.at[0], count_z, 0), (recv_up.at[0], count_z, 0), lambda e: link_ref[0, e, 0],
        table, at_table, 0, 1, *scratch,
    )
    down = x_terms(
        (received, count_z, 0), (own_down.at[0], count_z, 0),
        lambda e: packed_link(received, count_z, 0, e, count_z, count_y),
        table, at_table, 2, 0, *scratch,
    )
    for m, parts in enumerate((up, down)):
        for at, part in enumerate(parts):
            out_ref[m, at] = part


def x_part(last, core_ref, swap_ref, recv_up, recv_down, table, rows, phased, moved):
    held_z = rows.shape[2]
    depth, count_y = moved.shape[2:4]
    first = held_z - depth if last else 0
    nev = swap_ref.shape[2]
    at_table = pl.multiple_of((1 - core_ref[0]) * (held_z * count_y) + first * count_y, nev)
    own_up, own_down, received = swap_ref.at[0], swap_ref.at[1], recv_down.at[0]
    up = x_terms(
        (own_up, held_z, first), (recv_up.at[0], depth, 0),
        lambda e: packed_link(own_up, held_z, 0, e, held_z, count_y),
        table, at_table, 0, 1, rows, phased, moved,
    )
    down = x_terms(
        (received, depth, 0), (own_down, held_z, first),
        lambda e: packed_link(received, depth, 0, e, held_z, count_y),
        table, at_table, 2, 0, rows, phased, moved,
    )
    return up, down


def x_middle_kernel(core_ref, swap_ref, recv_up, recv_down, table, before, out_ref, *scratch):
    both = x_part(False, core_ref, swap_ref, recv_up, recv_down, table, *scratch)
    for m, parts in enumerate(both):
        for at, part in enumerate(parts):
            out_ref[m, at] = part + before[m, at]


def boundary(top, halo, lines, table, edge):
    lanes, nev = top.shape
    count_y = lanes // 6
    wide = lanes // 2
    same = site_masks(count_y, lanes)[0]

    def matrix(kind):
        blocks = []
        for ra in range(6):
            line = lines[kind * 8 + ra : kind * 8 + ra + 1, :lanes]
            blocks.append(jnp.broadcast_to(line, (count_y, lanes)).astype(BF16) * same)
        return jnp.concatenate(blocks, axis=0)

    products = 0.0
    for at, (phased, moved, kind) in enumerate(((top, halo, 0), (halo, top, 1))):
        put_phased(
            phased[:wide].T.astype(F32), phased[wide:].T.astype(F32), table, 0,
            table.shape[1] - (at + 1) * nev, edge, at * nev,
        )
        terms = jnp.dot(matrix(kind), moved[...], preferred_element_type=F32).astype(BF16)
        displaced = jnp.concatenate([terms[:wide], terms[wide:]], axis=1)
        products += jnp.dot(edge[:, at * nev : at * nev + wide], displaced, preferred_element_type=F32)
    return combine(products, nev)


def x_last_kernel(core_ref, swap_ref, recv_up, recv_down, table, before, sent_ref,
                  top_ref, halo_ref, line_ref, out_ref, rows, phased, moved, edge):
    nev = before.shape[3]
    out_ref[:, :, :, :nev] = sent_ref[:, :, :, :nev]
    for m in range(2):
        above = partial_rows(boundary(top_ref.at[m], halo_ref.at[m], line_ref.at[m], table, edge))
        out_ref[:, m, :, nev : 2 * nev] = (sent_ref[:, m, :, nev:].astype(F32) + above).astype(BF16)
    both = x_part(True, core_ref, swap_ref, recv_up, recv_down, table, rows, phased, moved)
    for m, parts in enumerate(both):
        parts = [part + before[m, at] for at, part in enumerate(parts)]
        out_ref[:, m, :, 2 * nev :] = partial_rows(parts).astype(BF16)


def total_kernel(directions_ref, got_ref, out_ref):
    total = jnp.sum(got_ref[...].astype(F32), axis=0)
    nev = total.shape[1] // 3
    group = out_ref.shape[0]
    in_y, in_z, in_x = (total[:, k * nev : (k + 1) * nev] for k in range(3))
    for d in range(3):
        direction = directions_ref[d]
        chosen = jnp.where(direction == 0, in_x, jnp.where(direction == 1, in_y, in_z))
        for r in range(2):
            for p in range(2):
                for i in range(group):
                    row = (r * 2 + p) * group + i
                    out_ref[i, 0, p, r : r + 1, d * nev : (d + 1) * nev] = chosen[row : row + 1]


def shift(value, steps):
    count = lax.axis_size("ts")
    return lax.ppermute(value, "ts", [(source, (source + steps) % count) for source in range(count)])


def shards(eigvecs, gauge_links, momenta, directions):
    _, _, count_t, _, count_z, count_y, nev = eigvecs.shape
    vectors = eigvecs.reshape(2, 3, count_t, count_z, count_y, nev)
    links = gauge_links.reshape(3, 18, count_t, count_z, count_y)
    size_x, size_g = lax.axis_size("ts"), lax.axis_size("gz")
    x, g = lax.axis_index("ts"), lax.axis_index("gz")
    core, chip = g % 2, g // 2
    deep = 2 * count_z
    sites = count_z * count_y
    group = nev // size_x

    small = pl.CostEstimate(flops=1_000_000, bytes_accessed=100_000, transcendentals=0)
    limit = pltpu.CompilerParams(vmem_limit_bytes=28 * 1024 * 1024)
    in_vmem = pl.BlockSpec(memory_space=pltpu.VMEM)
    in_smem = pl.BlockSpec(memory_space=pltpu.SMEM)
    planes = link_planes(nev, count_z, count_y)

    core_at = jnp.reshape(core, (1,)).astype(jnp.int32)
    one_time = (2, 3, 1, count_z, count_y, nev)

    def whole(shape):
        return pl.BlockSpec(shape, lambda i, core: (0,) * len(shape))

    def packed(times, depth, directions):
        return times, 6 * depth + directions * planes, count_y, nev

    def arrays(*shapes):
        return [jax.ShapeDtypeStruct(array, BF16) for array in shapes]

    def rows(array):
        return array.reshape(array.shape[0], -1, nev)

    def pack(name, first_of, shapes, times):
        if times == 1:
            out_specs = [whole(shape) for shape in shapes]
        else:
            out_specs = [pl.BlockSpec((1,) + shapes[0][1:], lambda i, core: (i, 0, 0, 0))]
        return pl.pallas_call(
            functools.partial(pack_kernel, times),
            grid_spec=pltpu.PrefetchScalarGridSpec(
                num_scalar_prefetch=1,
                grid=(2,),
                in_specs=[
                    pl.BlockSpec(one_time, lambda i, core: (0, 0, first_of(core[0]) + 2 * i, 0, 0, 0)),
                    pl.BlockSpec((3, 18, 1, count_z, count_y), lambda i, core: (0, 0, first_of(core[0]) + 2 * i, 0, 0)),
                ],
                out_specs=out_specs,
            ),
            out_shape=arrays(*shapes),
            compiler_params=pltpu.CompilerParams(vmem_limit_bytes=28 * 1024 * 1024),
            cost_estimate=small,
            name=name,
        )

    up, down = pack("pack_own", lambda core: core, (packed(1, count_z, 0), packed(1, count_z, 1)), 1)(
        core_at, vectors, links
    )
    after, _ = lax.optimization_barrier((core_at, up))
    (given,) = pack("pack_given", lambda core: 1 - core, (packed(2, count_z, 3),), 2)(after, vectors, links)
    recv_up = [shift(rows(up), -1)]
    recv_down = [shift(rows(down), 1)]
    swapped = lax.ppermute(given, "gz", [(0, 1), (1, 0), (2, 3), (3, 2)])
    tail = nev // count_y
    lead = count_z - tail
    shapes = packed(1, lead, 0), packed(1, lead, 1), (2, 6, count_y, nev)
    up_a, down_a, lowest = pl.pallas_call(
        functools.partial(split_first_kernel, count_z),
        grid_spec=pltpu.PrefetchScalarGridSpec(
            num_scalar_prefetch=1,
            grid=(1,),
            in_specs=[
                whole(swapped.shape),
                pl.BlockSpec((2, 3, count_t, 1, count_y, nev), lambda i, core: (0, 0, 0, 0, 0, 0)),
            ],
            out_specs=[whole(shape) for shape in shapes],
        ),
        out_shape=arrays(*shapes),
        compiler_params=limit,
        cost_estimate=small,
        name="split_first",
    )(core_at, swapped, vectors)
    recv_up.append(shift(rows(up_a), -1))
    recv_down.append(shift(rows(down_a), 1))
    halo = lax.ppermute(rows(lowest), "gz", [(0, 2), (2, 0), (1, 3), (3, 1)])

    place = jnp.stack([core, x, chip * deep]).astype(jnp.int32)
    place, _ = lax.optimization_barrier((place, up_a))
    wide = jax.ShapeDtypeStruct((16, 2 * sites + 2 * nev), F32)
    sent, top, lines, table = pl.pallas_call(
        functools.partial(yz_kernel, (size_x, count_z * size_g, count_y)),
        grid_spec=pltpu.PrefetchScalarGridSpec(
            num_scalar_prefetch=1,
            grid=(2,),
            in_specs=[
                pl.BlockSpec(one_time, lambda m, core: (0, 0, core[0] + 2 * m, 0, 0, 0)),
                pl.BlockSpec((1,) + rows(swapped).shape[1:], lambda m, core: (m, 0, 0)),
                pl.BlockSpec((3, 18, 1, count_z, count_y), lambda m, core: (0, 0, core[0] + 2 * m, 0, 0)),
                in_smem,
            ],
            out_specs=[
                pl.BlockSpec((size_x, 1, 4 * group, 2 * nev), lambda m, core: (0, m, 0, 0)),
                pl.BlockSpec((1, 6 * count_y, nev), lambda m, core: (m, 0, 0)),
                pl.BlockSpec((1, 16, 2 * nev), lambda m, core: (m, 0, 0)),
                whole(wide.shape),
            ],
            scratch_shapes=[
                pltpu.VMEM((4, 6, deep, 2 * nev), F32),
                pltpu.VMEM((2, 3, deep, count_y, nev), BF16),
                pltpu.VMEM((4 * nev, 6 * sites), BF16),
                pltpu.VMEM((3, deep, count_y, 2 * nev), BF16),
                pltpu.VMEM((3, deep, count_y, 2 * nev), BF16),
            ],
        ),
        out_shape=[
            jax.ShapeDtypeStruct((size_x, 2, 4 * group, 2 * nev), BF16),
            jax.ShapeDtypeStruct((2, 6 * count_y, nev), BF16),
            jax.ShapeDtypeStruct((2, 16, 2 * nev), F32),
            wide,
        ],
        compiler_params=limit,
        cost_estimate=small,
        name="yz_terms",
    )(place, vectors, rows(swapped), links, momenta)

    core_at, _ = lax.optimization_barrier((core_at, sent))
    shapes = packed(1, tail, 0), packed(1, tail, 1)
    up_b, down_b = pl.pallas_call(
        functools.partial(split_last_kernel, count_z),
        in_specs=[in_smem, in_vmem],
        out_specs=[in_vmem] * 2,
        out_shape=arrays(*shapes),
        compiler_params=limit,
        cost_estimate=small,
        name="split_last",
    )(core_at, swapped)
    recv_up.append(shift(rows(up_b), -1))
    recv_down.append(shift(rows(down_b), 1))

    def scratch(depth):
        return [
            pltpu.VMEM((2, 6, count_z, 6 * count_y), F32),
            pltpu.VMEM((4 * nev, 6 * depth * count_y), BF16),
            pltpu.VMEM((2, 3, depth, count_y, 2 * nev), BF16),
        ]

    parts = jax.ShapeDtypeStruct((2, 4, nev, nev), F32)
    part = pl.pallas_call(
        x_first_kernel,
        grid_spec=pltpu.PrefetchScalarGridSpec(
            num_scalar_prefetch=1,
            grid=(1,),
            in_specs=[whole(array.shape) for array in (rows(up), recv_up[0], rows(down), recv_down[0])]
            + [pl.BlockSpec((1, 18, 1, count_z, count_y), lambda i, core: (0, 0, core[0], 0, 0))]
            + [whole(wide.shape)],
            out_specs=whole(parts.shape),
            scratch_shapes=scratch(count_z),
        ),
        out_shape=parts,
        compiler_params=limit,
        cost_estimate=small,
        name="x_first",
    )(core_at, rows(up), recv_up[0], rows(down), recv_down[0], links, table)
    part = pl.pallas_call(
        x_middle_kernel,
        in_specs=[in_smem] + [in_vmem] * 5,
        out_specs=in_vmem,
        out_shape=parts,
        scratch_shapes=scratch(lead),
        compiler_params=limit,
        cost_estimate=small,
        name="x_middle",
    )(core_at, rows(swapped), recv_up[1], recv_down[1], table, part)
    sent = pl.pallas_call(
        x_last_kernel,
        in_specs=[in_smem] + [in_vmem] * 9,
        out_specs=in_vmem,
        out_shape=jax.ShapeDtypeStruct((size_x, 2, 4 * group, 3 * nev), BF16),
        scratch_shapes=scratch(tail) + [pltpu.VMEM((4 * nev, 2 * nev), BF16)],
        compiler_params=limit,
        cost_estimate=small,
        name="x_last",
    )(core_at, rows(swapped), recv_up[2], recv_down[2], table, part, sent, top, halo, lines)

    pieces = sent.reshape(2 * size_x, 4 * group, 3 * nev)
    groups = [[(ts * 2 + h) * 2 + c for ts in range(size_x) for h in range(2)] for c in range(2)]
    got = lax.all_to_all(pieces, ("ts", "gz"), 0, 0, tiled=True, axis_index_groups=groups)
    return pl.pallas_call(
        total_kernel,
        in_specs=[in_smem, in_vmem],
        out_specs=in_vmem,
        out_shape=jax.ShapeDtypeStruct((group, 1, 2, 2, 3 * nev), F32),
        name="total",
    )(directions, got)


def solution(mesh):
    in_specs = (
        P(None, None, None, "ts", "gz", None, None),
        P(None, None, None, "ts", "gz", None),
        P(),
        P(),
    )
    out_specs = P("ts", "gz", None, None, None)
    return jax.shard_map(shards, mesh=mesh, in_specs=in_specs, out_specs=out_specs, check_vma=False)
```

```python
import functools
import math

import jax
import jax.numpy as jnp
from jax import lax
from jax.experimental import pallas as pl
from jax.experimental.pallas import tpu as pltpu
from jax.sharding import PartitionSpec as P

BF16 = jnp.bfloat16
F32 = jnp.float32


def link_rows(entries, adjoint, width):
    rows = []
    for r in range(2):
        for a in range(3):
            pieces = []
            for q in range(2):
                for b in range(3):
                    first = ((b * 3 + a) if adjoint else (a * 3 + b)) * 2
                    if r == q:
                        pieces.append(entries[first])
                    elif (q == 1) == adjoint:
                        pieces.append(entries[first + 1])
                    else:
                        pieces.append(-entries[first + 1])
            lanes = sum(piece.shape[1] for piece in pieces)
            if lanes < width:
                pieces.append(jnp.zeros((pieces[0].shape[0], width - lanes), F32))
            rows.append(jnp.concatenate(pieces, axis=1))
    return rows


def site_masks(count_y, lanes):
    row = lax.broadcasted_iota(jnp.int32, (count_y, lanes), 0)
    lane = lax.broadcasted_iota(jnp.int32, (count_y, lanes), 1) % count_y
    same = jnp.where(lane == row, 1.0, 0.0).astype(BF16)
    above = jnp.where(lane == (row + 1) % count_y, 1.0, 0.0).astype(BF16)
    below = jnp.where(lane == (row + count_y - 1) % count_y, 1.0, 0.0).astype(BF16)
    return same, above, below


def spread(rows_ref, kind, row, mask):
    count_y, lanes = mask.shape
    blocks = []
    for ra in range(6):
        line = rows_ref[kind, ra, pl.ds(row, 1), :lanes]
        blocks.append(jnp.broadcast_to(line, (count_y, lanes)).astype(BF16) * mask)
    return jnp.concatenate(blocks, axis=0)


def fraction(component, coords, length):
    return jnp.mod(component * coords, length).astype(F32) / length


def table_kernel(lengths, deep, place_ref, momenta_ref, table_ref):
    length_x, length_z, length_y = lengths
    half = table_ref.shape[0] // 2
    shape = 2 * half, table_ref.shape[2]
    row = lax.broadcasted_iota(jnp.int32, shape, 0)
    lane = lax.broadcasted_iota(jnp.int32, shape, 1)
    x_at = row // 2
    x = place_ref[1] + jnp.where(x_at == 2, -1, x_at)
    plane = lane // length_y
    above = deep + (shape[1] // length_y - deep) // 2
    z = place_ref[2] + jnp.where(plane < deep, plane, jnp.where(plane < above, deep, deep - 1))
    y = lane % length_y
    first = row % 2 == 0
    m_x, m_y, m_z = (jnp.where(first, momenta_ref[0, i], momenta_ref[1, i]) for i in range(3))
    angle = 2.0 * math.pi * (
        (fraction(m_x, x, length_x) + fraction(m_y, y, length_y)) + fraction(m_z, z, length_z)
    )
    for first, values in ((0, jnp.cos(angle)), (half, jnp.sin(angle))):
        for at in range(2 * half):
            table_ref[first + at // 2, at % 2 : at % 2 + 1] = values[at : at + 1]


def write_phased(planes_of, table, x_at, table_first, blocks, out_ref, first, colour_stride):
    for b in range(3):
        for block in range(blocks):
            real = planes_of(0, b, block).T.astype(F32)
            imag = planes_of(1, b, block).T.astype(F32)
            nev, sites = real.shape
            at = first + b * colour_stride + block * sites
            put_phased(real, imag, table, x_at, table_first + block * sites, out_ref, at)


def put_phased(real, imag, table, x_at, table_at, out_ref, at):
    nev, sites = real.shape
    for p in range(2):
        cosine, sine = (table[half + x_at, p : p + 1, pl.ds(table_at, sites)] for half in (0, table.shape[0] // 2))
        out_ref[2 * p * nev : (2 * p + 1) * nev, at : at + sites] = (cosine * real - sine * imag).astype(BF16)
        out_ref[(2 * p + 1) * nev : (2 * p + 2) * nev, at : at + sites] = (sine * real + cosine * imag).astype(BF16)


def put_displaced(out_ref, z, terms, count_y, nev):
    for r in range(2):
        for a in range(3):
            rows = terms[(r * 3 + a) * count_y : (r * 3 + a + 1) * count_y]
            out_ref[a, z, :, r * nev : (r + 1) * nev] = rows.astype(BF16)


def combine(products, nev):
    real, imag = [], []
    for p in range(2):
        rr = products[2 * p * nev : (2 * p + 1) * nev, :nev]
        ri = products[2 * p * nev : (2 * p + 1) * nev, nev:]
        ir = products[(2 * p + 1) * nev : (2 * p + 2) * nev, :nev]
        ii = products[(2 * p + 1) * nev : (2 * p + 2) * nev, nev:]
        real.append(rr + ii)
        imag.append(ri - ir)
    return real + imag


def by_owner(first, second):
    nev, lanes = first.shape
    a = first.reshape(nev // 8, 8, lanes)
    b = second.reshape(nev // 8, 8, lanes)
    upper = lax.broadcasted_iota(jnp.int32, a.shape, 1) < 4
    even = jnp.where(upper, a, pltpu.roll(b, 4, 1))
    odd = jnp.where(upper, pltpu.roll(a, 4, 1), b)
    return jnp.stack([even, odd], axis=1).reshape(nev // 4, 8, lanes)


def partial_rows(parts):
    return jnp.concatenate([by_owner(parts[0], parts[1]), by_owner(parts[2], parts[3])], axis=1)


def packed_plane(packed, depth, q, b, z, count, count_y):
    first = ((q * 3 + b) * depth + z) * count_y
    return packed[first : first + count * count_y]


def link_planes(nev, count_z, count_y):
    return -(-18 * count_y * count_z // (nev * count_y))


def packed_link(packed, depth, k, e, count_z, count_y):
    nev = packed.shape[1]
    per_row = nev // count_y
    first = (6 * depth + k * link_planes(nev, count_z, count_y)) * count_y + e // per_row * count_z
    lane = e % per_row * count_y
    return packed[first : first + count_z, lane : lane + count_y]


def put_links(out_ref, at, first_plane, link, count_z, count_y, nev):
    per_row = nev // count_y
    per_plane = count_y // count_z
    for row in range(link_planes(nev, count_z, count_y) * per_plane):
        held = [link(e) for e in range(row * per_row, min(18, (row + 1) * per_row))]
        held += [jnp.zeros((count_z, count_y), BF16)] * (per_row - len(held))
        first = row % per_plane * count_z
        out_ref[at, first_plane + row // per_plane, first : first + count_z] = jnp.concatenate(held, axis=1)


def pack_kernel(place_ref, v_ref, link_ref, first_ref, second_ref, given_ref):
    count_z, count_y, nev = v_ref.shape[3:]
    core, odd = place_ref[0], place_ref[3]
    planes = link_planes(nev, count_z, count_y)
    for out_ref, at, t in (
        (first_ref, 0, core + 2 * (1 - odd)),
        (second_ref, 0, core + 2 * odd),
        (given_ref, 0, 1 - core),
        (given_ref, 1, 3 - core),
    ):
        for held in range(6):
            out_ref[at, held * count_z : (held + 1) * count_z] = v_ref[held // 3, held % 3, t]
    for out_ref, at, t, directions in (
        (first_ref, 0, core + 2 * (1 - odd), 1),
        (second_ref, 0, core + 2 * odd, 1),
        (given_ref, 0, 1 - core, 3),
        (given_ref, 1, 3 - core, 3),
    ):
        for k in range(directions):
            put_links(
                out_ref, at, 6 * count_z + k * planes, lambda e, k=k, t=t: link_ref[k, e, t], count_z, count_y, nev
            )


def split(place_ref, swap_ref, start, count_z, out_refs):
    odd = place_ref[3]
    for i, out_ref in enumerate(out_refs):
        m = odd if i else 1 - odd
        behind = out_ref.shape[1] % 6
        depth = out_ref.shape[1] // 6
        for held in range(6):
            first = held * count_z + start
            out_ref[0, held * depth : (held + 1) * depth] = swap_ref[m, first : first + depth]
        if behind:
            out_ref[0, 6 * depth :] = swap_ref[m, 6 * count_z : 6 * count_z + behind]


def split_first_kernel(count_z, place_ref, swap_ref, v_ref, first_ref, second_ref, lowest_ref):
    split(place_ref, swap_ref, 0, count_z, (first_ref, second_ref))
    core = place_ref[0]
    for m in range(2):
        for i in range(6):
            own = v_ref[i // 3, i % 3, core + 2 * m, 0]
            lowest_ref[m, i] = jnp.where(core == 0, own, swap_ref[m, i * count_z])


def split_last_kernel(count_z, place_ref, swap_ref, first_ref, second_ref):
    split(place_ref, swap_ref, count_z - first_ref.shape[1] // 6, count_z, (first_ref, second_ref))


def yz_kernel(place_ref, v_ref, swap_ref, link_ref, table_ref, out_ref, top_ref, line_ref,
              rows, padded, phased, moved_y, moved_z):
    core = place_ref[0]
    step_m = pl.program_id(0)
    t = core + 2 * step_m
    count_z, count_y, nev = v_ref.shape[3:]
    deep = 2 * count_z
    lanes = 6 * count_y
    sites = deep * count_y
    same, above, below = site_masks(count_y, lanes)
    mine = pl.multiple_of(core * count_z, count_z)
    theirs = pl.multiple_of((1 - core) * count_z, count_z)
    wide = rows.shape[3]
    lane = lax.broadcasted_iota(jnp.int32, (count_z, wide), 1) % count_y

    def fill_rows(link, start):
        at = pl.ds(start, count_z)
        link_y = [0.5 * link(1, e).astype(F32) for e in range(18)]
        for ra, line in enumerate(link_rows(link_y, False, wide)):
            rows[0, ra, at, :] = jnp.where(
                lane == 0, pltpu.roll(line, wide - (count_y - 1), 1), pltpu.roll(line, 1, 1)
            )
        for ra, line in enumerate(link_rows(link_y, True, wide)):
            rows[1, ra, at, :] = -line
        link_z = [0.5 * link(2, e).astype(F32) for e in range(18)]
        for ra, line in enumerate(link_rows(link_z, False, wide)):
            rows[2, ra, at, :] = line
        for ra, line in enumerate(link_rows(link_z, True, wide)):
            rows[3, ra, at, :] = -line

    padded[:, :, pl.ds(mine, count_z)] = v_ref[:, :, t]
    swapped = swap_ref.at[step_m]
    for q in range(2):
        for b in range(3):
            block = packed_plane(swapped, count_z, q, b, 0, count_z, count_y)
            padded[q, b, pl.ds(theirs, count_z)] = block.reshape(count_z, count_y, nev)
    fill_rows(lambda k, e: packed_link(swapped, count_z, k, e, count_z, count_y), theirs)
    fill_rows(lambda k, e: link_ref[k, e, t], mine)

    table = table_ref
    step = nev // count_y
    write_phased(
        lambda q, b, block: padded[q, b, block * step : (block + 1) * step].reshape(nev, nev),
        table, 0, 0, sites // nev, phased, 0, sites,
    )
    def forward(z):
        return jnp.dot(
            spread(rows, 2, z, same), padded[:, :, z + 1].reshape(lanes, nev), preferred_element_type=F32
        )

    def backward(z):
        return jnp.dot(
            spread(rows, 3, z - 1, same), padded[:, :, z - 1].reshape(lanes, nev), preferred_element_type=F32
        )

    for z in range(deep):
        in_y = spread(rows, 0, z, above) + spread(rows, 1, z, below)
        terms = jnp.dot(in_y, padded[:, :, z].reshape(lanes, nev), preferred_element_type=F32)
        put_displaced(moved_y, z, terms, count_y, nev)
        terms = forward(z) if z + 1 < deep else 0.0
        if z > 0:
            terms += backward(z)
        put_displaced(moved_z, z, terms, count_y, nev)
    for at, moved in enumerate((moved_y, moved_z)):
        products = jnp.dot(phased[...], moved[...].reshape(3 * sites, 2 * nev), preferred_element_type=F32)
        out_ref[:, 0, :, at * nev : (at + 1) * nev] = partial_rows(combine(products, nev)).astype(BF16)
    top_ref[0] = padded[:, :, deep - 1].reshape(lanes, nev)
    for kind in range(2):
        for ra in range(6):
            line_ref[0, kind * 8 + ra : kind * 8 + ra + 1] = rows[2 + kind, ra, deep - 1 : deep]


def from_rows(ref, depth, count_y, first=0):
    return lambda q, b, z, count: packed_plane(ref, depth, q, b, first + z, count, count_y)


def from_times(ref, t):
    count_y, nev = ref.shape[4:]
    return lambda q, b, z, count: ref[q, b, t, z : z + count].reshape(count * count_y, nev)


def x_terms(odd, at, own, received, own_link, received_link, link_first, table, table_first, rows, phased, moved):
    lanes = rows.shape[3]
    count_z, count_y = moved.shape[2:4]
    nev = moved.shape[4] // 2
    below = odd if at else 1 - odd
    same = site_masks(count_y, lanes)[0]
    entries = [0.5 * jnp.where(below == 1, own_link(e), received_link(e)).astype(F32) for e in range(18)]
    for ra, line in enumerate(link_rows(entries, False, lanes)):
        rows[below, ra] = line
    for ra, line in enumerate(link_rows(entries, True, lanes)):
        rows[1 - below, ra] = -line
    sites = count_z * count_y
    step = nev // count_y
    for vectors, x_at, first in ((own, 0, 0), (received, 2 - below, 3 * sites)):
        write_phased(
            lambda q, b, block: vectors(q, b, block * step, step),
            table, x_at, table_first, sites // nev, phased, first, sites,
        )

    def plane(vectors, z):
        return jnp.concatenate([vectors(q, b, z, 1) for q in range(2) for b in range(3)], axis=0)

    for z in range(count_z):
        line = link_first + z
        terms = jnp.dot(spread(rows, 1, line, same), plane(received, z), preferred_element_type=F32)
        put_displaced(moved.at[0], z, terms, count_y, nev)
        terms = jnp.dot(spread(rows, 0, line, same), plane(own, z), preferred_element_type=F32)
        put_displaced(moved.at[1], z, terms, count_y, nev)
    products = jnp.dot(phased[...], moved[...].reshape(6 * sites, 2 * nev), preferred_element_type=F32)
    return combine(products, nev)


def x_first_kernel(place_ref, v_ref, link_ref, first_ref, second_ref, table, out_ref, rows, phased, moved):
    count_z, count_y = link_ref.shape[3:]
    core, odd = place_ref[0], place_ref[3]
    at_table = pl.multiple_of(core * (count_z * count_y), count_z * count_y)
    for at, got in enumerate((first_ref.at[0], second_ref.at[0])):
        m = 1 - odd if at else odd
        t = core + 2 * m
        parts = x_terms(
            odd, at, from_times(v_ref, t), from_rows(got, count_z, count_y),
            lambda e, t=t: link_ref[0, e, t], lambda e, got=got: packed_link(got, count_z, 0, e, count_z, count_y),
            0, table, at_table, rows, phased, moved,
        )
        for i, part in enumerate(parts):
            out_ref[m, i] = part


def x_part(first, at, place_ref, swap_ref, got, received_link, table, rows, phased, moved):
    held_z = rows.shape[2]
    depth, count_y = moved.shape[2:4]
    odd = place_ref[3]
    at_table = pl.multiple_of((1 - place_ref[0]) * (held_z * count_y) + first * count_y, moved.shape[4] // 2)
    own = swap_ref.at[1 - odd if at else odd]
    return x_terms(
        odd, at, from_rows(own, held_z, count_y, first), from_rows(got, depth, count_y),
        lambda e: packed_link(own, held_z, 0, e, held_z, count_y), received_link,
        first, table, at_table, rows, phased, moved,
    )


def x_middle_kernel(place_ref, swap_ref, first_ref, second_ref, table, before, out_ref, links_ref, *scratch):
    held_z = scratch[0].shape[2]
    depth, count_y = scratch[2].shape[2:4]
    odd = place_ref[3]
    for at, got in enumerate((first_ref.at[0], second_ref.at[0])):
        m = 1 - odd if at else odd
        links_ref[at] = got[got.shape[0] - links_ref.shape[1] :]
        parts = x_part(
            0, at, place_ref, swap_ref, got,
            lambda e, got=got: packed_link(got, depth, 0, e, held_z, count_y), table, *scratch,
        )
        for i, part in enumerate(parts):
            out_ref[m, i] = part + before[m, i]


def boundary(top, halo, lines, table, edge):
    lanes, nev = top.shape
    count_y = lanes // 6
    wide = lanes // 2
    same = site_masks(count_y, lanes)[0]

    def matrix(kind):
        blocks = []
        for ra in range(6):
            line = lines[kind * 8 + ra : kind * 8 + ra + 1, :lanes]
            blocks.append(jnp.broadcast_to(line, (count_y, lanes)).astype(BF16) * same)
        return jnp.concatenate(blocks, axis=0)

    products = 0.0
    for at, (phased, moved, kind) in enumerate(((top, halo, 0), (halo, top, 1))):
        put_phased(
            phased[:wide].T.astype(F32), phased[wide:].T.astype(F32), table, 0,
            table.shape[2] - (at + 1) * nev, edge, at * nev,
        )
        terms = jnp.dot(matrix(kind), moved[...], preferred_element_type=F32).astype(BF16)
        displaced = jnp.concatenate([terms[:wide], terms[wide:]], axis=1)
        products += jnp.dot(edge[:, at * nev : at * nev + wide], displaced, preferred_element_type=F32)
    return combine(products, nev)


def x_last_kernel(place_ref, swap_ref, first_ref, second_ref, link_rows_ref, table, before, sent_ref,
                  top_ref, halo_ref, line_ref, out_ref, rows, phased, moved, edge):
    nev = before.shape[3]
    held_z = rows.shape[2]
    depth, count_y = moved.shape[2:4]
    odd = place_ref[3]
    out_ref[:, :, :, :nev] = sent_ref[:, :, :, :nev]
    for m in range(2):
        above = partial_rows(boundary(top_ref.at[m], halo_ref.at[m], line_ref.at[m], table, edge))
        out_ref[:, m, :, nev : 2 * nev] = (sent_ref[:, m, :, nev:].astype(F32) + above).astype(BF16)
    for at, got in enumerate((first_ref.at[0], second_ref.at[0])):
        m = 1 - odd if at else odd
        parts = x_part(
            held_z - depth, at, place_ref, swap_ref, got,
            lambda e, at=at: packed_link(link_rows_ref.at[at], 0, 0, e, held_z, count_y), table,
            rows, phased, moved,
        )
        parts = [part + before[m, i] for i, part in enumerate(parts)]
        out_ref[:, m, :, 2 * nev :] = partial_rows(parts).astype(BF16)


def total_kernel(directions_ref, got_ref, out_ref, total_ref):
    step = pl.program_id(0)
    part = jnp.sum(got_ref[...].astype(F32), axis=0)

    @pl.when(step == 0)
    def _():
        total_ref[...] = part

    @pl.when(step > 0)
    def _():
        total_ref[...] += part

    @pl.when(step == pl.num_programs(0) - 1)
    def _():
        total = total_ref[...]
        nev = total.shape[1] // 3
        group = out_ref.shape[0]
        in_y, in_z, in_x = (total[:, k * nev : (k + 1) * nev] for k in range(3))
        for d in range(3):
            direction = directions_ref[d]
            chosen = jnp.where(direction == 0, in_x, jnp.where(direction == 1, in_y, in_z))
            for r in range(2):
                for p in range(2):
                    for i in range(group):
                        row = (r * 2 + p) * group + i
                        out_ref[i, 0, p, r : r + 1, d * nev : (d + 1) * nev] = chosen[row : row + 1]


def exchange(first, second):
    count = lax.axis_size("ts")
    got = [None, None]
    for at, array in ((1, second), (0, first)):
        pairs = [(i, (i + 1 if (i + at) % 2 == 0 else i - 1) % count) for i in range(count)]
        got[at] = lax.ppermute(array.reshape(1, -1, array.shape[-1]), "ts", pairs)
    return got


def shards(eigvecs, gauge_links, momenta, directions):
    _, _, count_t, _, count_z, count_y, nev = eigvecs.shape
    vectors = eigvecs.reshape(2, 3, count_t, count_z, count_y, nev)
    links = gauge_links.reshape(3, 18, count_t, count_z, count_y)
    size_x, size_g = lax.axis_size("ts"), lax.axis_size("gz")
    x, g = lax.axis_index("ts"), lax.axis_index("gz")
    core, chip = g % 2, g // 2
    deep = 2 * count_z
    sites = count_z * count_y
    group = nev // size_x

    small = pl.CostEstimate(flops=1_000_000, bytes_accessed=100_000, transcendentals=0)
    limit = pltpu.CompilerParams(vmem_limit_bytes=28 * 1024 * 1024)
    in_vmem = pl.BlockSpec(memory_space=pltpu.VMEM)
    in_smem = pl.BlockSpec(memory_space=pltpu.SMEM)
    planes = link_planes(nev, count_z, count_y)

    place = jnp.stack([core, x, chip * deep, x % 2]).astype(jnp.int32)

    def planes_of(times, depth, directions):
        return jax.ShapeDtypeStruct((times, 6 * depth + directions * planes, count_y, nev), BF16)

    def call(kernel, name, out_shape, scratch_shapes, *operands):
        in_specs = [in_smem] + [in_vmem] * (len(operands) - 1)
        return pl.pallas_call(
            kernel,
            in_specs=in_specs,
            out_specs=jax.tree.map(lambda _: in_vmem, out_shape),
            out_shape=out_shape,
            scratch_shapes=scratch_shapes,
            compiler_params=limit,
            cost_estimate=small,
            name=name,
        )(*operands)

    *mine, given = call(
        pack_kernel, "pack", [planes_of(1, count_z, 1)] * 2 + [planes_of(2, count_z, 3)], [],
        place, vectors, links,
    )
    got_first = exchange(*mine)
    swapped = lax.ppermute(given, "gz", [(0, 1), (1, 0), (2, 3), (3, 2)])
    tail = nev // count_y
    lead = count_z - tail
    table = pl.pallas_call(
        functools.partial(table_kernel, (size_x, count_z * size_g, count_y), deep),
        in_specs=[in_smem, in_smem],
        out_specs=in_vmem,
        out_shape=jax.ShapeDtypeStruct((8, 2, 2 * sites + 2 * nev), F32),
        compiler_params=limit,
        cost_estimate=pl.CostEstimate(flops=10_000_000_000, bytes_accessed=100_000, transcendentals=0),
        name="phase_table",
    )(place, momenta)
    after, _ = lax.optimization_barrier((place, table))
    shapes = [planes_of(1, lead, 1)] * 2 + [jax.ShapeDtypeStruct((2, 6, count_y, nev), BF16)]
    *mine, lowest = call(
        functools.partial(split_first_kernel, count_z), "split_first", shapes, [], after, swapped, vectors
    )
    got_second = exchange(*mine)
    halo = lax.ppermute(lowest.reshape(2, 6 * count_y, nev), "gz", [(0, 2), (2, 0), (1, 3), (3, 1)])

    after, _ = lax.optimization_barrier((place, lowest))
    swapped_rows = swapped.reshape(2, -1, nev)
    sent, top, lines = pl.pallas_call(
        yz_kernel,
        grid=(2,),
        in_specs=[in_smem] + [in_vmem] * 4,
        out_specs=[
            pl.BlockSpec((size_x, 1, 4 * group, 2 * nev), lambda m: (0, m, 0, 0)),
            pl.BlockSpec((1, 6 * count_y, nev), lambda m: (m, 0, 0)),
            pl.BlockSpec((1, 16, 2 * nev), lambda m: (m, 0, 0)),
        ],
        out_shape=[
            jax.ShapeDtypeStruct((size_x, 2, 4 * group, 2 * nev), BF16),
            jax.ShapeDtypeStruct((2, 6 * count_y, nev), BF16),
            jax.ShapeDtypeStruct((2, 16, 2 * nev), F32),
        ],
        scratch_shapes=[
            pltpu.VMEM((4, 6, deep, 2 * nev), F32),
            pltpu.VMEM((2, 3, deep, count_y, nev), BF16),
            pltpu.VMEM((4 * nev, 6 * sites), BF16),
            pltpu.VMEM((3, deep, count_y, 2 * nev), BF16),
            pltpu.VMEM((3, deep, count_y, 2 * nev), BF16),
        ],
        compiler_params=limit,
        cost_estimate=small,
        name="yz_terms",
    )(after, vectors, swapped_rows, links, table)

    after, _, got_first[1] = lax.optimization_barrier((place, sent, got_first[1]))
    mine = call(
        functools.partial(split_last_kernel, count_z), "split_last", [planes_of(1, tail, 0)] * 2, [], after, swapped
    )
    got_last = exchange(*mine)

    def scratch(depth):
        return [
            pltpu.VMEM((2, 6, count_z, 6 * count_y), F32),
            pltpu.VMEM((4 * nev, 6 * depth * count_y), BF16),
            pltpu.VMEM((2, 3, depth, count_y, 2 * nev), BF16),
        ]

    parts = jax.ShapeDtypeStruct((2, 4, nev, nev), F32)
    (part,) = call(
        x_first_kernel, "x_first", [parts], scratch(count_z), after, vectors, links, *got_first, table
    )
    part, links_down = call(
        x_middle_kernel, "x_middle", [parts, jax.ShapeDtypeStruct((2, planes * count_y, nev), BF16)],
        scratch(lead), after, swapped_rows, *got_second, table, part,
    )
    (sent,) = call(
        x_last_kernel, "x_last", [jax.ShapeDtypeStruct((size_x, 2, 4 * group, 3 * nev), BF16)],
        scratch(tail) + [pltpu.VMEM((4 * nev, 2 * nev), BF16)],
        after, swapped_rows, *got_last, links_down, table, part, sent, top, halo, lines,
    )

    pieces = sent.reshape(2 * size_x, 4 * group, 3 * nev)
    groups = [[(ts * 2 + h) * 2 + c for ts in range(size_x) for h in range(2)] for c in range(2)]
    got = lax.all_to_all(pieces, ("ts", "gz"), 0, 0, tiled=True, axis_index_groups=groups)
    out_shape = (group, 1, 2, 2, 3 * nev)
    return pl.pallas_call(
        total_kernel,
        grid=(4,),
        in_specs=[in_smem, pl.BlockSpec((size_x // 2, 4 * group, 3 * nev), lambda i: (i, 0, 0))],
        out_specs=pl.BlockSpec(out_shape, lambda i: (0, 0, 0, 0, 0)),
        out_shape=jax.ShapeDtypeStruct(out_shape, F32),
        scratch_shapes=[pltpu.VMEM((4 * group, 3 * nev), F32)],
        compiler_params=limit,
        name="total",
    )(directions, got)


def solution(mesh):
    in_specs = (
        P(None, None, None, "ts", "gz", None, None),
        P(None, None, None, "ts", "gz", None),
        P(),
        P(),
    )
    out_specs = P("ts", "gz", None, None, None)
    return jax.shard_map(shards, mesh=mesh, in_specs=in_specs, out_specs=out_specs, check_vma=False)
```

```python
import functools
import math

import jax
import jax.numpy as jnp
from jax import lax
from jax.experimental import pallas as pl
from jax.experimental.pallas import tpu as pltpu
from jax.sharding import PartitionSpec as P

BF16 = jnp.bfloat16
F32 = jnp.float32


def link_rows(entries, adjoint, width):
    rows = []
    for r in range(2):
        for a in range(3):
            pieces = []
            for q in range(2):
                for b in range(3):
                    first = ((b * 3 + a) if adjoint else (a * 3 + b)) * 2
                    if r == q:
                        pieces.append(entries[first])
                    elif (q == 1) == adjoint:
                        pieces.append(entries[first + 1])
                    else:
                        pieces.append(-entries[first + 1])
            lanes = sum(piece.shape[1] for piece in pieces)
            if lanes < width:
                pieces.append(jnp.zeros((pieces[0].shape[0], width - lanes), F32))
            rows.append(jnp.concatenate(pieces, axis=1))
    return rows


def site_masks(count_y, lanes):
    row = lax.broadcasted_iota(jnp.int32, (count_y, lanes), 0)
    lane = lax.broadcasted_iota(jnp.int32, (count_y, lanes), 1) % count_y
    same = jnp.where(lane == row, 1.0, 0.0).astype(BF16)
    above = jnp.where(lane == (row + 1) % count_y, 1.0, 0.0).astype(BF16)
    below = jnp.where(lane == (row + count_y - 1) % count_y, 1.0, 0.0).astype(BF16)
    return same, above, below


def spread(rows_ref, kind, row, mask):
    count_y, lanes = mask.shape
    blocks = []
    for ra in range(6):
        line = rows_ref[kind, ra, pl.ds(row, 1), :lanes]
        blocks.append(jnp.broadcast_to(line, (count_y, lanes)).astype(BF16) * mask)
    return jnp.concatenate(blocks, axis=0)


def fraction(component, coords, length):
    return jnp.mod(component * coords, length).astype(F32) / length


def table_kernel(lengths, deep, place_ref, momenta_ref, table_ref):
    length_x, length_z, length_y = lengths
    half = table_ref.shape[0] // 2
    shape = 2 * half, table_ref.shape[2]
    row = lax.broadcasted_iota(jnp.int32, shape, 0)
    lane = lax.broadcasted_iota(jnp.int32, shape, 1)
    x_at = row // 2
    x = place_ref[1] + jnp.where(x_at == 2, -1, x_at)
    plane = lane // length_y
    above = deep + (shape[1] // length_y - deep) // 2
    z = place_ref[2] + jnp.where(plane < deep, plane, jnp.where(plane < above, deep, deep - 1))
    y = lane % length_y
    first = row % 2 == 0
    m_x, m_y, m_z = (jnp.where(first, momenta_ref[0, i], momenta_ref[1, i]) for i in range(3))
    angle = 2.0 * math.pi * (
        (fraction(m_x, x, length_x) + fraction(m_y, y, length_y)) + fraction(m_z, z, length_z)
    )
    for first, values in ((0, jnp.cos(angle)), (half, jnp.sin(angle))):
        for at in range(2 * half):
            table_ref[first + at // 2, at % 2 : at % 2 + 1] = values[at : at + 1]


def write_phased(planes_of, table, x_at, table_first, blocks, out_ref, first, colour_stride):
    for b in range(3):
        for block in range(blocks):
            real = planes_of(0, b, block).T.astype(F32)
            imag = planes_of(1, b, block).T.astype(F32)
            nev, sites = real.shape
            at = first + b * colour_stride + block * sites
            put_phased(real, imag, table, x_at, table_first + block * sites, out_ref, at)


def put_phased(real, imag, table, x_at, table_at, out_ref, at):
    nev, sites = real.shape
    for p in range(2):
        cosine, sine = (table[half + x_at, p : p + 1, pl.ds(table_at, sites)] for half in (0, table.shape[0] // 2))
        out_ref[2 * p * nev : (2 * p + 1) * nev, at : at + sites] = (cosine * real - sine * imag).astype(BF16)
        out_ref[(2 * p + 1) * nev : (2 * p + 2) * nev, at : at + sites] = (sine * real + cosine * imag).astype(BF16)


def put_displaced(out_ref, z, terms, count_y, nev):
    for r in range(2):
        for a in range(3):
            rows = terms[(r * 3 + a) * count_y : (r * 3 + a + 1) * count_y]
            out_ref[a, z, :, r * nev : (r + 1) * nev] = rows.astype(BF16)


def combine(products, nev):
    real, imag = [], []
    for p in range(2):
        rr = products[2 * p * nev : (2 * p + 1) * nev, :nev]
        ri = products[2 * p * nev : (2 * p + 1) * nev, nev:]
        ir = products[(2 * p + 1) * nev : (2 * p + 2) * nev, :nev]
        ii = products[(2 * p + 1) * nev : (2 * p + 2) * nev, nev:]
        real.append(rr + ii)
        imag.append(ri - ir)
    return real + imag


def by_owner(first, second):
    nev, lanes = first.shape
    a = first.reshape(nev // 8, 8, lanes)
    b = second.reshape(nev // 8, 8, lanes)
    upper = lax.broadcasted_iota(jnp.int32, a.shape, 1) < 4
    even = jnp.where(upper, a, pltpu.roll(b, 4, 1))
    odd = jnp.where(upper, pltpu.roll(a, 4, 1), b)
    return jnp.stack([even, odd], axis=1).reshape(nev // 4, 8, lanes)


def partial_rows(parts):
    return jnp.concatenate([by_owner(parts[0], parts[1]), by_owner(parts[2], parts[3])], axis=1)


def packed_plane(packed, depth, q, b, z, count, count_y):
    first = ((q * 3 + b) * depth + z) * count_y
    return packed[first : first + count * count_y]


def link_planes(nev, count_z, count_y):
    return -(-18 * count_y * count_z // (nev * count_y))


def packed_link(packed, depth, k, e, count_z, count_y):
    nev = packed.shape[1]
    per_row = nev // count_y
    first = (6 * depth + k * link_planes(nev, count_z, count_y)) * count_y + e // per_row * count_z
    lane = e % per_row * count_y
    return packed[first : first + count_z, lane : lane + count_y]


def put_links(out_ref, at, first_plane, link, count_z, count_y, nev):
    per_row = nev // count_y
    per_plane = count_y // count_z
    for row in range(link_planes(nev, count_z, count_y) * per_plane):
        held = [link(e) for e in range(row * per_row, min(18, (row + 1) * per_row))]
        held += [jnp.zeros((count_z, count_y), BF16)] * (per_row - len(held))
        first = row % per_plane * count_z
        out_ref[at, first_plane + row // per_plane, first : first + count_z] = jnp.concatenate(held, axis=1)


def pack_own_kernel(place_ref, v_ref, link_ref, first_ref, second_ref):
    count_z, count_y, nev = v_ref.shape[3:]
    core, odd = place_ref[0], place_ref[3]
    for out_ref, t in ((first_ref, core + 2 * (1 - odd)), (second_ref, core + 2 * odd)):
        for held in range(6):
            out_ref[0, held * count_z : (held + 1) * count_z] = v_ref[held // 3, held % 3, t]
        put_links(out_ref, 0, 6 * count_z, lambda e, t=t: link_ref[0, e, t], count_z, count_y, nev)


def pack_given_kernel(place_ref, v_ref, given_ref):
    count_z = v_ref.shape[3]
    for m in range(2):
        for held in range(6):
            given_ref[m, held * count_z : (held + 1) * count_z] = v_ref[held // 3, held % 3, 1 - place_ref[0] + 2 * m]


def split(place_ref, swap_ref, start, count_z, out_refs):
    odd = place_ref[3]
    depth = out_refs[0].shape[1] // 6
    for i, out_ref in enumerate(out_refs):
        for held in range(6):
            first = held * count_z + start
            out_ref[0, held * depth : (held + 1) * depth] = swap_ref[odd if i else 1 - odd, first : first + depth]


def split_first_kernel(count_z, place_ref, swap_ref, link_ref, v_ref, first_ref, second_ref, lowest_ref):
    count_y, nev = v_ref.shape[4:]
    split(place_ref, swap_ref, 0, count_z, (first_ref, second_ref))
    core, odd = place_ref[0], place_ref[3]
    for out_ref, t in ((first_ref, core + 2 * (1 - odd)), (second_ref, core + 2 * odd)):
        depth = out_ref.shape[1] // 6
        put_links(out_ref, 0, 6 * depth, lambda e, t=t: link_ref[0, e, t], count_z, count_y, nev)
    for m in range(2):
        for i in range(6):
            own = v_ref[i // 3, i % 3, core + 2 * m, 0]
            lowest_ref[m, i] = jnp.where(core == 0, own, swap_ref[m, i * count_z])


def split_last_kernel(count_z, place_ref, swap_ref, first_ref, second_ref):
    split(place_ref, swap_ref, count_z - first_ref.shape[1] // 6, count_z, (first_ref, second_ref))


def yz_kernel(place_ref, v_ref, swap_ref, link_ref, other_link_ref, table_ref, out_ref, top_ref, line_ref,
              rows, padded, phased, moved_y, moved_z):
    core = place_ref[0]
    step_m = pl.program_id(0)
    t = core + 2 * step_m
    count_z, count_y, nev = v_ref.shape[3:]
    deep = 2 * count_z
    lanes = 6 * count_y
    sites = deep * count_y
    same, above, below = site_masks(count_y, lanes)
    mine = pl.multiple_of(core * count_z, count_z)
    theirs = pl.multiple_of((1 - core) * count_z, count_z)
    wide = rows.shape[3]
    lane = lax.broadcasted_iota(jnp.int32, (count_z, wide), 1) % count_y

    def fill_rows(link, start):
        at = pl.ds(start, count_z)
        link_y = [0.5 * link(1, e).astype(F32) for e in range(18)]
        for ra, line in enumerate(link_rows(link_y, False, wide)):
            rows[0, ra, at, :] = jnp.where(
                lane == 0, pltpu.roll(line, wide - (count_y - 1), 1), pltpu.roll(line, 1, 1)
            )
        for ra, line in enumerate(link_rows(link_y, True, wide)):
            rows[1, ra, at, :] = -line
        link_z = [0.5 * link(2, e).astype(F32) for e in range(18)]
        for ra, line in enumerate(link_rows(link_z, False, wide)):
            rows[2, ra, at, :] = line
        for ra, line in enumerate(link_rows(link_z, True, wide)):
            rows[3, ra, at, :] = -line

    padded[:, :, pl.ds(mine, count_z)] = v_ref[:, :, t]
    swapped = swap_ref.at[step_m]
    for q in range(2):
        for b in range(3):
            block = packed_plane(swapped, count_z, q, b, 0, count_z, count_y)
            padded[q, b, pl.ds(theirs, count_z)] = block.reshape(count_z, count_y, nev)
    fill_rows(lambda k, e: other_link_ref[k, e, t], theirs)
    fill_rows(lambda k, e: link_ref[k, e, t], mine)

    table = table_ref
    step = nev // count_y
    write_phased(
        lambda q, b, block: padded[q, b, block * step : (block + 1) * step].reshape(nev, nev),
        table, 0, 0, sites // nev, phased, 0, sites,
    )
    def forward(z):
        return jnp.dot(
            spread(rows, 2, z, same), padded[:, :, z + 1].reshape(lanes, nev), preferred_element_type=F32
        )

    def backward(z):
        return jnp.dot(
            spread(rows, 3, z - 1, same), padded[:, :, z - 1].reshape(lanes, nev), preferred_element_type=F32
        )

    for z in range(deep):
        in_y = spread(rows, 0, z, above) + spread(rows, 1, z, below)
        terms = jnp.dot(in_y, padded[:, :, z].reshape(lanes, nev), preferred_element_type=F32)
        put_displaced(moved_y, z, terms, count_y, nev)
        terms = forward(z) if z + 1 < deep else 0.0
        if z > 0:
            terms += backward(z)
        put_displaced(moved_z, z, terms, count_y, nev)
    for at, moved in enumerate((moved_y, moved_z)):
        products = jnp.dot(phased[...], moved[...].reshape(3 * sites, 2 * nev), preferred_element_type=F32)
        out_ref[:, 0, :, at * nev : (at + 1) * nev] = partial_rows(combine(products, nev)).astype(BF16)
    top_ref[0] = padded[:, :, deep - 1].reshape(lanes, nev)
    for kind in range(2):
        for ra in range(6):
            line_ref[0, kind * 8 + ra : kind * 8 + ra + 1] = rows[2 + kind, ra, deep - 1 : deep]


def from_rows(ref, depth, count_y, first=0):
    return lambda q, b, z, count: packed_plane(ref, depth, q, b, first + z, count, count_y)


def from_times(ref, t):
    count_y, nev = ref.shape[4:]
    return lambda q, b, z, count: ref[q, b, t, z : z + count].reshape(count * count_y, nev)


def x_terms(odd, at, own, received, own_link, received_link, link_first, table, table_first, rows, phased, moved):
    lanes = rows.shape[3]
    count_z, count_y = moved.shape[2:4]
    nev = moved.shape[4] // 2
    below = odd if at else 1 - odd
    same = site_masks(count_y, lanes)[0]
    entries = [0.5 * jnp.where(below == 1, own_link(e), received_link(e)).astype(F32) for e in range(18)]
    for ra, line in enumerate(link_rows(entries, False, lanes)):
        rows[below, ra] = line
    for ra, line in enumerate(link_rows(entries, True, lanes)):
        rows[1 - below, ra] = -line
    sites = count_z * count_y
    step = nev // count_y
    for vectors, x_at, first in ((own, 0, 0), (received, 2 - below, 3 * sites)):
        write_phased(
            lambda q, b, block: vectors(q, b, block * step, step),
            table, x_at, table_first, sites // nev, phased, first, sites,
        )

    def plane(vectors, z):
        return jnp.concatenate([vectors(q, b, z, 1) for q in range(2) for b in range(3)], axis=0)

    for z in range(count_z):
        line = link_first + z
        terms = jnp.dot(spread(rows, 1, line, same), plane(received, z), preferred_element_type=F32)
        put_displaced(moved.at[0], z, terms, count_y, nev)
        terms = jnp.dot(spread(rows, 0, line, same), plane(own, z), preferred_element_type=F32)
        put_displaced(moved.at[1], z, terms, count_y, nev)
    products = jnp.dot(phased[...], moved[...].reshape(6 * sites, 2 * nev), preferred_element_type=F32)
    return combine(products, nev)


def x_first_kernel(place_ref, v_ref, link_ref, first_ref, second_ref, table, out_ref, rows, phased, moved):
    count_z, count_y = link_ref.shape[3:]
    core, odd = place_ref[0], place_ref[3]
    at_table = pl.multiple_of(core * (count_z * count_y), count_z * count_y)
    for at, got in enumerate((first_ref.at[0], second_ref.at[0])):
        m = 1 - odd if at else odd
        t = core + 2 * m
        parts = x_terms(
            odd, at, from_times(v_ref, t), from_rows(got, count_z, count_y),
            lambda e, t=t: link_ref[0, e, t], lambda e, got=got: packed_link(got, count_z, 0, e, count_z, count_y),
            0, table, at_table, rows, phased, moved,
        )
        for i, part in enumerate(parts):
            out_ref[m, i] = part


def x_part(first, at, place_ref, swap_ref, link_ref, got, received_link, table, rows, phased, moved):
    held_z = rows.shape[2]
    depth, count_y = moved.shape[2:4]
    core, odd = place_ref[0], place_ref[3]
    m = 1 - odd if at else odd
    at_table = pl.multiple_of((1 - core) * (held_z * count_y) + first * count_y, moved.shape[4] // 2)
    return x_terms(
        odd, at, from_rows(swap_ref.at[m], held_z, count_y, first), from_rows(got, depth, count_y),
        lambda e: link_ref[0, e, core + 2 * m], received_link,
        first, table, at_table, rows, phased, moved,
    )


def boundary(top, halo, lines, table, edge):
    lanes, nev = top.shape
    count_y = lanes // 6
    wide = lanes // 2
    same = site_masks(count_y, lanes)[0]

    def matrix(kind):
        blocks = []
        for ra in range(6):
            line = lines[kind * 8 + ra : kind * 8 + ra + 1, :lanes]
            blocks.append(jnp.broadcast_to(line, (count_y, lanes)).astype(BF16) * same)
        return jnp.concatenate(blocks, axis=0)

    products = 0.0
    for at, (phased, moved, kind) in enumerate(((top, halo, 0), (halo, top, 1))):
        put_phased(
            phased[:wide].T.astype(F32), phased[wide:].T.astype(F32), table, 0,
            table.shape[2] - (at + 1) * nev, edge, at * nev,
        )
        terms = jnp.dot(matrix(kind), moved[...], preferred_element_type=F32).astype(BF16)
        displaced = jnp.concatenate([terms[:wide], terms[wide:]], axis=1)
        products += jnp.dot(edge[:, at * nev : at * nev + wide], displaced, preferred_element_type=F32)
    return combine(products, nev)


def x_middle(at, place_ref, swap_ref, link_ref, got_ref, table, before, out_ref, links_ref, *scratch):
    held_z = scratch[0].shape[2]
    depth, count_y = scratch[2].shape[2:4]
    odd = place_ref[3]
    got = got_ref.at[0]
    links_ref[...] = got[got.shape[0] - links_ref.shape[0] :]
    parts = x_part(
        0, at, place_ref, swap_ref, link_ref, got,
        lambda e: packed_link(got, depth, 0, e, held_z, count_y), table, *scratch,
    )
    for i, part in enumerate(parts):
        out_ref[i] = part + before[1 - odd if at else odd, i]


def x_last(at, place_ref, swap_ref, link_ref, got_ref, links_ref, table, before, pieces_ref, rows, phased, moved):
    nev = before.shape[2]
    held_z = rows.shape[2]
    depth, count_y = moved.shape[2:4]
    odd = place_ref[3]
    parts = x_part(
        held_z - depth, at, place_ref, swap_ref, link_ref, got_ref.at[0],
        lambda e: packed_link(links_ref, 0, 0, e, held_z, count_y), table, rows, phased, moved,
    )
    parts = [part + before[i] for i, part in enumerate(parts)]
    pieces_ref[:, 1 - odd if at else odd, :, 2 * nev :] = partial_rows(parts).astype(BF16)


def x_last_first(place_ref, swap_ref, link_ref, got_ref, links_ref, table, before, sent_ref, pieces_ref, *scratch):
    pieces_ref[:, :, :, : sent_ref.shape[3]] = sent_ref[...]
    x_last(0, place_ref, swap_ref, link_ref, got_ref, links_ref, table, before, pieces_ref, *scratch)


def x_last_second(place_ref, swap_ref, link_ref, got_ref, links_ref, table, before, top_ref, halo_ref, line_ref, sent_ref,
                  pieces_ref, rows, phased, moved, edge):
    nev = before.shape[2]
    for m in range(2):
        above = partial_rows(boundary(top_ref.at[m], halo_ref.at[m], line_ref.at[m], table, edge))
        pieces_ref[:, m, :, nev : 2 * nev] = (sent_ref[:, m, :, nev : 2 * nev].astype(F32) + above).astype(BF16)
    x_last(1, place_ref, swap_ref, link_ref, got_ref, links_ref, table, before, pieces_ref, rows, phased, moved)


def total_kernel(directions_ref, got_ref, out_ref, total_ref):
    step = pl.program_id(0)
    part = jnp.sum(got_ref[...].astype(F32), axis=0)

    @pl.when(step == 0)
    def _():
        total_ref[...] = part

    @pl.when(step > 0)
    def _():
        total_ref[...] += part

    @pl.when(step == pl.num_programs(0) - 1)
    def _():
        total = total_ref[...]
        nev = total.shape[1] // 3
        group = out_ref.shape[0]
        in_y, in_z, in_x = (total[:, k * nev : (k + 1) * nev] for k in range(3))
        for d in range(3):
            direction = directions_ref[d]
            chosen = jnp.where(direction == 0, in_x, jnp.where(direction == 1, in_y, in_z))
            for r in range(2):
                for p in range(2):
                    for i in range(group):
                        row = (r * 2 + p) * group + i
                        out_ref[i, 0, p, r : r + 1, d * nev : (d + 1) * nev] = chosen[row : row + 1]


def exchange(first, second):
    count = lax.axis_size("ts")
    got = [None, None]
    for at, array in ((0, first), (1, second)):
        pairs = [(i, (i + 1 if (i + at) % 2 == 0 else i - 1) % count) for i in range(count)]
        got[at] = lax.ppermute(array.reshape(1, -1, array.shape[-1]), "ts", pairs)
    return got


def shards(eigvecs, gauge_links, momenta, directions):
    _, _, count_t, _, count_z, count_y, nev = eigvecs.shape
    vectors = eigvecs.reshape(2, 3, count_t, count_z, count_y, nev)
    links = gauge_links.reshape(3, 18, count_t, count_z, count_y)
    size_x, size_g = lax.axis_size("ts"), lax.axis_size("gz")
    x, g = lax.axis_index("ts"), lax.axis_index("gz")
    core, chip = g % 2, g // 2
    deep = 2 * count_z
    sites = count_z * count_y
    group = nev // size_x

    small = pl.CostEstimate(flops=1_000_000, bytes_accessed=100_000, transcendentals=0)
    limit = pltpu.CompilerParams(vmem_limit_bytes=20 * 1024 * 1024)
    in_vmem = pl.BlockSpec(memory_space=pltpu.VMEM)
    in_smem = pl.BlockSpec(memory_space=pltpu.SMEM)
    planes = link_planes(nev, count_z, count_y)

    place = jnp.stack([core, x, chip * deep, x % 2]).astype(jnp.int32)

    def planes_of(times, depth, directions):
        return jax.ShapeDtypeStruct((times, 6 * depth + directions * planes, count_y, nev), BF16)

    def call(kernel, name, out_shape, scratch_shapes, *operands, aliases={}):
        in_specs = [in_smem] + [in_vmem] * (len(operands) - 1)
        return pl.pallas_call(
            kernel,
            in_specs=in_specs,
            out_specs=jax.tree.map(lambda _: in_vmem, out_shape),
            out_shape=out_shape,
            scratch_shapes=scratch_shapes,
            input_output_aliases=aliases,
            compiler_params=limit,
            cost_estimate=small,
            name=name,
        )(*operands)

    swap = [(0, 1), (1, 0), (2, 3), (3, 2)]
    other_links = lax.ppermute(gauge_links, "gz", swap).reshape(links.shape)
    mine = call(pack_own_kernel, "pack_own", [planes_of(1, count_z, 1)] * 2, [], place, vectors, links)
    got_first = exchange(*mine)
    after, other_links, _ = lax.optimization_barrier((place, other_links, mine[0]))
    (given,) = call(pack_given_kernel, "pack_given", [planes_of(2, count_z, 0)], [], after, vectors)
    swapped = lax.ppermute(given, "gz", swap)
    tail = nev // count_y
    lead = count_z - tail
    table = pl.pallas_call(
        functools.partial(table_kernel, (size_x, count_z * size_g, count_y), deep),
        in_specs=[in_smem, in_smem],
        out_specs=in_vmem,
        out_shape=jax.ShapeDtypeStruct((8, 2, 2 * sites + 2 * nev), F32),
        compiler_params=limit,
        cost_estimate=pl.CostEstimate(flops=20_000_000_000, bytes_accessed=100_000, transcendentals=0),
        name="phase_table",
    )(place, momenta)
    after, _ = lax.optimization_barrier((place, table))
    shapes = [planes_of(1, lead, 1)] * 2 + [jax.ShapeDtypeStruct((2, 6, count_y, nev), BF16)]
    *mine, lowest = call(
        functools.partial(split_first_kernel, count_z), "split_first", shapes, [], after, swapped, other_links, vectors
    )
    got_second = exchange(*mine)
    halo = lax.ppermute(lowest.reshape(2, 6 * count_y, nev), "gz", [(0, 2), (2, 0), (1, 3), (3, 1)])

    after, _ = lax.optimization_barrier((place, lowest))
    swapped_rows = swapped.reshape(2, -1, nev)
    sent, top, lines = pl.pallas_call(
        yz_kernel,
        grid=(2,),
        in_specs=[in_smem] + [in_vmem] * 5,
        out_specs=[
            pl.BlockSpec((size_x, 1, 4 * group, 2 * nev), lambda m: (0, m, 0, 0)),
            pl.BlockSpec((1, 6 * count_y, nev), lambda m: (m, 0, 0)),
            pl.BlockSpec((1, 16, 2 * nev), lambda m: (m, 0, 0)),
        ],
        out_shape=[
            jax.ShapeDtypeStruct((size_x, 2, 4 * group, 2 * nev), BF16),
            jax.ShapeDtypeStruct((2, 6 * count_y, nev), BF16),
            jax.ShapeDtypeStruct((2, 16, 2 * nev), F32),
        ],
        scratch_shapes=[
            pltpu.VMEM((4, 6, deep, 2 * nev), F32),
            pltpu.VMEM((2, 3, deep, count_y, nev), BF16),
            pltpu.VMEM((4 * nev, 6 * sites), BF16),
            pltpu.VMEM((3, deep, count_y, 2 * nev), BF16),
            pltpu.VMEM((3, deep, count_y, 2 * nev), BF16),
        ],
        compiler_params=limit,
        cost_estimate=small,
        name="yz_terms",
    )(after, vectors, swapped_rows, links, other_links, table)

    after, _ = lax.optimization_barrier((place, sent))
    mine = call(
        functools.partial(split_last_kernel, count_z), "split_last", [planes_of(1, tail, 0)] * 2, [], after, swapped
    )
    got_last = exchange(*mine)

    def scratch(depth):
        return [
            pltpu.VMEM((2, 6, count_z, 6 * count_y), F32),
            pltpu.VMEM((4 * nev, 6 * depth * count_y), BF16),
            pltpu.VMEM((2, 3, depth, count_y, 2 * nev), BF16),
        ]

    parts = jax.ShapeDtypeStruct((2, 4, nev, nev), F32)
    (part,) = call(
        x_first_kernel, "x_first", [parts], scratch(count_z), after, vectors, links, *got_first, table
    )
    one = [jax.ShapeDtypeStruct(parts.shape[1:], F32), jax.ShapeDtypeStruct((planes * count_y, nev), BF16)]
    all_pieces = [jax.ShapeDtypeStruct((size_x, 2, 4 * group, 3 * nev), BF16)]
    operands = after, swapped_rows, other_links
    first, first_links = call(
        functools.partial(x_middle, 0), "x_middle_first", one, scratch(lead), *operands, got_second[0], table, part
    )
    (pieces,) = call(
        x_last_first, "x_last_first", all_pieces, scratch(tail), *operands, got_last[0], first_links, table, first, sent
    )
    after, _ = lax.optimization_barrier((after, pieces))
    operands = after, swapped_rows, other_links
    second, second_links = call(
        functools.partial(x_middle, 1), "x_middle_second", one, scratch(lead), *operands, got_second[1], table, part
    )
    (pieces,) = call(
        x_last_second, "x_last_second", all_pieces, scratch(tail) + [pltpu.VMEM((4 * nev, 2 * nev), BF16)],
        *operands, got_last[1], second_links, table, second, top, halo, lines, pieces, aliases={10: 0},
    )

    pieces = pieces.reshape(2 * size_x, 4 * group, 3 * nev)
    groups = [[(ts * 2 + h) * 2 + c for ts in range(size_x) for h in range(2)] for c in range(2)]
    got = lax.all_to_all(pieces, ("ts", "gz"), 0, 0, tiled=True, axis_index_groups=groups)
    out_shape = (group, 1, 2, 2, 3 * nev)
    return pl.pallas_call(
        total_kernel,
        grid=(4,),
        in_specs=[in_smem, pl.BlockSpec((size_x // 2, 4 * group, 3 * nev), lambda i: (i, 0, 0))],
        out_specs=pl.BlockSpec(out_shape, lambda i: (0, 0, 0, 0, 0)),
        out_shape=jax.ShapeDtypeStruct(out_shape, F32),
        scratch_shapes=[pltpu.VMEM((4 * group, 3 * nev), F32)],
        compiler_params=limit,
        name="total",
    )(directions, got)


def solution(mesh):
    in_specs = (
        P(None, None, None, "ts", "gz", None, None),
        P(None, None, None, "ts", "gz", None),
        P(),
        P(),
    )
    out_specs = P("ts", "gz", None, None, None)
    return jax.shard_map(shards, mesh=mesh, in_specs=in_specs, out_specs=out_specs, check_vma=False)
```

```python
import functools
import math

import jax
import jax.numpy as jnp
from jax import lax
from jax.experimental import pallas as pl
from jax.experimental.pallas import tpu as pltpu
from jax.sharding import PartitionSpec as P

BF16 = jnp.bfloat16
F32 = jnp.float32


def link_rows(entries, adjoint, width):
    rows = []
    for r in range(2):
        for a in range(3):
            pieces = []
            for q in range(2):
                for b in range(3):
                    first = ((b * 3 + a) if adjoint else (a * 3 + b)) * 2
                    if r == q:
                        pieces.append(entries[first])
                    elif (q == 1) == adjoint:
                        pieces.append(entries[first + 1])
                    else:
                        pieces.append(-entries[first + 1])
            lanes = sum(piece.shape[1] for piece in pieces)
            if lanes < width:
                pieces.append(jnp.zeros((pieces[0].shape[0], width - lanes), F32))
            rows.append(jnp.concatenate(pieces, axis=1))
    return rows


def site_masks(count_y, lanes):
    row = lax.broadcasted_iota(jnp.int32, (count_y, lanes), 0)
    lane = lax.broadcasted_iota(jnp.int32, (count_y, lanes), 1) % count_y
    same = jnp.where(lane == row, 1.0, 0.0).astype(BF16)
    above = jnp.where(lane == (row + 1) % count_y, 1.0, 0.0).astype(BF16)
    below = jnp.where(lane == (row + count_y - 1) % count_y, 1.0, 0.0).astype(BF16)
    return same, above, below


def spread(rows_ref, kind, row, mask):
    count_y, lanes = mask.shape
    blocks = []
    for ra in range(6):
        line = rows_ref[kind, ra, pl.ds(row, 1), :lanes]
        blocks.append(jnp.broadcast_to(line, (count_y, lanes)).astype(BF16) * mask)
    return jnp.concatenate(blocks, axis=0)


def fraction(component, coords, length):
    return jnp.mod(component * coords, length).astype(F32) / length


def table_kernel(lengths, deep, place_ref, momenta_ref, table_ref):
    length_x, length_z, length_y = lengths
    half = table_ref.shape[0] // 2
    shape = 2 * half, table_ref.shape[2]
    row = lax.broadcasted_iota(jnp.int32, shape, 0)
    lane = lax.broadcasted_iota(jnp.int32, shape, 1)
    x_at = row // 2
    x = place_ref[1] + jnp.where(x_at == 2, -1, x_at)
    plane = lane // length_y
    above = deep + (shape[1] // length_y - deep) // 2
    z = place_ref[2] + jnp.where(plane < deep, plane, jnp.where(plane < above, deep, deep - 1))
    y = lane % length_y
    first = row % 2 == 0
    m_x, m_y, m_z = (jnp.where(first, momenta_ref[0, i], momenta_ref[1, i]) for i in range(3))
    angle = 2.0 * math.pi * (
        (fraction(m_x, x, length_x) + fraction(m_y, y, length_y)) + fraction(m_z, z, length_z)
    )
    for first, values in ((0, jnp.cos(angle)), (half, jnp.sin(angle))):
        for at in range(2 * half):
            table_ref[first + at // 2, at % 2 : at % 2 + 1] = values[at : at + 1]


def write_phased(planes_of, table, x_at, table_first, blocks, out_ref, first, colour_stride):
    for b in range(3):
        for block in range(blocks):
            real = planes_of(0, b, block).T.astype(F32)
            imag = planes_of(1, b, block).T.astype(F32)
            nev, sites = real.shape
            at = first + b * colour_stride + block * sites
            put_phased(real, imag, table, x_at, table_first + block * sites, out_ref, at)


def put_phased(real, imag, table, x_at, table_at, out_ref, at):
    nev, sites = real.shape
    for p in range(2):
        cosine, sine = (table[half + x_at, p : p + 1, pl.ds(table_at, sites)] for half in (0, table.shape[0] // 2))
        out_ref[2 * p * nev : (2 * p + 1) * nev, at : at + sites] = (cosine * real - sine * imag).astype(BF16)
        out_ref[(2 * p + 1) * nev : (2 * p + 2) * nev, at : at + sites] = (sine * real + cosine * imag).astype(BF16)


def put_displaced(out_ref, z, terms, count_y, nev):
    for r in range(2):
        for a in range(3):
            rows = terms[(r * 3 + a) * count_y : (r * 3 + a + 1) * count_y]
            out_ref[a, z, :, r * nev : (r + 1) * nev] = rows.astype(BF16)


def combine(products, nev):
    real, imag = [], []
    for p in range(2):
        rr = products[2 * p * nev : (2 * p + 1) * nev, :nev]
        ri = products[2 * p * nev : (2 * p + 1) * nev, nev:]
        ir = products[(2 * p + 1) * nev : (2 * p + 2) * nev, :nev]
        ii = products[(2 * p + 1) * nev : (2 * p + 2) * nev, nev:]
        real.append(rr + ii)
        imag.append(ri - ir)
    return real + imag


def by_owner(first, second):
    nev, lanes = first.shape
    a = first.reshape(nev // 8, 8, lanes)
    b = second.reshape(nev // 8, 8, lanes)
    upper = lax.broadcasted_iota(jnp.int32, a.shape, 1) < 4
    even = jnp.where(upper, a, pltpu.roll(b, 4, 1))
    odd = jnp.where(upper, pltpu.roll(a, 4, 1), b)
    return jnp.stack([even, odd], axis=1).reshape(nev // 4, 8, lanes)


def partial_rows(parts):
    return jnp.concatenate([by_owner(parts[0], parts[1]), by_owner(parts[2], parts[3])], axis=1)


def packed_plane(packed, depth, q, b, z, count, count_y):
    first = ((q * 3 + b) * depth + z) * count_y
    return packed[first : first + count * count_y]


def link_planes(nev, count_z, count_y):
    return -(-18 * count_y * count_z // (nev * count_y))


def packed_link(packed, depth, k, e, count_z, count_y):
    nev = packed.shape[1]
    per_row = nev // count_y
    first = (6 * depth + k * link_planes(nev, count_z, count_y)) * count_y + e // per_row * count_z
    lane = e % per_row * count_y
    return packed[first : first + count_z, lane : lane + count_y]


def put_links(out_ref, at, first_plane, link, count_z, count_y, nev):
    per_row = nev // count_y
    per_plane = count_y // count_z
    for row in range(link_planes(nev, count_z, count_y) * per_plane):
        held = [link(e) for e in range(row * per_row, min(18, (row + 1) * per_row))]
        held += [jnp.zeros((count_z, count_y), BF16)] * (per_row - len(held))
        first = row % per_plane * count_z
        out_ref[at, first_plane + row // per_plane, first : first + count_z] = jnp.concatenate(held, axis=1)


def pack_own_kernel(place_ref, v_ref, link_ref, first_ref, second_ref):
    count_z, count_y, nev = v_ref.shape[3:]
    core, odd = place_ref[0], place_ref[3]
    for out_ref, t in ((first_ref, core + 2 * (1 - odd)), (second_ref, core + 2 * odd)):
        for held in range(6):
            out_ref[0, held * count_z : (held + 1) * count_z] = v_ref[held // 3, held % 3, t]
        put_links(out_ref, 0, 6 * count_z, lambda e, t=t: link_ref[0, e, t], count_z, count_y, nev)


def pack_given_kernel(place_ref, v_ref, given_ref):
    count_z = v_ref.shape[3]
    for m in range(2):
        for held in range(6):
            given_ref[m, held * count_z : (held + 1) * count_z] = v_ref[held // 3, held % 3, 1 - place_ref[0] + 2 * m]


def split(place_ref, swap_ref, start, count_z, out_refs):
    odd = place_ref[3]
    depth = out_refs[0].shape[1] // 6
    for i, out_ref in enumerate(out_refs):
        for held in range(6):
            first = held * count_z + start
            out_ref[0, held * depth : (held + 1) * depth] = swap_ref[odd if i else 1 - odd, first : first + depth]


def split_first_kernel(count_z, place_ref, swap_ref, link_ref, v_ref, first_ref, second_ref, lowest_ref):
    count_y, nev = v_ref.shape[4:]
    split(place_ref, swap_ref, 0, count_z, (first_ref, second_ref))
    core, odd = place_ref[0], place_ref[3]
    for out_ref, t in ((first_ref, core + 2 * (1 - odd)), (second_ref, core + 2 * odd)):
        depth = out_ref.shape[1] // 6
        put_links(out_ref, 0, 6 * depth, lambda e, t=t: link_ref[0, e, t], count_z, count_y, nev)
    for m in range(2):
        for i in range(6):
            own = v_ref[i // 3, i % 3, core + 2 * m, 0]
            lowest_ref[m, i] = jnp.where(core == 0, own, swap_ref[m, i * count_z])


def split_last_kernel(count_z, place_ref, swap_ref, first_ref, second_ref):
    split(place_ref, swap_ref, count_z - first_ref.shape[1] // 6, count_z, (first_ref, second_ref))


def yz_kernel(place_ref, v_ref, swap_ref, link_ref, other_link_ref, table_ref, out_ref, top_ref, line_ref,
              rows, padded, phased, moved_y, moved_z):
    core = place_ref[0]
    step_m = pl.program_id(0)
    t = core + 2 * step_m
    count_z, count_y, nev = v_ref.shape[3:]
    deep = 2 * count_z
    lanes = 6 * count_y
    sites = deep * count_y
    same, above, below = site_masks(count_y, lanes)
    mine = pl.multiple_of(core * count_z, count_z)
    theirs = pl.multiple_of((1 - core) * count_z, count_z)
    wide = rows.shape[3]
    lane = lax.broadcasted_iota(jnp.int32, (count_z, wide), 1) % count_y

    def fill_rows(link, start):
        at = pl.ds(start, count_z)
        link_y = [0.5 * link(1, e).astype(F32) for e in range(18)]
        for ra, line in enumerate(link_rows(link_y, False, wide)):
            rows[0, ra, at, :] = jnp.where(
                lane == 0, pltpu.roll(line, wide - (count_y - 1), 1), pltpu.roll(line, 1, 1)
            )
        for ra, line in enumerate(link_rows(link_y, True, wide)):
            rows[1, ra, at, :] = -line
        link_z = [0.5 * link(2, e).astype(F32) for e in range(18)]
        for ra, line in enumerate(link_rows(link_z, False, wide)):
            rows[2, ra, at, :] = line
        for ra, line in enumerate(link_rows(link_z, True, wide)):
            rows[3, ra, at, :] = -line

    padded[:, :, pl.ds(mine, count_z)] = v_ref[:, :, t]
    swapped = swap_ref.at[step_m]
    for q in range(2):
        for b in range(3):
            block = packed_plane(swapped, count_z, q, b, 0, count_z, count_y)
            padded[q, b, pl.ds(theirs, count_z)] = block.reshape(count_z, count_y, nev)
    fill_rows(lambda k, e: other_link_ref[k, e, t], theirs)
    fill_rows(lambda k, e: link_ref[k, e, t], mine)

    table = table_ref
    step = nev // count_y
    write_phased(
        lambda q, b, block: padded[q, b, block * step : (block + 1) * step].reshape(nev, nev),
        table, 0, 0, sites // nev, phased, 0, sites,
    )
    def forward(z):
        return jnp.dot(
            spread(rows, 2, z, same), padded[:, :, z + 1].reshape(lanes, nev), preferred_element_type=F32
        )

    def backward(z):
        return jnp.dot(
            spread(rows, 3, z - 1, same), padded[:, :, z - 1].reshape(lanes, nev), preferred_element_type=F32
        )

    for z in range(deep):
        in_y = spread(rows, 0, z, above) + spread(rows, 1, z, below)
        terms = jnp.dot(in_y, padded[:, :, z].reshape(lanes, nev), preferred_element_type=F32)
        put_displaced(moved_y, z, terms, count_y, nev)
        terms = forward(z) if z + 1 < deep else 0.0
        if z > 0:
            terms += backward(z)
        put_displaced(moved_z, z, terms, count_y, nev)
    for at, moved in enumerate((moved_y, moved_z)):
        products = jnp.dot(phased[...], moved[...].reshape(3 * sites, 2 * nev), preferred_element_type=F32)
        out_ref[:, 0, :, at * nev : (at + 1) * nev] = partial_rows(combine(products, nev)).astype(BF16)
    top_ref[0] = padded[:, :, deep - 1].reshape(lanes, nev)
    for kind in range(2):
        for ra in range(6):
            line_ref[0, kind * 8 + ra : kind * 8 + ra + 1] = rows[2 + kind, ra, deep - 1 : deep]


def from_rows(ref, depth, count_y, first=0):
    return lambda q, b, z, count: packed_plane(ref, depth, q, b, first + z, count, count_y)


def from_times(ref, t):
    count_y, nev = ref.shape[4:]
    return lambda q, b, z, count: ref[q, b, t, z : z + count].reshape(count * count_y, nev)


def pair_rows(odd, at, own_link, received_link, rows):
    below = odd if at else 1 - odd
    entries = [0.5 * jnp.where(below == 1, own_link(e), received_link(e)).astype(F32) for e in range(18)]
    for ra, line in enumerate(link_rows(entries, False, rows.shape[3])):
        rows[below, ra] = line
    for ra, line in enumerate(link_rows(entries, True, rows.shape[3])):
        rows[1 - below, ra] = -line


def x_terms(odd, at, own, received, link_first, table, table_first, rows, phased, moved):
    lanes = rows.shape[3]
    count_z, count_y = moved.shape[2:4]
    nev = moved.shape[4] // 2
    below = odd if at else 1 - odd
    same = site_masks(count_y, lanes)[0]
    sites = count_z * count_y
    step = nev // count_y
    for vectors, x_at, first in ((own, 0, 0), (received, 2 - below, 3 * sites)):
        write_phased(
            lambda q, b, block: vectors(q, b, block * step, step),
            table, x_at, table_first, sites // nev, phased, first, sites,
        )

    def plane(vectors, z):
        return jnp.concatenate([vectors(q, b, z, 1) for q in range(2) for b in range(3)], axis=0)

    for z in range(count_z):
        line = link_first + z
        terms = jnp.dot(spread(rows, 1, line, same), plane(received, z), preferred_element_type=F32)
        put_displaced(moved.at[0], z, terms, count_y, nev)
        terms = jnp.dot(spread(rows, 0, line, same), plane(own, z), preferred_element_type=F32)
        put_displaced(moved.at[1], z, terms, count_y, nev)
    products = jnp.dot(phased[...], moved[...].reshape(6 * sites, 2 * nev), preferred_element_type=F32)
    return combine(products, nev)


def x_first_kernel(place_ref, v_ref, link_ref, first_ref, second_ref, table, out_ref, rows, phased, moved):
    count_z, count_y = link_ref.shape[3:]
    core, odd = place_ref[0], place_ref[3]
    at_table = pl.multiple_of(core * (count_z * count_y), count_z * count_y)
    for at, got in enumerate((first_ref.at[0], second_ref.at[0])):
        m = 1 - odd if at else odd
        t = core + 2 * m
        pair_rows(
            odd, at, lambda e, t=t: link_ref[0, e, t],
            lambda e, got=got: packed_link(got, count_z, 0, e, count_z, count_y), rows,
        )
        parts = x_terms(
            odd, at, from_times(v_ref, t), from_rows(got, count_z, count_y), 0, table, at_table, rows, phased, moved
        )
        for i, part in enumerate(parts):
            out_ref[m, i] = part


def x_part(first, at, place_ref, swap_ref, got, table, rows, phased, moved):
    held_z = rows.shape[2]
    depth, count_y = moved.shape[2:4]
    core, odd = place_ref[0], place_ref[3]
    at_table = pl.multiple_of((1 - core) * (held_z * count_y) + first * count_y, moved.shape[4] // 2)
    return x_terms(
        odd, at, from_rows(swap_ref.at[1 - odd if at else odd], held_z, count_y, first), from_rows(got, depth, count_y),
        first, table, at_table, rows, phased, moved,
    )


def boundary_below(top, lines, table, phased, displaced, forward):
    lanes, nev = top.shape
    count_y = lanes // 6
    wide = lanes // 2
    same = site_masks(count_y, lanes)[0]

    def matrix(kind):
        blocks = []
        for ra in range(6):
            line = lines[kind * 8 + ra : kind * 8 + ra + 1, :lanes]
            blocks.append(jnp.broadcast_to(line, (count_y, lanes)).astype(BF16) * same)
        return jnp.concatenate(blocks, axis=0)

    put_phased(top[:wide].T.astype(F32), top[wide:].T.astype(F32), table, 0, table.shape[2] - nev, phased, 0)
    terms = jnp.dot(matrix(1), top[...], preferred_element_type=F32).astype(BF16)
    displaced[...] = jnp.concatenate([terms[:wide], terms[wide:]], axis=1)
    forward[:, :lanes] = matrix(0)


def boundary(halo, phased, displaced, forward, table, edge):
    lanes, nev = halo.shape
    wide = lanes // 2
    put_phased(halo[:wide].T.astype(F32), halo[wide:].T.astype(F32), table, 0, table.shape[2] - 2 * nev, edge, 0)
    products = jnp.dot(edge[:, :wide], displaced[...], preferred_element_type=F32)
    terms = jnp.dot(forward[:, :lanes], halo[...], preferred_element_type=F32).astype(BF16)
    terms = jnp.concatenate([terms[:wide], terms[wide:]], axis=1)
    products += jnp.dot(phased[:, :wide], terms, preferred_element_type=F32)
    return combine(products, nev)


def x_middle(at, place_ref, swap_ref, link_ref, got_ref, table, before, out_ref, rows_ref, *scratch):
    held_z = rows_ref.shape[2]
    depth, count_y = scratch[1].shape[2:4]
    core, odd = place_ref[0], place_ref[3]
    m = 1 - odd if at else odd
    got = got_ref.at[0]
    pair_rows(
        odd, at, lambda e: link_ref[0, e, core + 2 * m], lambda e: packed_link(got, depth, 0, e, held_z, count_y), rows_ref
    )
    parts = x_part(0, at, place_ref, swap_ref, got, table, rows_ref, *scratch)
    for i, part in enumerate(parts):
        out_ref[i] = part + before[m, i]


def x_middle_first(place_ref, swap_ref, link_ref, got_ref, table, before, top_ref, line_ref,
                   out_ref, rows_ref, phased_ref, displaced_ref, forward_ref, *scratch):
    for m in range(2):
        boundary_below(
            top_ref.at[m], line_ref.at[m], table, phased_ref.at[m], displaced_ref.at[m], forward_ref.at[m]
        )
    x_middle(0, place_ref, swap_ref, link_ref, got_ref, table, before, out_ref, rows_ref, *scratch)


def x_last(at, place_ref, swap_ref, got_ref, rows_ref, table, before, pieces_ref, *scratch):
    nev = before.shape[2]
    odd = place_ref[3]
    first = rows_ref.shape[2] - scratch[1].shape[2]
    parts = x_part(first, at, place_ref, swap_ref, got_ref.at[0], table, rows_ref, *scratch)
    parts = [part + before[i] for i, part in enumerate(parts)]
    pieces_ref[:, 1 - odd if at else odd, :, 2 * nev :] = partial_rows(parts).astype(BF16)


def x_last_first(place_ref, swap_ref, got_ref, rows_ref, table, before, sent_ref, pieces_ref, *scratch):
    pieces_ref[:, :, :, : sent_ref.shape[3]] = sent_ref[...]
    x_last(0, place_ref, swap_ref, got_ref, rows_ref, table, before, pieces_ref, *scratch)


def x_last_second(place_ref, swap_ref, got_ref, rows_ref, table, before, halo_ref, phased_ref, displaced_ref,
                  forward_ref, sent_ref, pieces_ref, phased, moved, edge):
    nev = before.shape[2]
    for m in range(2):
        parts = boundary(halo_ref.at[m], phased_ref.at[m], displaced_ref.at[m], forward_ref.at[m], table, edge.at[m])
        above = partial_rows(parts)
        pieces_ref[:, m, :, nev : 2 * nev] = (sent_ref[:, m, :, nev : 2 * nev].astype(F32) + above).astype(BF16)
    x_last(1, place_ref, swap_ref, got_ref, rows_ref, table, before, pieces_ref, phased, moved)


def total_kernel(directions_ref, got_ref, out_ref, total_ref):
    step = pl.program_id(0)
    part = jnp.sum(got_ref[...].astype(F32), axis=0)

    @pl.when(step == 0)
    def _():
        total_ref[...] = part

    @pl.when(step > 0)
    def _():
        total_ref[...] += part

    @pl.when(step == pl.num_programs(0) - 1)
    def _():
        total = total_ref[...]
        nev = total.shape[1] // 3
        group = out_ref.shape[0]
        in_y, in_z, in_x = (total[:, k * nev : (k + 1) * nev] for k in range(3))
        for d in range(3):
            direction = directions_ref[d]
            chosen = jnp.where(direction == 0, in_x, jnp.where(direction == 1, in_y, in_z))
            for r in range(2):
                for p in range(2):
                    for i in range(group):
                        row = (r * 2 + p) * group + i
                        out_ref[i, 0, p, r : r + 1, d * nev : (d + 1) * nev] = chosen[row : row + 1]


def exchange(first, second):
    count = lax.axis_size("ts")
    got = [None, None]
    for at, array in ((0, first), (1, second)):
        pairs = [(i, (i + 1 if (i + at) % 2 == 0 else i - 1) % count) for i in range(count)]
        got[at] = lax.ppermute(array.reshape(1, -1, array.shape[-1]), "ts", pairs)
    return got


def shards(eigvecs, gauge_links, momenta, directions):
    _, _, count_t, _, count_z, count_y, nev = eigvecs.shape
    vectors = eigvecs.reshape(2, 3, count_t, count_z, count_y, nev)
    links = gauge_links.reshape(3, 18, count_t, count_z, count_y)
    size_x, size_g = lax.axis_size("ts"), lax.axis_size("gz")
    x, g = lax.axis_index("ts"), lax.axis_index("gz")
    core, chip = g % 2, g // 2
    deep = 2 * count_z
    sites = count_z * count_y
    group = nev // size_x

    small = pl.CostEstimate(flops=1_000_000, bytes_accessed=100_000, transcendentals=0)
    limit = pltpu.CompilerParams(vmem_limit_bytes=20 * 1024 * 1024)
    in_vmem = pl.BlockSpec(memory_space=pltpu.VMEM)
    in_smem = pl.BlockSpec(memory_space=pltpu.SMEM)
    planes = link_planes(nev, count_z, count_y)

    place = jnp.stack([core, x, chip * deep, x % 2]).astype(jnp.int32)

    def planes_of(times, depth, directions):
        return jax.ShapeDtypeStruct((times, 6 * depth + directions * planes, count_y, nev), BF16)

    def call(kernel, name, out_shape, scratch_shapes, *operands, aliases={}):
        in_specs = [in_smem] + [in_vmem] * (len(operands) - 1)
        return pl.pallas_call(
            kernel,
            in_specs=in_specs,
            out_specs=jax.tree.map(lambda _: in_vmem, out_shape),
            out_shape=out_shape,
            scratch_shapes=scratch_shapes,
            input_output_aliases=aliases,
            compiler_params=limit,
            cost_estimate=small,
            name=name,
        )(*operands)

    swap = [(0, 1), (1, 0), (2, 3), (3, 2)]
    other_links = lax.ppermute(gauge_links, "gz", swap).reshape(links.shape)
    mine = call(pack_own_kernel, "pack_own", [planes_of(1, count_z, 1)] * 2, [], place, vectors, links)
    got_first = exchange(*mine)
    after, other_links, _ = lax.optimization_barrier((place, other_links, mine[0]))
    (given,) = call(pack_given_kernel, "pack_given", [planes_of(2, count_z, 0)], [], after, vectors)
    swapped = lax.ppermute(given, "gz", swap)
    tail = nev // count_y
    lead = count_z - tail
    table = pl.pallas_call(
        functools.partial(table_kernel, (size_x, count_z * size_g, count_y), deep),
        in_specs=[in_smem, in_smem],
        out_specs=in_vmem,
        out_shape=jax.ShapeDtypeStruct((8, 2, 2 * sites + 2 * nev), F32),
        compiler_params=limit,
        cost_estimate=pl.CostEstimate(flops=20_000_000_000, bytes_accessed=100_000, transcendentals=0),
        name="phase_table",
    )(place, momenta)
    after, _ = lax.optimization_barrier((place, table))
    shapes = [planes_of(1, lead, 1)] * 2 + [jax.ShapeDtypeStruct((2, 6, count_y, nev), BF16)]
    *mine, lowest = call(
        functools.partial(split_first_kernel, count_z), "split_first", shapes, [], after, swapped, other_links, vectors
    )
    got_second = exchange(*mine)
    halo = lax.ppermute(lowest.reshape(2, 6 * count_y, nev), "gz", [(0, 2), (2, 0), (1, 3), (3, 1)])

    after, _ = lax.optimization_barrier((place, lowest))
    swapped_rows = swapped.reshape(2, -1, nev)
    sent, top, lines = pl.pallas_call(
        yz_kernel,
        grid=(2,),
        in_specs=[in_smem] + [in_vmem] * 5,
        out_specs=[
            pl.BlockSpec((size_x, 1, 4 * group, 2 * nev), lambda m: (0, m, 0, 0)),
            pl.BlockSpec((1, 6 * count_y, nev), lambda m: (m, 0, 0)),
            pl.BlockSpec((1, 16, 2 * nev), lambda m: (m, 0, 0)),
        ],
        out_shape=[
            jax.ShapeDtypeStruct((size_x, 2, 4 * group, 2 * nev), BF16),
            jax.ShapeDtypeStruct((2, 6 * count_y, nev), BF16),
            jax.ShapeDtypeStruct((2, 16, 2 * nev), F32),
        ],
        scratch_shapes=[
            pltpu.VMEM((4, 6, deep, 2 * nev), F32),
            pltpu.VMEM((2, 3, deep, count_y, nev), BF16),
            pltpu.VMEM((4 * nev, 6 * sites), BF16),
            pltpu.VMEM((3, deep, count_y, 2 * nev), BF16),
            pltpu.VMEM((3, deep, count_y, 2 * nev), BF16),
        ],
        compiler_params=limit,
        cost_estimate=small,
        name="yz_terms",
    )(after, vectors, swapped_rows, links, other_links, table)

    after, _ = lax.optimization_barrier((place, sent))
    mine = call(
        functools.partial(split_last_kernel, count_z), "split_last", [planes_of(1, tail, 0)] * 2, [], after, swapped
    )
    got_last = exchange(*mine)

    def scratch(depth):
        return [
            pltpu.VMEM((4 * nev, 6 * depth * count_y), BF16),
            pltpu.VMEM((2, 3, depth, count_y, 2 * nev), BF16),
        ]

    parts = jax.ShapeDtypeStruct((2, 4, nev, nev), F32)
    rows_shape = (2, 6, count_z, 6 * count_y)
    (part,) = call(
        x_first_kernel, "x_first", [parts], [pltpu.VMEM(rows_shape, F32)] + scratch(count_z), after, vectors, links, *got_first, table
    )
    one = [jax.ShapeDtypeStruct(parts.shape[1:], F32), jax.ShapeDtypeStruct(rows_shape, F32)]
    all_pieces = [jax.ShapeDtypeStruct((size_x, 2, 4 * group, 3 * nev), BF16)]
    operands = after, swapped_rows, other_links
    edges = [
        jax.ShapeDtypeStruct((2, 4 * nev, nev), BF16),
        jax.ShapeDtypeStruct((2, 3 * count_y, 2 * nev), BF16),
        jax.ShapeDtypeStruct((2, 6 * count_y, 2 * nev), BF16),
    ]
    first, first_rows, *edges = call(
        x_middle_first, "x_middle_first", one + edges, scratch(lead),
        *operands, got_second[0], table, part, top, lines,
    )
    after, _ = lax.optimization_barrier((after, first_rows))
    operands = after, swapped_rows, other_links
    second, second_rows = call(
        functools.partial(x_middle, 1), "x_middle_second", one, scratch(lead), *operands, got_second[1], table, part
    )
    after, _ = lax.optimization_barrier((after, second_rows))
    operands = after, swapped_rows, other_links
    (pieces,) = call(
        x_last_first, "x_last_first", all_pieces, scratch(tail), *operands[:2], got_last[0], first_rows, table, first, sent
    )
    (pieces,) = call(
        x_last_second, "x_last_second", all_pieces, scratch(tail) + [pltpu.VMEM((2, 4 * nev, nev), BF16)],
        *operands[:2], got_last[1], second_rows, table, second, halo, *edges, pieces, aliases={10: 0},
    )

    pieces = pieces.reshape(2 * size_x, 4 * group, 3 * nev)
    groups = [[(ts * 2 + h) * 2 + c for ts in range(size_x) for h in range(2)] for c in range(2)]
    got = lax.all_to_all(pieces, ("ts", "gz"), 0, 0, tiled=True, axis_index_groups=groups)
    out_shape = (group, 1, 2, 2, 3 * nev)
    return pl.pallas_call(
        total_kernel,
        grid=(4,),
        in_specs=[in_smem, pl.BlockSpec((size_x // 2, 4 * group, 3 * nev), lambda i: (i, 0, 0))],
        out_specs=pl.BlockSpec(out_shape, lambda i: (0, 0, 0, 0, 0)),
        out_shape=jax.ShapeDtypeStruct(out_shape, F32),
        scratch_shapes=[pltpu.VMEM((4 * group, 3 * nev), F32)],
        compiler_params=limit,
        name="total",
    )(directions, got)


def solution(mesh):
    in_specs = (
        P(None, None, None, "ts", "gz", None, None),
        P(None, None, None, "ts", "gz", None),
        P(),
        P(),
    )
    out_specs = P("ts", "gz", None, None, None)
    return jax.shard_map(shards, mesh=mesh, in_specs=in_specs, out_specs=out_specs, check_vma=False)
```

```python
import functools
import math

import jax
import jax.numpy as jnp
from jax import lax
from jax.experimental import pallas as pl
from jax.experimental.pallas import tpu as pltpu
from jax.sharding import PartitionSpec as P

BF16 = jnp.bfloat16
F32 = jnp.float32


def link_rows(entries, adjoint, width):
    rows = []
    for r in range(2):
        for a in range(3):
            pieces = []
            for q in range(2):
                for b in range(3):
                    first = ((b * 3 + a) if adjoint else (a * 3 + b)) * 2
                    if r == q:
                        pieces.append(entries[first])
                    elif (q == 1) == adjoint:
                        pieces.append(entries[first + 1])
                    else:
                        pieces.append(-entries[first + 1])
            lanes = sum(piece.shape[1] for piece in pieces)
            if lanes < width:
                pieces.append(jnp.zeros((pieces[0].shape[0], width - lanes), F32))
            rows.append(jnp.concatenate(pieces, axis=1))
    return rows


def site_masks(count_y, lanes):
    row = lax.broadcasted_iota(jnp.int32, (count_y, lanes), 0)
    lane = lax.broadcasted_iota(jnp.int32, (count_y, lanes), 1) % count_y
    same = jnp.where(lane == row, 1.0, 0.0).astype(BF16)
    above = jnp.where(lane == (row + 1) % count_y, 1.0, 0.0).astype(BF16)
    below = jnp.where(lane == (row + count_y - 1) % count_y, 1.0, 0.0).astype(BF16)
    return same, above, below


def spread(rows_ref, kind, row, mask):
    count_y, lanes = mask.shape
    blocks = []
    for ra in range(6):
        line = rows_ref[kind, ra, pl.ds(row, 1), :lanes]
        blocks.append(jnp.broadcast_to(line, (count_y, lanes)).astype(BF16) * mask)
    return jnp.concatenate(blocks, axis=0)


def fraction(component, coords, length):
    return jnp.mod(component * coords, length).astype(F32) / length


def table_kernel(lengths, deep, place_ref, momenta_ref, table_ref):
    length_x, length_z, length_y = lengths
    half = table_ref.shape[0] // 2
    shape = 2 * half, table_ref.shape[2]
    row = lax.broadcasted_iota(jnp.int32, shape, 0)
    lane = lax.broadcasted_iota(jnp.int32, shape, 1)
    x_at = row // 2
    x = place_ref[1] + jnp.where(x_at == 2, -1, x_at)
    plane = lane // length_y
    above = deep + (shape[1] // length_y - deep) // 2
    z = place_ref[2] + jnp.where(plane < deep, plane, jnp.where(plane < above, deep, deep - 1))
    y = lane % length_y
    first = row % 2 == 0
    m_x, m_y, m_z = (jnp.where(first, momenta_ref[0, i], momenta_ref[1, i]) for i in range(3))
    angle = 2.0 * math.pi * (
        (fraction(m_x, x, length_x) + fraction(m_y, y, length_y)) + fraction(m_z, z, length_z)
    )
    for first, values in ((0, jnp.cos(angle)), (half, jnp.sin(angle))):
        for at in range(2 * half):
            table_ref[first + at // 2, at % 2 : at % 2 + 1] = values[at : at + 1]


def write_phased(planes_of, table, x_at, table_first, blocks, out_ref, first, colour_stride):
    for b in range(3):
        for block in range(blocks):
            real = planes_of(0, b, block).T.astype(F32)
            imag = planes_of(1, b, block).T.astype(F32)
            nev, sites = real.shape
            at = first + b * colour_stride + block * sites
            put_phased(real, imag, table, x_at, table_first + block * sites, out_ref, at)


def put_phased(real, imag, table, x_at, table_at, out_ref, at):
    nev, sites = real.shape
    for p in range(2):
        cosine, sine = (table[half + x_at, p : p + 1, pl.ds(table_at, sites)] for half in (0, table.shape[0] // 2))
        out_ref[2 * p * nev : (2 * p + 1) * nev, at : at + sites] = (cosine * real - sine * imag).astype(BF16)
        out_ref[(2 * p + 1) * nev : (2 * p + 2) * nev, at : at + sites] = (sine * real + cosine * imag).astype(BF16)


def put_displaced(out_ref, z, terms, count_y, nev):
    for r in range(2):
        for a in range(3):
            rows = terms[(r * 3 + a) * count_y : (r * 3 + a + 1) * count_y]
            out_ref[a, z, :, r * nev : (r + 1) * nev] = rows.astype(BF16)


def combine(products, nev):
    real, imag = [], []
    for p in range(2):
        rr = products[2 * p * nev : (2 * p + 1) * nev, :nev]
        ri = products[2 * p * nev : (2 * p + 1) * nev, nev:]
        ir = products[(2 * p + 1) * nev : (2 * p + 2) * nev, :nev]
        ii = products[(2 * p + 1) * nev : (2 * p + 2) * nev, nev:]
        real.append(rr + ii)
        imag.append(ri - ir)
    return real + imag


def by_owner(first, second):
    nev, lanes = first.shape
    a = first.reshape(nev // 8, 8, lanes)
    b = second.reshape(nev // 8, 8, lanes)
    upper = lax.broadcasted_iota(jnp.int32, a.shape, 1) < 4
    even = jnp.where(upper, a, pltpu.roll(b, 4, 1))
    odd = jnp.where(upper, pltpu.roll(a, 4, 1), b)
    return jnp.stack([even, odd], axis=1).reshape(nev // 4, 8, lanes)


def partial_rows(parts):
    return jnp.concatenate([by_owner(parts[0], parts[1]), by_owner(parts[2], parts[3])], axis=1)


def packed_plane(packed, depth, q, b, z, count, count_y):
    first = ((q * 3 + b) * depth + z) * count_y
    return packed[first : first + count * count_y]


def link_planes(nev, count_z, count_y):
    return -(-18 * count_y * count_z // (nev * count_y))


def packed_link(packed, depth, k, e, count_z, count_y):
    nev = packed.shape[1]
    per_row = nev // count_y
    first = (6 * depth + k * link_planes(nev, count_z, count_y)) * count_y + e // per_row * count_z
    lane = e % per_row * count_y
    return packed[first : first + count_z, lane : lane + count_y]


def put_links(out_ref, at, first_plane, link, count_z, count_y, nev):
    per_row = nev // count_y
    per_plane = count_y // count_z
    for row in range(link_planes(nev, count_z, count_y) * per_plane):
        held = [link(e) for e in range(row * per_row, min(18, (row + 1) * per_row))]
        held += [jnp.zeros((count_z, count_y), BF16)] * (per_row - len(held))
        first = row % per_plane * count_z
        out_ref[at, first_plane + row // per_plane, first : first + count_z] = jnp.concatenate(held, axis=1)


def pack_own_kernel(place_ref, v_ref, link_ref, first_ref, second_ref):
    count_z, count_y, nev = v_ref.shape[3:]
    core, odd = place_ref[0], place_ref[3]
    for out_ref, t in ((first_ref, core + 2 * (1 - odd)), (second_ref, core + 2 * odd)):
        for held in range(6):
            out_ref[0, held * count_z : (held + 1) * count_z] = v_ref[held // 3, held % 3, t]
        put_links(out_ref, 0, 6 * count_z, lambda e, t=t: link_ref[0, e, t], count_z, count_y, nev)


def pack_given_kernel(place_ref, v_ref, link_ref, given_ref):
    count_z, count_y, nev = v_ref.shape[3:]
    planes = link_planes(nev, count_z, count_y)
    for m in range(2):
        t = 1 - place_ref[0] + 2 * m
        for held in range(6):
            given_ref[m, held * count_z : (held + 1) * count_z] = v_ref[held // 3, held % 3, t]
        for k in range(3):
            put_links(
                given_ref, m, 6 * count_z + k * planes, lambda e, k=k, t=t: link_ref[k, e, t], count_z, count_y, nev
            )


def split(place_ref, swap_ref, start, count_z, out_refs):
    odd = place_ref[3]
    depth = out_refs[0].shape[1] // 6
    for i, out_ref in enumerate(out_refs):
        for held in range(6):
            first = held * count_z + start
            out_ref[0, held * depth : (held + 1) * depth] = swap_ref[odd if i else 1 - odd, first : first + depth]


def split_first_kernel(count_z, place_ref, swap_ref, v_ref, first_ref, second_ref, lowest_ref):
    split(place_ref, swap_ref, 0, count_z, (first_ref, second_ref))
    core, odd = place_ref[0], place_ref[3]
    for out_ref, m in ((first_ref, 1 - odd), (second_ref, odd)):
        depth = out_ref.shape[1] // 6
        planes = out_ref.shape[1] - 6 * depth
        out_ref[0, 6 * depth :] = swap_ref[m, 6 * count_z : 6 * count_z + planes]
    for m in range(2):
        for i in range(6):
            own = v_ref[i // 3, i % 3, core + 2 * m, 0]
            lowest_ref[m, i] = jnp.where(core == 0, own, swap_ref[m, i * count_z])


def split_last_kernel(count_z, place_ref, swap_ref, first_ref, second_ref):
    split(place_ref, swap_ref, count_z - first_ref.shape[1] // 6, count_z, (first_ref, second_ref))


def yz_kernel(place_ref, v_ref, swap_ref, link_ref, table_ref, out_ref, top_ref, line_ref,
              rows, padded, phased, moved_y, moved_z):
    core = place_ref[0]
    step_m = pl.program_id(0)
    t = core + 2 * step_m
    count_z, count_y, nev = v_ref.shape[3:]
    deep = 2 * count_z
    lanes = 6 * count_y
    sites = deep * count_y
    same, above, below = site_masks(count_y, lanes)
    mine = pl.multiple_of(core * count_z, count_z)
    theirs = pl.multiple_of((1 - core) * count_z, count_z)
    wide = rows.shape[3]
    lane = lax.broadcasted_iota(jnp.int32, (count_z, wide), 1) % count_y

    def fill_rows(link, start):
        at = pl.ds(start, count_z)
        link_y = [0.5 * link(1, e).astype(F32) for e in range(18)]
        for ra, line in enumerate(link_rows(link_y, False, wide)):
            rows[0, ra, at, :] = jnp.where(
                lane == 0, pltpu.roll(line, wide - (count_y - 1), 1), pltpu.roll(line, 1, 1)
            )
        for ra, line in enumerate(link_rows(link_y, True, wide)):
            rows[1, ra, at, :] = -line
        link_z = [0.5 * link(2, e).astype(F32) for e in range(18)]
        for ra, line in enumerate(link_rows(link_z, False, wide)):
            rows[2, ra, at, :] = line
        for ra, line in enumerate(link_rows(link_z, True, wide)):
            rows[3, ra, at, :] = -line

    padded[:, :, pl.ds(mine, count_z)] = v_ref[:, :, t]
    swapped = swap_ref.at[step_m]
    for q in range(2):
        for b in range(3):
            block = packed_plane(swapped, count_z, q, b, 0, count_z, count_y)
            padded[q, b, pl.ds(theirs, count_z)] = block.reshape(count_z, count_y, nev)
    fill_rows(lambda k, e: packed_link(swapped, count_z, k, e, count_z, count_y), theirs)
    fill_rows(lambda k, e: link_ref[k, e, t], mine)

    table = table_ref
    step = nev // count_y
    write_phased(
        lambda q, b, block: padded[q, b, block * step : (block + 1) * step].reshape(nev, nev),
        table, 0, 0, sites // nev, phased, 0, sites,
    )
    def forward(z):
        return jnp.dot(
            spread(rows, 2, z, same), padded[:, :, z + 1].reshape(lanes, nev), preferred_element_type=F32
        )

    def backward(z):
        return jnp.dot(
            spread(rows, 3, z - 1, same), padded[:, :, z - 1].reshape(lanes, nev), preferred_element_type=F32
        )

    for z in range(deep):
        in_y = spread(rows, 0, z, above) + spread(rows, 1, z, below)
        terms = jnp.dot(in_y, padded[:, :, z].reshape(lanes, nev), preferred_element_type=F32)
        put_displaced(moved_y, z, terms, count_y, nev)
        terms = forward(z) if z + 1 < deep else 0.0
        if z > 0:
            terms += backward(z)
        put_displaced(moved_z, z, terms, count_y, nev)
    for at, moved in enumerate((moved_y, moved_z)):
        products = jnp.dot(phased[...], moved[...].reshape(3 * sites, 2 * nev), preferred_element_type=F32)
        out_ref[:, 0, :, at * nev : (at + 1) * nev] = partial_rows(combine(products, nev)).astype(BF16)
    top_ref[0] = padded[:, :, deep - 1].reshape(lanes, nev)
    for kind in range(2):
        for ra in range(6):
            line_ref[0, kind * 8 + ra : kind * 8 + ra + 1] = rows[2 + kind, ra, deep - 1 : deep]


def from_rows(ref, depth, count_y, first=0):
    return lambda q, b, z, count: packed_plane(ref, depth, q, b, first + z, count, count_y)


def from_times(ref, t):
    count_y, nev = ref.shape[4:]
    return lambda q, b, z, count: ref[q, b, t, z : z + count].reshape(count * count_y, nev)


def pair_rows(odd, at, own_link, received_link, rows):
    below = odd if at else 1 - odd
    entries = [0.5 * jnp.where(below == 1, own_link(e), received_link(e)).astype(F32) for e in range(18)]
    for ra, line in enumerate(link_rows(entries, False, rows.shape[3])):
        rows[below, ra] = line
    for ra, line in enumerate(link_rows(entries, True, rows.shape[3])):
        rows[1 - below, ra] = -line


def x_terms(odd, at, own, received, link_first, table, table_first, rows, phased, moved):
    lanes = rows.shape[3]
    count_z, count_y = moved.shape[2:4]
    nev = moved.shape[4] // 2
    below = odd if at else 1 - odd
    same = site_masks(count_y, lanes)[0]
    sites = count_z * count_y
    step = nev // count_y
    for vectors, x_at, first in ((own, 0, 0), (received, 2 - below, 3 * sites)):
        write_phased(
            lambda q, b, block: vectors(q, b, block * step, step),
            table, x_at, table_first, sites // nev, phased, first, sites,
        )

    def plane(vectors, z):
        return jnp.concatenate([vectors(q, b, z, 1) for q in range(2) for b in range(3)], axis=0)

    for z in range(count_z):
        line = link_first + z
        terms = jnp.dot(spread(rows, 1, line, same), plane(received, z), preferred_element_type=F32)
        put_displaced(moved.at[0], z, terms, count_y, nev)
        terms = jnp.dot(spread(rows, 0, line, same), plane(own, z), preferred_element_type=F32)
        put_displaced(moved.at[1], z, terms, count_y, nev)
    products = jnp.dot(phased[...], moved[...].reshape(6 * sites, 2 * nev), preferred_element_type=F32)
    return combine(products, nev)


def x_first_kernel(place_ref, v_ref, link_ref, first_ref, second_ref, table, out_ref, rows, phased, moved):
    count_z, count_y = link_ref.shape[3:]
    core, odd = place_ref[0], place_ref[3]
    at_table = pl.multiple_of(core * (count_z * count_y), count_z * count_y)
    for at, got in enumerate((first_ref.at[0], second_ref.at[0])):
        m = 1 - odd if at else odd
        t = core + 2 * m
        pair_rows(
            odd, at, lambda e, t=t: link_ref[0, e, t],
            lambda e, got=got: packed_link(got, count_z, 0, e, count_z, count_y), rows,
        )
        parts = x_terms(
            odd, at, from_times(v_ref, t), from_rows(got, count_z, count_y), 0, table, at_table, rows, phased, moved
        )
        for i, part in enumerate(parts):
            out_ref[m, i] = part


def x_part(first, at, place_ref, swap_ref, got, table, rows, phased, moved):
    held_z = rows.shape[2]
    depth, count_y = moved.shape[2:4]
    core, odd = place_ref[0], place_ref[3]
    at_table = pl.multiple_of((1 - core) * (held_z * count_y) + first * count_y, moved.shape[4] // 2)
    return x_terms(
        odd, at, from_rows(swap_ref.at[1 - odd if at else odd], held_z, count_y, first), from_rows(got, depth, count_y),
        first, table, at_table, rows, phased, moved,
    )


def boundary_below(top, lines, table, phased, displaced, forward):
    lanes, nev = top.shape
    count_y = lanes // 6
    wide = lanes // 2
    same = site_masks(count_y, lanes)[0]

    def matrix(kind):
        blocks = []
        for ra in range(6):
            line = lines[kind * 8 + ra : kind * 8 + ra + 1, :lanes]
            blocks.append(jnp.broadcast_to(line, (count_y, lanes)).astype(BF16) * same)
        return jnp.concatenate(blocks, axis=0)

    put_phased(top[:wide].T.astype(F32), top[wide:].T.astype(F32), table, 0, table.shape[2] - nev, phased, 0)
    terms = jnp.dot(matrix(1), top[...], preferred_element_type=F32).astype(BF16)
    displaced[...] = jnp.concatenate([terms[:wide], terms[wide:]], axis=1)
    forward[:, :lanes] = matrix(0)


def boundary(halo, phased, displaced, forward, table, edge):
    lanes, nev = halo.shape
    wide = lanes // 2
    put_phased(halo[:wide].T.astype(F32), halo[wide:].T.astype(F32), table, 0, table.shape[2] - 2 * nev, edge, 0)
    products = jnp.dot(edge[:, :wide], displaced[...], preferred_element_type=F32)
    terms = jnp.dot(forward[:, :lanes], halo[...], preferred_element_type=F32).astype(BF16)
    terms = jnp.concatenate([terms[:wide], terms[wide:]], axis=1)
    products += jnp.dot(phased[:, :wide], terms, preferred_element_type=F32)
    return combine(products, nev)


def x_middle(at, place_ref, swap_ref, got_ref, table, before, out_ref, rows_ref, *scratch):
    held_z = rows_ref.shape[2]
    depth, count_y = scratch[1].shape[2:4]
    odd = place_ref[3]
    m = 1 - odd if at else odd
    own, got = swap_ref.at[m], got_ref.at[0]
    pair_rows(
        odd, at, lambda e: packed_link(own, held_z, 0, e, held_z, count_y),
        lambda e: packed_link(got, depth, 0, e, held_z, count_y), rows_ref,
    )
    parts = x_part(0, at, place_ref, swap_ref, got, table, rows_ref, *scratch)
    for i, part in enumerate(parts):
        out_ref[i] = part + before[m, i]


def x_middle_first(place_ref, swap_ref, got_ref, table, before, top_ref, line_ref,
                   out_ref, rows_ref, phased_ref, displaced_ref, forward_ref, *scratch):
    for m in range(2):
        boundary_below(
            top_ref.at[m], line_ref.at[m], table, phased_ref.at[m], displaced_ref.at[m], forward_ref.at[m]
        )
    x_middle(0, place_ref, swap_ref, got_ref, table, before, out_ref, rows_ref, *scratch)


def x_last(at, place_ref, swap_ref, got_ref, rows_ref, table, before, pieces_ref, *scratch):
    nev = before.shape[2]
    odd = place_ref[3]
    first = rows_ref.shape[2] - scratch[1].shape[2]
    parts = x_part(first, at, place_ref, swap_ref, got_ref.at[0], table, rows_ref, *scratch)
    parts = [part + before[i] for i, part in enumerate(parts)]
    pieces_ref[:, 1 - odd if at else odd, :, 2 * nev :] = partial_rows(parts).astype(BF16)


def x_last_first(place_ref, swap_ref, got_ref, rows_ref, table, before, sent_ref, pieces_ref, *scratch):
    pieces_ref[:, :, :, : sent_ref.shape[3]] = sent_ref[...]
    x_last(0, place_ref, swap_ref, got_ref, rows_ref, table, before, pieces_ref, *scratch)


def x_last_second(place_ref, swap_ref, got_ref, rows_ref, table, before, halo_ref, phased_ref, displaced_ref,
                  forward_ref, sent_ref, pieces_ref, phased, moved, edge):
    nev = before.shape[2]
    for m in range(2):
        parts = boundary(halo_ref.at[m], phased_ref.at[m], displaced_ref.at[m], forward_ref.at[m], table, edge.at[m])
        above = partial_rows(parts)
        pieces_ref[:, m, :, nev : 2 * nev] = (sent_ref[:, m, :, nev : 2 * nev].astype(F32) + above).astype(BF16)
    x_last(1, place_ref, swap_ref, got_ref, rows_ref, table, before, pieces_ref, phased, moved)


def total_kernel(directions_ref, got_ref, out_ref, total_ref):
    step = pl.program_id(0)
    part = jnp.sum(got_ref[...].astype(F32), axis=0)

    @pl.when(step == 0)
    def _():
        total_ref[...] = part

    @pl.when(step > 0)
    def _():
        total_ref[...] += part

    @pl.when(step == pl.num_programs(0) - 1)
    def _():
        total = total_ref[...]
        nev = total.shape[1] // 3
        group = out_ref.shape[0]
        in_y, in_z, in_x = (total[:, k * nev : (k + 1) * nev] for k in range(3))
        for d in range(3):
            direction = directions_ref[d]
            chosen = jnp.where(direction == 0, in_x, jnp.where(direction == 1, in_y, in_z))
            for r in range(2):
                for p in range(2):
                    for i in range(group):
                        row = (r * 2 + p) * group + i
                        out_ref[i, 0, p, r : r + 1, d * nev : (d + 1) * nev] = chosen[row : row + 1]


def exchange(first, second):
    count = lax.axis_size("ts")
    got = [None, None]
    for at, array in ((0, first), (1, second)):
        pairs = [(i, (i + 1 if (i + at) % 2 == 0 else i - 1) % count) for i in range(count)]
        got[at] = lax.ppermute(array.reshape(1, -1, array.shape[-1]), "ts", pairs)
    return got


def shards(eigvecs, gauge_links, momenta, directions):
    _, _, count_t, _, count_z, count_y, nev = eigvecs.shape
    vectors = eigvecs.reshape(2, 3, count_t, count_z, count_y, nev)
    links = gauge_links.reshape(3, 18, count_t, count_z, count_y)
    size_x, size_g = lax.axis_size("ts"), lax.axis_size("gz")
    x, g = lax.axis_index("ts"), lax.axis_index("gz")
    core, chip = g % 2, g // 2
    deep = 2 * count_z
    sites = count_z * count_y
    group = nev // size_x

    small = pl.CostEstimate(flops=1_000_000, bytes_accessed=100_000, transcendentals=0)
    limit = pltpu.CompilerParams(vmem_limit_bytes=20 * 1024 * 1024)
    in_vmem = pl.BlockSpec(memory_space=pltpu.VMEM)
    in_smem = pl.BlockSpec(memory_space=pltpu.SMEM)
    planes = link_planes(nev, count_z, count_y)

    place = jnp.stack([core, x, chip * deep, x % 2]).astype(jnp.int32)

    def planes_of(times, depth, directions):
        return jax.ShapeDtypeStruct((times, 6 * depth + directions * planes, count_y, nev), BF16)

    def call(kernel, name, out_shape, scratch_shapes, *operands, aliases={}):
        in_specs = [in_smem] + [in_vmem] * (len(operands) - 1)
        return pl.pallas_call(
            kernel,
            in_specs=in_specs,
            out_specs=jax.tree.map(lambda _: in_vmem, out_shape),
            out_shape=out_shape,
            scratch_shapes=scratch_shapes,
            input_output_aliases=aliases,
            compiler_params=limit,
            cost_estimate=small,
            name=name,
        )(*operands)

    swap = [(0, 1), (1, 0), (2, 3), (3, 2)]
    mine = call(pack_own_kernel, "pack_own", [planes_of(1, count_z, 1)] * 2, [], place, vectors, links)
    got_first = exchange(*mine)
    after, _ = lax.optimization_barrier((place, mine[0]))
    (given,) = call(pack_given_kernel, "pack_given", [planes_of(2, count_z, 3)], [], after, vectors, links)
    swapped = lax.ppermute(given, "gz", swap)
    tail = nev // count_y
    lead = count_z - tail
    table = pl.pallas_call(
        functools.partial(table_kernel, (size_x, count_z * size_g, count_y), deep),
        in_specs=[in_smem, in_smem],
        out_specs=in_vmem,
        out_shape=jax.ShapeDtypeStruct((8, 2, 2 * sites + 2 * nev), F32),
        compiler_params=limit,
        cost_estimate=pl.CostEstimate(flops=20_000_000_000, bytes_accessed=100_000, transcendentals=0),
        name="phase_table",
    )(place, momenta)
    after, _ = lax.optimization_barrier((place, table))
    shapes = [planes_of(1, lead, 1)] * 2 + [jax.ShapeDtypeStruct((2, 6, count_y, nev), BF16)]
    *mine, lowest = call(
        functools.partial(split_first_kernel, count_z), "split_first", shapes, [], after, swapped, vectors
    )
    got_second = exchange(*mine)
    halo = lax.ppermute(lowest.reshape(2, 6 * count_y, nev), "gz", [(0, 2), (2, 0), (1, 3), (3, 1)])

    after, _ = lax.optimization_barrier((place, lowest))
    swapped_rows = swapped.reshape(2, -1, nev)
    sent, top, lines = pl.pallas_call(
        yz_kernel,
        grid=(2,),
        in_specs=[in_smem] + [in_vmem] * 4,
        out_specs=[
            pl.BlockSpec((size_x, 1, 4 * group, 2 * nev), lambda m: (0, m, 0, 0)),
            pl.BlockSpec((1, 6 * count_y, nev), lambda m: (m, 0, 0)),
            pl.BlockSpec((1, 16, 2 * nev), lambda m: (m, 0, 0)),
        ],
        out_shape=[
            jax.ShapeDtypeStruct((size_x, 2, 4 * group, 2 * nev), BF16),
            jax.ShapeDtypeStruct((2, 6 * count_y, nev), BF16),
            jax.ShapeDtypeStruct((2, 16, 2 * nev), F32),
        ],
        scratch_shapes=[
            pltpu.VMEM((4, 6, deep, 2 * nev), F32),
            pltpu.VMEM((2, 3, deep, count_y, nev), BF16),
            pltpu.VMEM((4 * nev, 6 * sites), BF16),
            pltpu.VMEM((3, deep, count_y, 2 * nev), BF16),
            pltpu.VMEM((3, deep, count_y, 2 * nev), BF16),
        ],
        compiler_params=limit,
        cost_estimate=small,
        name="yz_terms",
    )(after, vectors, swapped_rows, links, table)

    after, _ = lax.optimization_barrier((place, sent))
    mine = call(
        functools.partial(split_last_kernel, count_z), "split_last", [planes_of(1, tail, 0)] * 2, [], after, swapped
    )
    got_last = exchange(*mine)

    def scratch(depth):
        return [
            pltpu.VMEM((4 * nev, 6 * depth * count_y), BF16),
            pltpu.VMEM((2, 3, depth, count_y, 2 * nev), BF16),
        ]

    parts = jax.ShapeDtypeStruct((2, 4, nev, nev), F32)
    rows_shape = (2, 6, count_z, 6 * count_y)
    (part,) = call(
        x_first_kernel, "x_first", [parts], [pltpu.VMEM(rows_shape, F32)] + scratch(count_z), after, vectors, links, *got_first, table
    )
    one = [jax.ShapeDtypeStruct(parts.shape[1:], F32), jax.ShapeDtypeStruct(rows_shape, F32)]
    all_pieces = [jax.ShapeDtypeStruct((size_x, 2, 4 * group, 3 * nev), BF16)]
    operands = after, swapped_rows
    edges = [
        jax.ShapeDtypeStruct((2, 4 * nev, nev), BF16),
        jax.ShapeDtypeStruct((2, 3 * count_y, 2 * nev), BF16),
        jax.ShapeDtypeStruct((2, 6 * count_y, 2 * nev), BF16),
    ]
    first, first_rows, *edges = call(
        x_middle_first, "x_middle_first", one + edges, scratch(lead),
        *operands, got_second[0], table, part, top, lines,
    )
    after, _ = lax.optimization_barrier((after, first_rows))
    operands = after, swapped_rows
    second, second_rows = call(
        functools.partial(x_middle, 1), "x_middle_second", one, scratch(lead), *operands, got_second[1], table, part
    )
    after, _ = lax.optimization_barrier((after, second_rows))
    operands = after, swapped_rows
    (pieces,) = call(
        x_last_first, "x_last_first", all_pieces, scratch(tail), *operands, got_last[0], first_rows, table, first, sent
    )
    (pieces,) = call(
        x_last_second, "x_last_second", all_pieces, scratch(tail) + [pltpu.VMEM((2, 4 * nev, nev), BF16)],
        *operands, got_last[1], second_rows, table, second, halo, *edges, pieces, aliases={10: 0},
    )

    pieces = pieces.reshape(2 * size_x, 4 * group, 3 * nev)
    groups = [[(ts * 2 + h) * 2 + c for ts in range(size_x) for h in range(2)] for c in range(2)]
    got = lax.all_to_all(pieces, ("ts", "gz"), 0, 0, tiled=True, axis_index_groups=groups)
    out_shape = (group, 1, 2, 2, 3 * nev)
    return pl.pallas_call(
        total_kernel,
        grid=(4,),
        in_specs=[in_smem, pl.BlockSpec((size_x // 2, 4 * group, 3 * nev), lambda i: (i, 0, 0))],
        out_specs=pl.BlockSpec(out_shape, lambda i: (0, 0, 0, 0, 0)),
        out_shape=jax.ShapeDtypeStruct(out_shape, F32),
        scratch_shapes=[pltpu.VMEM((4 * group, 3 * nev), F32)],
        compiler_params=limit,
        name="total",
    )(directions, got)


def solution(mesh):
    in_specs = (
        P(None, None, None, "ts", "gz", None, None),
        P(None, None, None, "ts", "gz", None),
        P(),
        P(),
    )
    out_specs = P("ts", "gz", None, None, None)
    return jax.shard_map(shards, mesh=mesh, in_specs=in_specs, out_specs=out_specs, check_vma=False)
```

```python
import functools
import math

import jax
import jax.numpy as jnp
from jax import lax
from jax.experimental import pallas as pl
from jax.experimental.pallas import tpu as pltpu
from jax.sharding import PartitionSpec as P

BF16 = jnp.bfloat16
F32 = jnp.float32


def link_rows(entries, adjoint, width):
    rows = []
    for r in range(2):
        for a in range(3):
            pieces = []
            for q in range(2):
                for b in range(3):
                    first = ((b * 3 + a) if adjoint else (a * 3 + b)) * 2
                    if r == q:
                        pieces.append(entries[first])
                    elif (q == 1) == adjoint:
                        pieces.append(entries[first + 1])
                    else:
                        pieces.append(-entries[first + 1])
            lanes = sum(piece.shape[1] for piece in pieces)
            if lanes < width:
                pieces.append(jnp.zeros((pieces[0].shape[0], width - lanes), F32))
            rows.append(jnp.concatenate(pieces, axis=1))
    return rows


def site_masks(count_y, lanes):
    row = lax.broadcasted_iota(jnp.int32, (count_y, lanes), 0)
    lane = lax.broadcasted_iota(jnp.int32, (count_y, lanes), 1) % count_y
    same = jnp.where(lane == row, 1.0, 0.0).astype(BF16)
    above = jnp.where(lane == (row + 1) % count_y, 1.0, 0.0).astype(BF16)
    below = jnp.where(lane == (row + count_y - 1) % count_y, 1.0, 0.0).astype(BF16)
    return same, above, below


def spread(rows_ref, kind, row, mask):
    count_y, lanes = mask.shape
    blocks = []
    for ra in range(6):
        line = rows_ref[kind, ra, pl.ds(row, 1), :lanes]
        blocks.append(jnp.broadcast_to(line, (count_y, lanes)).astype(BF16) * mask)
    return jnp.concatenate(blocks, axis=0)


def fraction(component, coords, length):
    return jnp.mod(component * coords, length).astype(F32) / length


def table_kernel(lengths, deep, place_ref, momenta_ref, table_ref):
    length_x, length_z, length_y = lengths
    half = table_ref.shape[0] // 2
    shape = 2 * half, table_ref.shape[2]
    row = lax.broadcasted_iota(jnp.int32, shape, 0)
    lane = lax.broadcasted_iota(jnp.int32, shape, 1)
    x_at = row // 2
    x = place_ref[1] + jnp.where(x_at == 2, -1, x_at)
    plane = lane // length_y
    above = deep + (shape[1] // length_y - deep) // 2
    z = place_ref[2] + jnp.where(plane < deep, plane, jnp.where(plane < above, deep, deep - 1))
    y = lane % length_y
    first = row % 2 == 0
    m_x, m_y, m_z = (jnp.where(first, momenta_ref[0, i], momenta_ref[1, i]) for i in range(3))
    angle = 2.0 * math.pi * (
        (fraction(m_x, x, length_x) + fraction(m_y, y, length_y)) + fraction(m_z, z, length_z)
    )
    for first, values in ((0, jnp.cos(angle)), (half, jnp.sin(angle))):
        for at in range(2 * half):
            table_ref[first + at // 2, at % 2 : at % 2 + 1] = values[at : at + 1]


def write_phased(planes_of, table, x_at, table_first, blocks, out_ref, first, colour_stride):
    for b in range(3):
        for block in range(blocks):
            real = planes_of(0, b, block).T.astype(F32)
            imag = planes_of(1, b, block).T.astype(F32)
            nev, sites = real.shape
            at = first + b * colour_stride + block * sites
            put_phased(real, imag, table, x_at, table_first + block * sites, out_ref, at)


def put_phased(real, imag, table, x_at, table_at, out_ref, at):
    nev, sites = real.shape
    for p in range(2):
        cosine, sine = (table[half + x_at, p : p + 1, pl.ds(table_at, sites)] for half in (0, table.shape[0] // 2))
        out_ref[2 * p * nev : (2 * p + 1) * nev, at : at + sites] = (cosine * real - sine * imag).astype(BF16)
        out_ref[(2 * p + 1) * nev : (2 * p + 2) * nev, at : at + sites] = (sine * real + cosine * imag).astype(BF16)


def put_displaced(out_ref, z, terms, count_y, nev):
    for r in range(2):
        for a in range(3):
            rows = terms[(r * 3 + a) * count_y : (r * 3 + a + 1) * count_y]
            out_ref[a, z, :, r * nev : (r + 1) * nev] = rows.astype(BF16)


def combine(products, nev):
    real, imag = [], []
    for p in range(2):
        rr = products[2 * p * nev : (2 * p + 1) * nev, :nev]
        ri = products[2 * p * nev : (2 * p + 1) * nev, nev:]
        ir = products[(2 * p + 1) * nev : (2 * p + 2) * nev, :nev]
        ii = products[(2 * p + 1) * nev : (2 * p + 2) * nev, nev:]
        real.append(rr + ii)
        imag.append(ri - ir)
    return real + imag


def by_owner(first, second):
    nev, lanes = first.shape
    a = first.reshape(nev // 8, 8, lanes)
    b = second.reshape(nev // 8, 8, lanes)
    upper = lax.broadcasted_iota(jnp.int32, a.shape, 1) < 4
    even = jnp.where(upper, a, pltpu.roll(b, 4, 1))
    odd = jnp.where(upper, pltpu.roll(a, 4, 1), b)
    return jnp.stack([even, odd], axis=1).reshape(nev // 4, 8, lanes)


def partial_rows(parts):
    return jnp.concatenate([by_owner(parts[0], parts[1]), by_owner(parts[2], parts[3])], axis=1)


def packed_plane(packed, depth, q, b, z, count, count_y):
    first = ((q * 3 + b) * depth + z) * count_y
    return packed[first : first + count * count_y]


def link_planes(nev, count_z, count_y):
    return -(-18 * count_y * count_z // (nev * count_y))


def packed_link(packed, depth, k, e, count_z, count_y):
    nev = packed.shape[1]
    per_row = nev // count_y
    first = (6 * depth + k * link_planes(nev, count_z, count_y)) * count_y + e // per_row * count_z
    lane = e % per_row * count_y
    return packed[first : first + count_z, lane : lane + count_y]


def put_links(out_ref, at, first_plane, link, count_z, count_y, nev):
    per_row = nev // count_y
    per_plane = count_y // count_z
    for row in range(link_planes(nev, count_z, count_y) * per_plane):
        held = [link(e) for e in range(row * per_row, min(18, (row + 1) * per_row))]
        held += [jnp.zeros((count_z, count_y), BF16)] * (per_row - len(held))
        first = row % per_plane * count_z
        out_ref[at, first_plane + row // per_plane, first : first + count_z] = jnp.concatenate(held, axis=1)


def pack_own_kernel(place_ref, v_ref, link_ref, first_ref, second_ref):
    count_z, count_y, nev = v_ref.shape[3:]
    core, odd = place_ref[0], place_ref[3]
    for out_ref, t in ((first_ref, core + 2 * (1 - odd)), (second_ref, core + 2 * odd)):
        for held in range(6):
            out_ref[0, held * count_z : (held + 1) * count_z] = v_ref[held // 3, held % 3, t]
        put_links(out_ref, 0, 6 * count_z, lambda e, t=t: link_ref[0, e, t], count_z, count_y, nev)


def pack_given_kernel(place_ref, v_ref, link_ref, given_ref):
    count_z, count_y, nev = v_ref.shape[3:]
    planes = link_planes(nev, count_z, count_y)
    for m in range(2):
        t = 1 - place_ref[0] + 2 * m
        for held in range(6):
            given_ref[m, held * count_z : (held + 1) * count_z] = v_ref[held // 3, held % 3, t]
        for k in range(3):
            put_links(
                given_ref, m, 6 * count_z + k * planes, lambda e, k=k, t=t: link_ref[k, e, t], count_z, count_y, nev
            )


def split(place_ref, swap_ref, start, count_z, out_refs):
    odd = place_ref[3]
    depth = out_refs[0].shape[1] // 6
    for i, out_ref in enumerate(out_refs):
        for held in range(6):
            first = held * count_z + start
            out_ref[0, held * depth : (held + 1) * depth] = swap_ref[odd if i else 1 - odd, first : first + depth]


def split_first_kernel(count_z, place_ref, swap_ref, v_ref, first_ref, second_ref, lowest_ref):
    split(place_ref, swap_ref, 0, count_z, (first_ref, second_ref))
    core, odd = place_ref[0], place_ref[3]
    for out_ref, m in ((first_ref, 1 - odd), (second_ref, odd)):
        depth = out_ref.shape[1] // 6
        planes = out_ref.shape[1] - 6 * depth
        out_ref[0, 6 * depth :] = swap_ref[m, 6 * count_z : 6 * count_z + planes]
    for m in range(2):
        for i in range(6):
            own = v_ref[i // 3, i % 3, core + 2 * m, 0]
            lowest_ref[m, i] = jnp.where(core == 0, own, swap_ref[m, i * count_z])


def split_last_kernel(count_z, place_ref, swap_ref, first_ref, second_ref):
    split(place_ref, swap_ref, count_z - first_ref.shape[1] // 6, count_z, (first_ref, second_ref))


def yz_kernel(place_ref, v_ref, swap_ref, link_ref, table_ref, out_ref, top_ref, line_ref,
              rows, padded, phased, moved_y, moved_z):
    core = place_ref[0]
    step_m = pl.program_id(0)
    t = core + 2 * step_m
    count_z, count_y, nev = v_ref.shape[3:]
    deep = 2 * count_z
    lanes = 6 * count_y
    sites = deep * count_y
    same, above, below = site_masks(count_y, lanes)
    mine = pl.multiple_of(core * count_z, count_z)
    theirs = pl.multiple_of((1 - core) * count_z, count_z)
    wide = rows.shape[3]
    lane = lax.broadcasted_iota(jnp.int32, (count_z, wide), 1) % count_y

    def fill_rows(link, start):
        at = pl.ds(start, count_z)
        link_y = [0.5 * link(1, e).astype(F32) for e in range(18)]
        for ra, line in enumerate(link_rows(link_y, False, wide)):
            rows[0, ra, at, :] = jnp.where(
                lane == 0, pltpu.roll(line, wide - (count_y - 1), 1), pltpu.roll(line, 1, 1)
            )
        for ra, line in enumerate(link_rows(link_y, True, wide)):
            rows[1, ra, at, :] = -line
        link_z = [0.5 * link(2, e).astype(F32) for e in range(18)]
        for ra, line in enumerate(link_rows(link_z, False, wide)):
            rows[2, ra, at, :] = line
        for ra, line in enumerate(link_rows(link_z, True, wide)):
            rows[3, ra, at, :] = -line

    padded[:, :, pl.ds(mine, count_z)] = v_ref[:, :, t]
    swapped = swap_ref.at[step_m]
    for q in range(2):
        for b in range(3):
            block = packed_plane(swapped, count_z, q, b, 0, count_z, count_y)
            padded[q, b, pl.ds(theirs, count_z)] = block.reshape(count_z, count_y, nev)
    fill_rows(lambda k, e: packed_link(swapped, count_z, k, e, count_z, count_y), theirs)
    fill_rows(lambda k, e: link_ref[k, e, t], mine)

    table = table_ref
    step = nev // count_y
    write_phased(
        lambda q, b, block: padded[q, b, block * step : (block + 1) * step].reshape(nev, nev),
        table, 0, 0, sites // nev, phased, 0, sites,
    )
    def forward(z):
        return jnp.dot(
            spread(rows, 2, z, same), padded[:, :, z + 1].reshape(lanes, nev), preferred_element_type=F32
        )

    def backward(z):
        return jnp.dot(
            spread(rows, 3, z - 1, same), padded[:, :, z - 1].reshape(lanes, nev), preferred_element_type=F32
        )

    for z in range(deep):
        in_y = spread(rows, 0, z, above) + spread(rows, 1, z, below)
        terms = jnp.dot(in_y, padded[:, :, z].reshape(lanes, nev), preferred_element_type=F32)
        put_displaced(moved_y, z, terms, count_y, nev)
        terms = forward(z) if z + 1 < deep else 0.0
        if z > 0:
            terms += backward(z)
        put_displaced(moved_z, z, terms, count_y, nev)
    for at, moved in enumerate((moved_y, moved_z)):
        products = jnp.dot(phased[...], moved[...].reshape(3 * sites, 2 * nev), preferred_element_type=F32)
        out_ref[:, 0, :, at * nev : (at + 1) * nev] = partial_rows(combine(products, nev)).astype(BF16)
    top_ref[0] = padded[:, :, deep - 1].reshape(lanes, nev)
    for kind in range(2):
        for ra in range(6):
            line_ref[0, kind * 8 + ra : kind * 8 + ra + 1] = rows[2 + kind, ra, deep - 1 : deep]


def from_rows(ref, depth, count_y, first=0):
    return lambda q, b, z, count: packed_plane(ref, depth, q, b, first + z, count, count_y)


def from_times(ref, t):
    count_y, nev = ref.shape[4:]
    return lambda q, b, z, count: ref[q, b, t, z : z + count].reshape(count * count_y, nev)


def pair_rows(odd, at, own_link, received_link, rows):
    below = odd if at else 1 - odd
    entries = [0.5 * jnp.where(below == 1, own_link(e), received_link(e)).astype(F32) for e in range(18)]
    for ra, line in enumerate(link_rows(entries, False, rows.shape[3])):
        rows[below, ra] = line
    for ra, line in enumerate(link_rows(entries, True, rows.shape[3])):
        rows[1 - below, ra] = -line


def x_terms(odd, at, own, received, link_first, table, table_first, rows, phased, moved):
    lanes = rows.shape[3]
    count_z, count_y = moved.shape[2:4]
    nev = moved.shape[4] // 2
    below = odd if at else 1 - odd
    same = site_masks(count_y, lanes)[0]
    sites = count_z * count_y
    step = nev // count_y
    for vectors, x_at, first in ((own, 0, 0), (received, 2 - below, 3 * sites)):
        write_phased(
            lambda q, b, block: vectors(q, b, block * step, step),
            table, x_at, table_first, sites // nev, phased, first, sites,
        )

    def plane(vectors, z):
        return jnp.concatenate([vectors(q, b, z, 1) for q in range(2) for b in range(3)], axis=0)

    for z in range(count_z):
        line = link_first + z
        terms = jnp.dot(spread(rows, 1, line, same), plane(received, z), preferred_element_type=F32)
        put_displaced(moved.at[0], z, terms, count_y, nev)
        terms = jnp.dot(spread(rows, 0, line, same), plane(own, z), preferred_element_type=F32)
        put_displaced(moved.at[1], z, terms, count_y, nev)
    products = jnp.dot(phased[...], moved[...].reshape(6 * sites, 2 * nev), preferred_element_type=F32)
    return combine(products, nev)


def x_first_kernel(place_ref, v_ref, link_ref, first_ref, second_ref, table, out_ref, rows, phased, moved):
    count_z, count_y = link_ref.shape[3:]
    core, odd = place_ref[0], place_ref[3]
    at_table = pl.multiple_of(core * (count_z * count_y), count_z * count_y)
    for at, got in enumerate((first_ref.at[0], second_ref.at[0])):
        m = 1 - odd if at else odd
        t = core + 2 * m
        pair_rows(
            odd, at, lambda e, t=t: link_ref[0, e, t],
            lambda e, got=got: packed_link(got, count_z, 0, e, count_z, count_y), rows,
        )
        parts = x_terms(
            odd, at, from_times(v_ref, t), from_rows(got, count_z, count_y), 0, table, at_table, rows, phased, moved
        )
        for i, part in enumerate(parts):
            out_ref[m, i] = part


def x_part(first, at, place_ref, swap_ref, got, table, rows, phased, moved):
    held_z = rows.shape[2]
    depth, count_y = moved.shape[2:4]
    core, odd = place_ref[0], place_ref[3]
    at_table = pl.multiple_of((1 - core) * (held_z * count_y) + first * count_y, moved.shape[4] // 2)
    return x_terms(
        odd, at, from_rows(swap_ref.at[1 - odd if at else odd], held_z, count_y, first), from_rows(got, depth, count_y),
        first, table, at_table, rows, phased, moved,
    )


def boundary_below(top, lines, table, phased, displaced, forward):
    lanes, nev = top.shape
    count_y = lanes // 6
    wide = lanes // 2
    same = site_masks(count_y, lanes)[0]

    def matrix(kind):
        blocks = []
        for ra in range(6):
            line = lines[kind * 8 + ra : kind * 8 + ra + 1, :lanes]
            blocks.append(jnp.broadcast_to(line, (count_y, lanes)).astype(BF16) * same)
        return jnp.concatenate(blocks, axis=0)

    put_phased(top[:wide].T.astype(F32), top[wide:].T.astype(F32), table, 0, table.shape[2] - nev, phased, 0)
    terms = jnp.dot(matrix(1), top[...], preferred_element_type=F32).astype(BF16)
    displaced[...] = jnp.concatenate([terms[:wide], terms[wide:]], axis=1)
    forward[:, :lanes] = matrix(0)


def boundary(halo, phased, displaced, forward, table, edge):
    lanes, nev = halo.shape
    wide = lanes // 2
    put_phased(halo[:wide].T.astype(F32), halo[wide:].T.astype(F32), table, 0, table.shape[2] - 2 * nev, edge, 0)
    products = jnp.dot(edge[:, :wide], displaced[...], preferred_element_type=F32)
    terms = jnp.dot(forward[:, :lanes], halo[...], preferred_element_type=F32).astype(BF16)
    terms = jnp.concatenate([terms[:wide], terms[wide:]], axis=1)
    products += jnp.dot(phased[:, :wide], terms, preferred_element_type=F32)
    return combine(products, nev)


def x_middle(at, place_ref, swap_ref, got_ref, table, before, out_ref, rows_ref, *scratch):
    held_z = rows_ref.shape[2]
    depth, count_y = scratch[1].shape[2:4]
    odd = place_ref[3]
    m = 1 - odd if at else odd
    own, got = swap_ref.at[m], got_ref.at[0]
    pair_rows(
        odd, at, lambda e: packed_link(own, held_z, 0, e, held_z, count_y),
        lambda e: packed_link(got, depth, 0, e, held_z, count_y), rows_ref,
    )
    parts = x_part(0, at, place_ref, swap_ref, got, table, rows_ref, *scratch)
    for i, part in enumerate(parts):
        out_ref[i] = part + before[m, i]


def x_middle_first(place_ref, swap_ref, got_ref, table, before, top_ref, line_ref,
                   out_ref, rows_ref, phased_ref, displaced_ref, forward_ref, *scratch):
    for m in range(2):
        boundary_below(
            top_ref.at[m], line_ref.at[m], table, phased_ref.at[m], displaced_ref.at[m], forward_ref.at[m]
        )
    x_middle(0, place_ref, swap_ref, got_ref, table, before, out_ref, rows_ref, *scratch)


def x_last(at, place_ref, swap_ref, got_ref, rows_ref, table, before, pieces_ref, *scratch):
    nev = before.shape[2]
    odd = place_ref[3]
    first = rows_ref.shape[2] - scratch[1].shape[2]
    parts = x_part(first, at, place_ref, swap_ref, got_ref.at[0], table, rows_ref, *scratch)
    parts = [part + before[i] for i, part in enumerate(parts)]
    pieces_ref[:, 1 - odd if at else odd, :, 2 * nev :] = partial_rows(parts).astype(BF16)


def one_side(vectors, x_at, kind, at_table, first, rows, table, phased, displaced):
    depth, count_y, lanes = displaced.shape[1:]
    nev = lanes // 2
    sites = depth * count_y
    step = nev // count_y
    same = site_masks(count_y, rows.shape[3])[0]
    write_phased(
        lambda q, b, block: vectors(q, b, block * step, step), table, x_at, at_table, sites // nev, phased, 0, sites
    )
    for z in range(depth):
        plane = jnp.concatenate([vectors(q, b, z, 1) for q in range(2) for b in range(3)], axis=0)
        terms = jnp.dot(spread(rows, kind, first + z, same), plane, preferred_element_type=F32)
        put_displaced(displaced, z, terms, count_y, nev)


def last_place(place_ref, rows_ref, displaced):
    held_z = rows_ref.shape[2]
    depth, count_y, lanes = displaced.shape[1:]
    first = held_z - depth
    at = pl.multiple_of((1 - place_ref[0]) * (held_z * count_y) + first * count_y, lanes // 2)
    return held_z, depth, count_y, first, at


def x_last_first(place_ref, swap_ref, got_ref, rows_ref, second_rows, table, before, sent_ref,
                 pieces_ref, own_phased, own_displaced, *scratch):
    pieces_ref[:, :, :, : sent_ref.shape[3]] = sent_ref[...]
    x_last(0, place_ref, swap_ref, got_ref, rows_ref, table, before, pieces_ref, *scratch)
    held_z, depth, count_y, first, at_table = last_place(place_ref, second_rows, own_displaced)
    own = from_rows(swap_ref.at[1 - place_ref[3]], held_z, count_y, first)
    one_side(own, 0, 0, at_table, first, second_rows, table, own_phased, own_displaced)


def x_last_second(place_ref, got_ref, rows_ref, own_phased, own_displaced, table, before, halo_ref, phased_ref,
                  displaced_ref, forward_ref, sent_ref, pieces_ref, phased, displaced, edge):
    nev = before.shape[2]
    odd = place_ref[3]
    for m in range(2):
        parts = boundary(halo_ref.at[m], phased_ref.at[m], displaced_ref.at[m], forward_ref.at[m], table, edge.at[m])
        above = partial_rows(parts)
        pieces_ref[:, m, :, nev : 2 * nev] = (sent_ref[:, m, :, nev : 2 * nev].astype(F32) + above).astype(BF16)
    held_z, depth, count_y, first, at_table = last_place(place_ref, rows_ref, displaced)
    received = from_rows(got_ref.at[0], depth, count_y)
    one_side(received, 2 - odd, 1, at_table, first, rows_ref, table, phased, displaced)
    sites = 3 * depth * count_y
    products = jnp.dot(own_phased[...], displaced[...].reshape(sites, 2 * nev), preferred_element_type=F32)
    products += jnp.dot(phased[...], own_displaced[...].reshape(sites, 2 * nev), preferred_element_type=F32)
    parts = [part + before[i] for i, part in enumerate(combine(products, nev))]
    pieces_ref[:, 1 - odd, :, 2 * nev :] = partial_rows(parts).astype(BF16)


def total_kernel(directions_ref, got_ref, out_ref, total_ref):
    step = pl.program_id(0)
    part = jnp.sum(got_ref[...].astype(F32), axis=0)

    @pl.when(step == 0)
    def _():
        total_ref[...] = part

    @pl.when(step > 0)
    def _():
        total_ref[...] += part

    @pl.when(step == pl.num_programs(0) - 1)
    def _():
        total = total_ref[...]
        nev = total.shape[1] // 3
        group = out_ref.shape[0]
        in_y, in_z, in_x = (total[:, k * nev : (k + 1) * nev] for k in range(3))
        for d in range(3):
            direction = directions_ref[d]
            chosen = jnp.where(direction == 0, in_x, jnp.where(direction == 1, in_y, in_z))
            for r in range(2):
                for p in range(2):
                    for i in range(group):
                        row = (r * 2 + p) * group + i
                        out_ref[i, 0, p, r : r + 1, d * nev : (d + 1) * nev] = chosen[row : row + 1]


def exchange(first, second):
    count = lax.axis_size("ts")
    got = [None, None]
    for at, array in ((0, first), (1, second)):
        pairs = [(i, (i + 1 if (i + at) % 2 == 0 else i - 1) % count) for i in range(count)]
        got[at] = lax.ppermute(array.reshape(1, -1, array.shape[-1]), "ts", pairs)
    return got


def shards(eigvecs, gauge_links, momenta, directions):
    _, _, count_t, _, count_z, count_y, nev = eigvecs.shape
    vectors = eigvecs.reshape(2, 3, count_t, count_z, count_y, nev)
    links = gauge_links.reshape(3, 18, count_t, count_z, count_y)
    size_x, size_g = lax.axis_size("ts"), lax.axis_size("gz")
    x, g = lax.axis_index("ts"), lax.axis_index("gz")
    core, chip = g % 2, g // 2
    deep = 2 * count_z
    sites = count_z * count_y
    group = nev // size_x

    small = pl.CostEstimate(flops=1_000_000, bytes_accessed=100_000, transcendentals=0)
    limit = pltpu.CompilerParams(vmem_limit_bytes=20 * 1024 * 1024)
    in_vmem = pl.BlockSpec(memory_space=pltpu.VMEM)
    in_smem = pl.BlockSpec(memory_space=pltpu.SMEM)
    planes = link_planes(nev, count_z, count_y)

    place = jnp.stack([core, x, chip * deep, x % 2]).astype(jnp.int32)

    def planes_of(times, depth, directions):
        return jax.ShapeDtypeStruct((times, 6 * depth + directions * planes, count_y, nev), BF16)

    def call(kernel, name, out_shape, scratch_shapes, *operands, aliases={}):
        in_specs = [in_smem] + [in_vmem] * (len(operands) - 1)
        return pl.pallas_call(
            kernel,
            in_specs=in_specs,
            out_specs=jax.tree.map(lambda _: in_vmem, out_shape),
            out_shape=out_shape,
            scratch_shapes=scratch_shapes,
            input_output_aliases=aliases,
            compiler_params=limit,
            cost_estimate=small,
            name=name,
        )(*operands)

    swap = [(0, 1), (1, 0), (2, 3), (3, 2)]
    mine = call(pack_own_kernel, "pack_own", [planes_of(1, count_z, 1)] * 2, [], place, vectors, links)
    got_first = exchange(*mine)
    after, _ = lax.optimization_barrier((place, mine[0]))
    (given,) = call(pack_given_kernel, "pack_given", [planes_of(2, count_z, 3)], [], after, vectors, links)
    swapped = lax.ppermute(given, "gz", swap)
    tail = nev // count_y
    lead = count_z - tail
    table = pl.pallas_call(
        functools.partial(table_kernel, (size_x, count_z * size_g, count_y), deep),
        in_specs=[in_smem, in_smem],
        out_specs=in_vmem,
        out_shape=jax.ShapeDtypeStruct((8, 2, 2 * sites + 2 * nev), F32),
        compiler_params=limit,
        cost_estimate=pl.CostEstimate(flops=20_000_000_000, bytes_accessed=100_000, transcendentals=0),
        name="phase_table",
    )(place, momenta)
    after, _ = lax.optimization_barrier((place, table))
    shapes = [planes_of(1, lead, 1)] * 2 + [jax.ShapeDtypeStruct((2, 6, count_y, nev), BF16)]
    *mine, lowest = call(
        functools.partial(split_first_kernel, count_z), "split_first", shapes, [], after, swapped, vectors
    )
    got_second = exchange(*mine)
    halo = lax.ppermute(lowest.reshape(2, 6 * count_y, nev), "gz", [(0, 2), (2, 0), (1, 3), (3, 1)])

    after, _ = lax.optimization_barrier((place, lowest))
    swapped_rows = swapped.reshape(2, -1, nev)
    sent, top, lines = pl.pallas_call(
        yz_kernel,
        grid=(2,),
        in_specs=[in_smem] + [in_vmem] * 4,
        out_specs=[
            pl.BlockSpec((size_x, 1, 4 * group, 2 * nev), lambda m: (0, m, 0, 0)),
            pl.BlockSpec((1, 6 * count_y, nev), lambda m: (m, 0, 0)),
            pl.BlockSpec((1, 16, 2 * nev), lambda m: (m, 0, 0)),
        ],
        out_shape=[
            jax.ShapeDtypeStruct((size_x, 2, 4 * group, 2 * nev), BF16),
            jax.ShapeDtypeStruct((2, 6 * count_y, nev), BF16),
            jax.ShapeDtypeStruct((2, 16, 2 * nev), F32),
        ],
        scratch_shapes=[
            pltpu.VMEM((4, 6, deep, 2 * nev), F32),
            pltpu.VMEM((2, 3, deep, count_y, nev), BF16),
            pltpu.VMEM((4 * nev, 6 * sites), BF16),
            pltpu.VMEM((3, deep, count_y, 2 * nev), BF16),
            pltpu.VMEM((3, deep, count_y, 2 * nev), BF16),
        ],
        compiler_params=limit,
        cost_estimate=small,
        name="yz_terms",
    )(after, vectors, swapped_rows, links, table)

    after, _ = lax.optimization_barrier((place, sent))
    mine = call(
        functools.partial(split_last_kernel, count_z), "split_last", [planes_of(1, tail, 0)] * 2, [], after, swapped
    )
    got_last = exchange(*mine)

    def scratch(depth):
        return [
            pltpu.VMEM((4 * nev, 6 * depth * count_y), BF16),
            pltpu.VMEM((2, 3, depth, count_y, 2 * nev), BF16),
        ]

    parts = jax.ShapeDtypeStruct((2, 4, nev, nev), F32)
    rows_shape = (2, 6, count_z, 6 * count_y)
    (part,) = call(
        x_first_kernel, "x_first", [parts], [pltpu.VMEM(rows_shape, F32)] + scratch(count_z), after, vectors, links, *got_first, table
    )
    one = [jax.ShapeDtypeStruct(parts.shape[1:], F32), jax.ShapeDtypeStruct(rows_shape, F32)]
    all_pieces = [jax.ShapeDtypeStruct((size_x, 2, 4 * group, 3 * nev), BF16)]
    operands = after, swapped_rows
    edges = [
        jax.ShapeDtypeStruct((2, 4 * nev, nev), BF16),
        jax.ShapeDtypeStruct((2, 3 * count_y, 2 * nev), BF16),
        jax.ShapeDtypeStruct((2, 6 * count_y, 2 * nev), BF16),
    ]
    first, first_rows, *edges = call(
        x_middle_first, "x_middle_first", one + edges, scratch(lead),
        *operands, got_second[0], table, part, top, lines,
    )
    after, _ = lax.optimization_barrier((after, first_rows))
    operands = after, swapped_rows
    second, second_rows = call(
        functools.partial(x_middle, 1), "x_middle_second", one, scratch(lead), *operands, got_second[1], table, part
    )
    after, _ = lax.optimization_barrier((after, second_rows))
    operands = after, swapped_rows
    sides = [(4 * nev, 3 * tail * count_y), (3, tail, count_y, 2 * nev)]
    pieces, *own_side = call(
        x_last_first, "x_last_first", all_pieces + [jax.ShapeDtypeStruct(side, BF16) for side in sides], scratch(tail),
        *operands, got_last[0], first_rows, second_rows, table, first, sent,
    )
    (pieces,) = call(
        x_last_second, "x_last_second", all_pieces,
        [pltpu.VMEM(side, BF16) for side in sides] + [pltpu.VMEM((2, 4 * nev, nev), BF16)],
        after, got_last[1], second_rows, *own_side, table, second, halo, *edges, pieces, aliases={11: 0},
    )

    pieces = pieces.reshape(2 * size_x, 4 * group, 3 * nev)
    groups = [[(ts * 2 + h) * 2 + c for ts in range(size_x) for h in range(2)] for c in range(2)]
    got = lax.all_to_all(pieces, ("ts", "gz"), 0, 0, tiled=True, axis_index_groups=groups)
    out_shape = (group, 1, 2, 2, 3 * nev)
    return pl.pallas_call(
        total_kernel,
        grid=(4,),
        in_specs=[in_smem, pl.BlockSpec((size_x // 2, 4 * group, 3 * nev), lambda i: (i, 0, 0))],
        out_specs=pl.BlockSpec(out_shape, lambda i: (0, 0, 0, 0, 0)),
        out_shape=jax.ShapeDtypeStruct(out_shape, F32),
        scratch_shapes=[pltpu.VMEM((4 * group, 3 * nev), F32)],
        compiler_params=limit,
        name="total",
    )(directions, got)


def solution(mesh):
    in_specs = (
        P(None, None, None, "ts", "gz", None, None),
        P(None, None, None, "ts", "gz", None),
        P(),
        P(),
    )
    out_specs = P("ts", "gz", None, None, None)
    return jax.shard_map(shards, mesh=mesh, in_specs=in_specs, out_specs=out_specs, check_vma=False)
```

```python
import functools
import math

import jax
import jax.numpy as jnp
from jax import lax
from jax.experimental import pallas as pl
from jax.experimental.pallas import tpu as pltpu
from jax.sharding import PartitionSpec as P

BF16 = jnp.bfloat16
F32 = jnp.float32


def link_rows(entries, adjoint, width):
    rows = []
    for r in range(2):
        for a in range(3):
            pieces = []
            for q in range(2):
                for b in range(3):
                    first = ((b * 3 + a) if adjoint else (a * 3 + b)) * 2
                    if r == q:
                        pieces.append(entries[first])
                    elif (q == 1) == adjoint:
                        pieces.append(entries[first + 1])
                    else:
                        pieces.append(-entries[first + 1])
            lanes = sum(piece.shape[1] for piece in pieces)
            if lanes < width:
                pieces.append(jnp.zeros((pieces[0].shape[0], width - lanes), F32))
            rows.append(jnp.concatenate(pieces, axis=1))
    return rows


def site_masks(count_y, lanes):
    row = lax.broadcasted_iota(jnp.int32, (count_y, lanes), 0)
    lane = lax.broadcasted_iota(jnp.int32, (count_y, lanes), 1) % count_y
    same = jnp.where(lane == row, 1.0, 0.0).astype(BF16)
    above = jnp.where(lane == (row + 1) % count_y, 1.0, 0.0).astype(BF16)
    below = jnp.where(lane == (row + count_y - 1) % count_y, 1.0, 0.0).astype(BF16)
    return same, above, below


def spread(rows_ref, kind, row, mask):
    count_y, lanes = mask.shape
    blocks = []
    for ra in range(6):
        line = rows_ref[kind, ra, pl.ds(row, 1), :lanes]
        blocks.append(jnp.broadcast_to(line, (count_y, lanes)).astype(BF16) * mask)
    return jnp.concatenate(blocks, axis=0)


def fraction(component, coords, length):
    return jnp.mod(component * coords, length).astype(F32) / length


def table_kernel(lengths, deep, place_ref, momenta_ref, table_ref):
    length_x, length_z, length_y = lengths
    half = table_ref.shape[0] // 2
    shape = 2 * half, table_ref.shape[2]
    row = lax.broadcasted_iota(jnp.int32, shape, 0)
    lane = lax.broadcasted_iota(jnp.int32, shape, 1)
    x_at = row // 2
    x = place_ref[1] + jnp.where(x_at == 2, -1, x_at)
    plane = lane // length_y
    above = deep + (shape[1] // length_y - deep) // 2
    z = place_ref[2] + jnp.where(plane < deep, plane, jnp.where(plane < above, deep, deep - 1))
    y = lane % length_y
    first = row % 2 == 0
    m_x, m_y, m_z = (jnp.where(first, momenta_ref[0, i], momenta_ref[1, i]) for i in range(3))
    angle = 2.0 * math.pi * (
        (fraction(m_x, x, length_x) + fraction(m_y, y, length_y)) + fraction(m_z, z, length_z)
    )
    for first, values in ((0, jnp.cos(angle)), (half, jnp.sin(angle))):
        for at in range(2 * half):
            table_ref[first + at // 2, at % 2 : at % 2 + 1] = values[at : at + 1]


def write_phased(planes_of, table, x_at, table_first, blocks, out_ref, first, colour_stride):
    for b in range(3):
        for block in range(blocks):
            real = planes_of(0, b, block).T.astype(F32)
            imag = planes_of(1, b, block).T.astype(F32)
            nev, sites = real.shape
            at = first + b * colour_stride + block * sites
            put_phased(real, imag, table, x_at, table_first + block * sites, out_ref, at)


def put_phased(real, imag, table, x_at, table_at, out_ref, at):
    nev, sites = real.shape
    for p in range(2):
        cosine, sine = (table[half + x_at, p : p + 1, pl.ds(table_at, sites)] for half in (0, table.shape[0] // 2))
        out_ref[2 * p * nev : (2 * p + 1) * nev, at : at + sites] = (cosine * real - sine * imag).astype(BF16)
        out_ref[(2 * p + 1) * nev : (2 * p + 2) * nev, at : at + sites] = (sine * real + cosine * imag).astype(BF16)


def put_displaced(out_ref, z, terms, count_y, nev):
    for r in range(2):
        for a in range(3):
            rows = terms[(r * 3 + a) * count_y : (r * 3 + a + 1) * count_y]
            out_ref[a, z, :, r * nev : (r + 1) * nev] = rows.astype(BF16)


def combine(products, nev):
    real, imag = [], []
    for p in range(2):
        rr = products[2 * p * nev : (2 * p + 1) * nev, :nev]
        ri = products[2 * p * nev : (2 * p + 1) * nev, nev:]
        ir = products[(2 * p + 1) * nev : (2 * p + 2) * nev, :nev]
        ii = products[(2 * p + 1) * nev : (2 * p + 2) * nev, nev:]
        real.append(rr + ii)
        imag.append(ri - ir)
    return real + imag


def by_owner(first, second):
    nev, lanes = first.shape
    a = first.reshape(nev // 8, 8, lanes)
    b = second.reshape(nev // 8, 8, lanes)
    upper = lax.broadcasted_iota(jnp.int32, a.shape, 1) < 4
    even = jnp.where(upper, a, pltpu.roll(b, 4, 1))
    odd = jnp.where(upper, pltpu.roll(a, 4, 1), b)
    return jnp.stack([even, odd], axis=1).reshape(nev // 4, 8, lanes)


def partial_rows(parts):
    return jnp.concatenate([by_owner(parts[0], parts[1]), by_owner(parts[2], parts[3])], axis=1)


def packed_plane(packed, depth, q, b, z, count, count_y):
    first = ((q * 3 + b) * depth + z) * count_y
    return packed[first : first + count * count_y]


def link_planes(nev, count_z, count_y):
    return -(-18 * count_y * count_z // (nev * count_y))


def packed_link(packed, depth, k, e, count_z, count_y):
    nev = packed.shape[1]
    per_row = nev // count_y
    first = (6 * depth + k * link_planes(nev, count_z, count_y)) * count_y + e // per_row * count_z
    lane = e % per_row * count_y
    return packed[first : first + count_z, lane : lane + count_y]


def put_links(out_ref, at, first_plane, link, count_z, count_y, nev):
    per_row = nev // count_y
    per_plane = count_y // count_z
    for row in range(link_planes(nev, count_z, count_y) * per_plane):
        held = [link(e) for e in range(row * per_row, min(18, (row + 1) * per_row))]
        held += [jnp.zeros((count_z, count_y), BF16)] * (per_row - len(held))
        first = row % per_plane * count_z
        out_ref[at, first_plane + row // per_plane, first : first + count_z] = jnp.concatenate(held, axis=1)


def pack_own_kernel(place_ref, v_ref, link_ref, first_ref, second_ref):
    count_z, count_y, nev = v_ref.shape[3:]
    core, odd = place_ref[0], place_ref[3]
    for out_ref, t in ((first_ref, core + 2 * (1 - odd)), (second_ref, core + 2 * odd)):
        for held in range(6):
            out_ref[0, held * count_z : (held + 1) * count_z] = v_ref[held // 3, held % 3, t]
        put_links(out_ref, 0, 6 * count_z, lambda e, t=t: link_ref[0, e, t], count_z, count_y, nev)


def pack_given_kernel(place_ref, v_ref, link_ref, given_ref):
    count_z, count_y, nev = v_ref.shape[3:]
    planes = link_planes(nev, count_z, count_y)
    for m in range(2):
        t = 1 - place_ref[0] + 2 * m
        for held in range(6):
            given_ref[m, held * count_z : (held + 1) * count_z] = v_ref[held // 3, held % 3, t]
        for k in range(3):
            put_links(
                given_ref, m, 6 * count_z + k * planes, lambda e, k=k, t=t: link_ref[k, e, t], count_z, count_y, nev
            )


def split(place_ref, swap_ref, start, count_z, out_refs):
    odd = place_ref[3]
    depth = out_refs[0].shape[1] // 6
    for i, out_ref in enumerate(out_refs):
        for held in range(6):
            first = held * count_z + start
            out_ref[0, held * depth : (held + 1) * depth] = swap_ref[odd if i else 1 - odd, first : first + depth]


def split_first_kernel(count_z, place_ref, swap_ref, v_ref, first_ref, second_ref, lowest_ref):
    split(place_ref, swap_ref, 0, count_z, (first_ref, second_ref))
    core, odd = place_ref[0], place_ref[3]
    for out_ref, m in ((first_ref, 1 - odd), (second_ref, odd)):
        depth = out_ref.shape[1] // 6
        planes = out_ref.shape[1] - 6 * depth
        out_ref[0, 6 * depth :] = swap_ref[m, 6 * count_z : 6 * count_z + planes]
    for m in range(2):
        for i in range(6):
            own = v_ref[i // 3, i % 3, core + 2 * m, 0]
            lowest_ref[m, i] = jnp.where(core == 0, own, swap_ref[m, i * count_z])


def split_last_kernel(count_z, place_ref, swap_ref, first_ref, second_ref):
    split(place_ref, swap_ref, count_z - first_ref.shape[1] // 6, count_z, (first_ref, second_ref))


def yz_kernel(place_ref, v_ref, swap_ref, link_ref, table_ref, out_ref, top_ref, line_ref,
              rows, padded, phased, moved_y, moved_z):
    core = place_ref[0]
    step_m = pl.program_id(0)
    t = core + 2 * step_m
    count_z, count_y, nev = v_ref.shape[3:]
    deep = 2 * count_z
    lanes = 6 * count_y
    sites = deep * count_y
    same, above, below = site_masks(count_y, lanes)
    mine = pl.multiple_of(core * count_z, count_z)
    theirs = pl.multiple_of((1 - core) * count_z, count_z)
    wide = rows.shape[3]
    lane = lax.broadcasted_iota(jnp.int32, (count_z, wide), 1) % count_y

    def fill_rows(link, start):
        at = pl.ds(start, count_z)
        link_y = [0.5 * link(1, e).astype(F32) for e in range(18)]
        for ra, line in enumerate(link_rows(link_y, False, wide)):
            rows[0, ra, at, :] = jnp.where(
                lane == 0, pltpu.roll(line, wide - (count_y - 1), 1), pltpu.roll(line, 1, 1)
            )
        for ra, line in enumerate(link_rows(link_y, True, wide)):
            rows[1, ra, at, :] = -line
        link_z = [0.5 * link(2, e).astype(F32) for e in range(18)]
        for ra, line in enumerate(link_rows(link_z, False, wide)):
            rows[2, ra, at, :] = line
        for ra, line in enumerate(link_rows(link_z, True, wide)):
            rows[3, ra, at, :] = -line

    padded[:, :, pl.ds(mine, count_z)] = v_ref[:, :, t]
    swapped = swap_ref.at[step_m]
    for q in range(2):
        for b in range(3):
            block = packed_plane(swapped, count_z, q, b, 0, count_z, count_y)
            padded[q, b, pl.ds(theirs, count_z)] = block.reshape(count_z, count_y, nev)
    fill_rows(lambda k, e: packed_link(swapped, count_z, k, e, count_z, count_y), theirs)
    fill_rows(lambda k, e: link_ref[k, e, t], mine)

    table = table_ref
    step = nev // count_y
    write_phased(
        lambda q, b, block: padded[q, b, block * step : (block + 1) * step].reshape(nev, nev),
        table, 0, 0, sites // nev, phased, 0, sites,
    )
    def forward(z):
        return jnp.dot(
            spread(rows, 2, z, same), padded[:, :, z + 1].reshape(lanes, nev), preferred_element_type=F32
        )

    def backward(z):
        return jnp.dot(
            spread(rows, 3, z - 1, same), padded[:, :, z - 1].reshape(lanes, nev), preferred_element_type=F32
        )

    for z in range(deep):
        in_y = spread(rows, 0, z, above) + spread(rows, 1, z, below)
        terms = jnp.dot(in_y, padded[:, :, z].reshape(lanes, nev), preferred_element_type=F32)
        put_displaced(moved_y, z, terms, count_y, nev)
        terms = forward(z) if z + 1 < deep else 0.0
        if z > 0:
            terms += backward(z)
        put_displaced(moved_z, z, terms, count_y, nev)
    for at, moved in enumerate((moved_y, moved_z)):
        products = jnp.dot(phased[...], moved[...].reshape(3 * sites, 2 * nev), preferred_element_type=F32)
        out_ref[:, 0, :, at * nev : (at + 1) * nev] = partial_rows(combine(products, nev)).astype(BF16)
    top_ref[0] = padded[:, :, deep - 1].reshape(lanes, nev)
    for kind in range(2):
        for ra in range(6):
            line_ref[0, kind * 8 + ra : kind * 8 + ra + 1] = rows[2 + kind, ra, deep - 1 : deep]


def from_rows(ref, depth, count_y, first=0):
    return lambda q, b, z, count: packed_plane(ref, depth, q, b, first + z, count, count_y)


def from_times(ref, t):
    count_y, nev = ref.shape[4:]
    return lambda q, b, z, count: ref[q, b, t, z : z + count].reshape(count * count_y, nev)


def pair_rows(odd, at, own_link, received_link, rows):
    below = odd if at else 1 - odd
    entries = [0.5 * jnp.where(below == 1, own_link(e), received_link(e)).astype(F32) for e in range(18)]
    for ra, line in enumerate(link_rows(entries, False, rows.shape[3])):
        rows[below, ra] = line
    for ra, line in enumerate(link_rows(entries, True, rows.shape[3])):
        rows[1 - below, ra] = -line


def x_terms(odd, at, own, received, link_first, table, table_first, rows, phased, moved):
    lanes = rows.shape[3]
    count_z, count_y = moved.shape[2:4]
    nev = moved.shape[4] // 2
    below = odd if at else 1 - odd
    same = site_masks(count_y, lanes)[0]
    sites = count_z * count_y
    step = nev // count_y
    for vectors, x_at, first in ((own, 0, 0), (received, 2 - below, 3 * sites)):
        write_phased(
            lambda q, b, block: vectors(q, b, block * step, step),
            table, x_at, table_first, sites // nev, phased, first, sites,
        )

    def plane(vectors, z):
        return jnp.concatenate([vectors(q, b, z, 1) for q in range(2) for b in range(3)], axis=0)

    for z in range(count_z):
        line = link_first + z
        terms = jnp.dot(spread(rows, 1, line, same), plane(received, z), preferred_element_type=F32)
        put_displaced(moved.at[0], z, terms, count_y, nev)
        terms = jnp.dot(spread(rows, 0, line, same), plane(own, z), preferred_element_type=F32)
        put_displaced(moved.at[1], z, terms, count_y, nev)
    products = jnp.dot(phased[...], moved[...].reshape(6 * sites, 2 * nev), preferred_element_type=F32)
    return combine(products, nev)


def x_first_kernel(place_ref, v_ref, link_ref, first_ref, second_ref, table, out_ref, rows, phased, moved):
    count_z, count_y = link_ref.shape[3:]
    core, odd = place_ref[0], place_ref[3]
    at_table = pl.multiple_of(core * (count_z * count_y), count_z * count_y)
    for at, got in enumerate((first_ref.at[0], second_ref.at[0])):
        m = 1 - odd if at else odd
        t = core + 2 * m
        pair_rows(
            odd, at, lambda e, t=t: link_ref[0, e, t],
            lambda e, got=got: packed_link(got, count_z, 0, e, count_z, count_y), rows,
        )
        parts = x_terms(
            odd, at, from_times(v_ref, t), from_rows(got, count_z, count_y), 0, table, at_table, rows, phased, moved
        )
        for i, part in enumerate(parts):
            out_ref[m, i] = part


def x_part(first, at, place_ref, swap_ref, got, table, rows, phased, moved):
    held_z = rows.shape[2]
    depth, count_y = moved.shape[2:4]
    core, odd = place_ref[0], place_ref[3]
    at_table = pl.multiple_of((1 - core) * (held_z * count_y) + first * count_y, moved.shape[4] // 2)
    return x_terms(
        odd, at, from_rows(swap_ref.at[1 - odd if at else odd], held_z, count_y, first), from_rows(got, depth, count_y),
        first, table, at_table, rows, phased, moved,
    )


def boundary_below(top, lines, table, phased, displaced, forward):
    lanes, nev = top.shape
    count_y = lanes // 6
    wide = lanes // 2
    same = site_masks(count_y, lanes)[0]

    def matrix(kind):
        blocks = []
        for ra in range(6):
            line = lines[kind * 8 + ra : kind * 8 + ra + 1, :lanes]
            blocks.append(jnp.broadcast_to(line, (count_y, lanes)).astype(BF16) * same)
        return jnp.concatenate(blocks, axis=0)

    put_phased(top[:wide].T.astype(F32), top[wide:].T.astype(F32), table, 0, table.shape[2] - nev, phased, 0)
    terms = jnp.dot(matrix(1), top[...], preferred_element_type=F32).astype(BF16)
    displaced[...] = jnp.concatenate([terms[:wide], terms[wide:]], axis=1)
    forward[:, :lanes] = matrix(0)


def boundary(halo, phased, displaced, forward, table, edge):
    lanes, nev = halo.shape
    wide = lanes // 2
    put_phased(halo[:wide].T.astype(F32), halo[wide:].T.astype(F32), table, 0, table.shape[2] - 2 * nev, edge, 0)
    products = jnp.dot(edge[:, :wide], displaced[...], preferred_element_type=F32)
    terms = jnp.dot(forward[:, :lanes], halo[...], preferred_element_type=F32).astype(BF16)
    terms = jnp.concatenate([terms[:wide], terms[wide:]], axis=1)
    products += jnp.dot(phased[:, :wide], terms, preferred_element_type=F32)
    return combine(products, nev)


def x_middle(at, place_ref, swap_ref, got_ref, table, before, out_ref, rows_ref, *scratch):
    held_z = rows_ref.shape[2]
    depth, count_y = scratch[1].shape[2:4]
    odd = place_ref[3]
    m = 1 - odd if at else odd
    own, got = swap_ref.at[m], got_ref.at[0]
    pair_rows(
        odd, at, lambda e: packed_link(own, held_z, 0, e, held_z, count_y),
        lambda e: packed_link(got, depth, 0, e, held_z, count_y), rows_ref,
    )
    parts = x_part(0, at, place_ref, swap_ref, got, table, rows_ref, *scratch)
    for i, part in enumerate(parts):
        out_ref[i] = part + before[m, i]


def x_middle_first(place_ref, swap_ref, got_ref, table, before, top_ref, line_ref,
                   out_ref, rows_ref, phased_ref, displaced_ref, forward_ref, *scratch):
    for m in range(2):
        boundary_below(
            top_ref.at[m], line_ref.at[m], table, phased_ref.at[m], displaced_ref.at[m], forward_ref.at[m]
        )
    x_middle(0, place_ref, swap_ref, got_ref, table, before, out_ref, rows_ref, *scratch)


def x_last(at, place_ref, swap_ref, got_ref, rows_ref, table, before, pieces_ref, *scratch):
    nev = before.shape[2]
    odd = place_ref[3]
    first = rows_ref.shape[2] - scratch[1].shape[2]
    parts = x_part(first, at, place_ref, swap_ref, got_ref.at[0], table, rows_ref, *scratch)
    parts = [part + before[i] for i, part in enumerate(parts)]
    pieces_ref[:, 1 - odd if at else odd, :, 2 * nev :] = partial_rows(parts).astype(BF16)


def one_side(vectors, x_at, kind, at_table, first, rows, table, phased, displaced):
    depth, count_y, lanes = displaced.shape[1:]
    nev = lanes // 2
    sites = depth * count_y
    step = nev // count_y
    same = site_masks(count_y, rows.shape[3])[0]
    write_phased(
        lambda q, b, block: vectors(q, b, block * step, step), table, x_at, at_table, sites // nev, phased, 0, sites
    )
    for z in range(depth):
        plane = jnp.concatenate([vectors(q, b, z, 1) for q in range(2) for b in range(3)], axis=0)
        terms = jnp.dot(spread(rows, kind, first + z, same), plane, preferred_element_type=F32)
        put_displaced(displaced, z, terms, count_y, nev)


def last_place(place_ref, rows_ref, displaced):
    held_z = rows_ref.shape[2]
    depth, count_y, lanes = displaced.shape[1:]
    first = held_z - depth
    at = pl.multiple_of((1 - place_ref[0]) * (held_z * count_y) + first * count_y, lanes // 2)
    return held_z, depth, count_y, first, at


def x_last_first(place_ref, swap_ref, got_ref, rows_ref, second_rows, table, before, sent_ref,
                 pieces_ref, own_phased, own_displaced, *scratch):
    pieces_ref[:, :, :, : sent_ref.shape[3]] = sent_ref[...]
    x_last(0, place_ref, swap_ref, got_ref, rows_ref, table, before, pieces_ref, *scratch)
    held_z, depth, count_y, first, at_table = last_place(place_ref, second_rows, own_displaced)
    own = from_rows(swap_ref.at[1 - place_ref[3]], held_z, count_y, first)
    one_side(own, 0, 0, at_table, first, second_rows, table, own_phased, own_displaced)


def x_last_second(place_ref, got_ref, rows_ref, own_phased, own_displaced, table, before, halo_ref, phased_ref,
                  displaced_ref, forward_ref, sent_ref, pieces_ref, phased, displaced, edge):
    nev = before.shape[2]
    odd = place_ref[3]
    for m in range(2):
        parts = boundary(halo_ref.at[m], phased_ref.at[m], displaced_ref.at[m], forward_ref.at[m], table, edge.at[m])
        above = partial_rows(parts)
        pieces_ref[:, m, :, nev : 2 * nev] = (sent_ref[:, m, :, nev : 2 * nev].astype(F32) + above).astype(BF16)
    held_z, depth, count_y, first, at_table = last_place(place_ref, rows_ref, displaced)
    received = from_rows(got_ref.at[0], depth, count_y)
    one_side(received, 2 - odd, 1, at_table, first, rows_ref, table, phased, displaced)
    sites = 3 * depth * count_y
    products = jnp.dot(own_phased[...], displaced[...].reshape(sites, 2 * nev), preferred_element_type=F32)
    products += jnp.dot(phased[...], own_displaced[...].reshape(sites, 2 * nev), preferred_element_type=F32)
    parts = [part + before[i] for i, part in enumerate(combine(products, nev))]
    pieces_ref[:, 1 - odd, :, 2 * nev :] = partial_rows(parts).astype(BF16)


def total_kernel(directions_ref, got_ref, out_ref):
    total = jnp.sum(got_ref[...].astype(F32), axis=0)
    nev = total.shape[1] // 3
    group = out_ref.shape[0]
    in_y, in_z, in_x = (total[:, k * nev : (k + 1) * nev] for k in range(3))
    for d in range(3):
        direction = directions_ref[d]
        chosen = jnp.where(direction == 0, in_x, jnp.where(direction == 1, in_y, in_z))
        for r in range(2):
            for p in range(2):
                for i in range(group):
                    row = (r * 2 + p) * group + i
                    out_ref[i, 0, p, r : r + 1, d * nev : (d + 1) * nev] = chosen[row : row + 1]


def exchange(first, second):
    count = lax.axis_size("ts")
    got = [None, None]
    for at, array in ((0, first), (1, second)):
        pairs = [(i, (i + 1 if (i + at) % 2 == 0 else i - 1) % count) for i in range(count)]
        got[at] = lax.ppermute(array.reshape(1, -1, array.shape[-1]), "ts", pairs)
    return got


def shards(eigvecs, gauge_links, momenta, directions):
    _, _, count_t, _, count_z, count_y, nev = eigvecs.shape
    vectors = eigvecs.reshape(2, 3, count_t, count_z, count_y, nev)
    links = gauge_links.reshape(3, 18, count_t, count_z, count_y)
    size_x, size_g = lax.axis_size("ts"), lax.axis_size("gz")
    x, g = lax.axis_index("ts"), lax.axis_index("gz")
    core, chip = g % 2, g // 2
    deep = 2 * count_z
    sites = count_z * count_y
    group = nev // size_x

    small = pl.CostEstimate(flops=1_000_000, bytes_accessed=100_000, transcendentals=0)
    limit = pltpu.CompilerParams(vmem_limit_bytes=20 * 1024 * 1024)
    in_vmem = pl.BlockSpec(memory_space=pltpu.VMEM)
    in_smem = pl.BlockSpec(memory_space=pltpu.SMEM)
    planes = link_planes(nev, count_z, count_y)

    place = jnp.stack([core, x, chip * deep, x % 2]).astype(jnp.int32)

    def planes_of(times, depth, directions):
        return jax.ShapeDtypeStruct((times, 6 * depth + directions * planes, count_y, nev), BF16)

    def call(kernel, name, out_shape, scratch_shapes, *operands, aliases={}):
        in_specs = [in_smem] + [in_vmem] * (len(operands) - 1)
        return pl.pallas_call(
            kernel,
            in_specs=in_specs,
            out_specs=jax.tree.map(lambda _: in_vmem, out_shape),
            out_shape=out_shape,
            scratch_shapes=scratch_shapes,
            input_output_aliases=aliases,
            compiler_params=limit,
            cost_estimate=small,
            name=name,
        )(*operands)

    swap = [(0, 1), (1, 0), (2, 3), (3, 2)]
    mine = call(pack_own_kernel, "pack_own", [planes_of(1, count_z, 1)] * 2, [], place, vectors, links)
    got_first = exchange(*mine)
    after, _ = lax.optimization_barrier((place, mine[0]))
    (given,) = call(pack_given_kernel, "pack_given", [planes_of(2, count_z, 3)], [], after, vectors, links)
    swapped = lax.ppermute(given, "gz", swap)
    tail = nev // count_y
    lead = count_z - tail
    table = pl.pallas_call(
        functools.partial(table_kernel, (size_x, count_z * size_g, count_y), deep),
        in_specs=[in_smem, in_smem],
        out_specs=in_vmem,
        out_shape=jax.ShapeDtypeStruct((8, 2, 2 * sites + 2 * nev), F32),
        compiler_params=limit,
        cost_estimate=pl.CostEstimate(flops=20_000_000_000, bytes_accessed=100_000, transcendentals=0),
        name="phase_table",
    )(place, momenta)
    after, _ = lax.optimization_barrier((place, table))
    shapes = [planes_of(1, lead, 1)] * 2 + [jax.ShapeDtypeStruct((2, 6, count_y, nev), BF16)]
    *mine, lowest = call(
        functools.partial(split_first_kernel, count_z), "split_first", shapes, [], after, swapped, vectors
    )
    got_second = exchange(*mine)
    halo = lax.ppermute(lowest.reshape(2, 6 * count_y, nev), "gz", [(0, 2), (2, 0), (1, 3), (3, 1)])

    after, _ = lax.optimization_barrier((place, lowest))
    swapped_rows = swapped.reshape(2, -1, nev)
    sent, top, lines = pl.pallas_call(
        yz_kernel,
        grid=(2,),
        in_specs=[in_smem] + [in_vmem] * 4,
        out_specs=[
            pl.BlockSpec((size_x, 1, 4 * group, 2 * nev), lambda m: (0, m, 0, 0)),
            pl.BlockSpec((1, 6 * count_y, nev), lambda m: (m, 0, 0)),
            pl.BlockSpec((1, 16, 2 * nev), lambda m: (m, 0, 0)),
        ],
        out_shape=[
            jax.ShapeDtypeStruct((size_x, 2, 4 * group, 2 * nev), BF16),
            jax.ShapeDtypeStruct((2, 6 * count_y, nev), BF16),
            jax.ShapeDtypeStruct((2, 16, 2 * nev), F32),
        ],
        scratch_shapes=[
            pltpu.VMEM((4, 6, deep, 2 * nev), F32),
            pltpu.VMEM((2, 3, deep, count_y, nev), BF16),
            pltpu.VMEM((4 * nev, 6 * sites), BF16),
            pltpu.VMEM((3, deep, count_y, 2 * nev), BF16),
            pltpu.VMEM((3, deep, count_y, 2 * nev), BF16),
        ],
        compiler_params=limit,
        cost_estimate=small,
        name="yz_terms",
    )(after, vectors, swapped_rows, links, table)

    after, _ = lax.optimization_barrier((place, sent))
    mine = call(
        functools.partial(split_last_kernel, count_z), "split_last", [planes_of(1, tail, 0)] * 2, [], after, swapped
    )
    got_last = exchange(*mine)

    def scratch(depth):
        return [
            pltpu.VMEM((4 * nev, 6 * depth * count_y), BF16),
            pltpu.VMEM((2, 3, depth, count_y, 2 * nev), BF16),
        ]

    parts = jax.ShapeDtypeStruct((2, 4, nev, nev), F32)
    rows_shape = (2, 6, count_z, 6 * count_y)
    (part,) = call(
        x_first_kernel, "x_first", [parts], [pltpu.VMEM(rows_shape, F32)] + scratch(count_z), after, vectors, links, *got_first, table
    )
    one = [jax.ShapeDtypeStruct(parts.shape[1:], F32), jax.ShapeDtypeStruct(rows_shape, F32)]
    all_pieces = [jax.ShapeDtypeStruct((size_x, 2, 4 * group, 3 * nev), BF16)]
    operands = after, swapped_rows
    edges = [
        jax.ShapeDtypeStruct((2, 4 * nev, nev), BF16),
        jax.ShapeDtypeStruct((2, 3 * count_y, 2 * nev), BF16),
        jax.ShapeDtypeStruct((2, 6 * count_y, 2 * nev), BF16),
    ]
    first, first_rows, *edges = call(
        x_middle_first, "x_middle_first", one + edges, scratch(lead),
        *operands, got_second[0], table, part, top, lines,
    )
    after, _ = lax.optimization_barrier((after, first_rows))
    operands = after, swapped_rows
    second, second_rows = call(
        functools.partial(x_middle, 1), "x_middle_second", one, scratch(lead), *operands, got_second[1], table, part
    )
    after, _ = lax.optimization_barrier((after, second_rows))
    operands = after, swapped_rows
    sides = [(4 * nev, 3 * tail * count_y), (3, tail, count_y, 2 * nev)]
    pieces, *own_side = call(
        x_last_first, "x_last_first", all_pieces + [jax.ShapeDtypeStruct(side, BF16) for side in sides], scratch(tail),
        *operands, got_last[0], first_rows, second_rows, table, first, sent,
    )
    (pieces,) = call(
        x_last_second, "x_last_second", all_pieces,
        [pltpu.VMEM(side, BF16) for side in sides] + [pltpu.VMEM((2, 4 * nev, nev), BF16)],
        after, got_last[1], second_rows, *own_side, table, second, halo, *edges, pieces, aliases={11: 0},
    )

    pieces = pieces.reshape(2 * size_x, 4 * group, 3 * nev)
    groups = [[(ts * 2 + h) * 2 + c for ts in range(size_x) for h in range(2)] for c in range(2)]
    got = lax.all_to_all(pieces, ("ts", "gz"), 0, 0, tiled=True, axis_index_groups=groups)
    (out,) = call(
        total_kernel, "total", [jax.ShapeDtypeStruct((group, 1, 2, 2, 3 * nev), F32)], [], directions, got
    )
    return out


def solution(mesh):
    in_specs = (
        P(None, None, None, "ts", "gz", None, None),
        P(None, None, None, "ts", "gz", None),
        P(),
        P(),
    )
    out_specs = P("ts", "gz", None, None, None)
    return jax.shard_map(shards, mesh=mesh, in_specs=in_specs, out_specs=out_specs, check_vma=False)
```
